32 devices in a mesh: dp: 16 (over z, x, core), mp: 2 (over y).
Axes of the slice: x: 2, y: 2, z: 4, core: 2. Of those that a mesh axis runs over, the one named last changes fastest.
Arguments:
- tokens: bfloat16 [32, 256, 2048], P('dp'), may hold values from -6 to 6
- mod_table: float32 [32, 6, 2048], replicated, may hold values from -3 to 3
- w_qkv: bfloat16 [3, 2048, 2048], P(None, 'dp', 'mp'), may hold values from -0.125 to 0.125
- w_out_t: bfloat16 [2048, 2048], P('dp', 'mp'), may hold values from -1 to 1
- w_up: bfloat16 [2048, 8192], P('dp', 'mp'), may hold values from -0.125 to 0.125
- w_down: bfloat16 [2048, 8192], P('dp', 'mp'), may hold values from -0.0625 to 0.0625
- bins: int32 [32], P('dp'), may hold values from 0 to 31
- present: int32 [32], P('dp'), may hold values from 0 to 1, as said below
- cotangent: bfloat16 [32, 256, 2048], P('dp'), may hold values from -6 to 6
Outputs:
- block_out: bfloat16 [32, 256, 2048], P('dp')
- input_grad: float32 [32, 256, 2048], P('dp')
- table_grad: float32 [32, 6, 2048], P(None, None, 'dp')
- qkv_grad: float32 [3, 2048, 2048], P(None, 'dp', 'mp')
- out_grad: float32 [2048, 2048], P('dp', 'mp')
- up_grad: float32 [2048, 8192], P('dp', 'mp')
- down_grad: float32 [2048, 8192], P('dp', 'mp')
The draws below stay inside these ranges and needn't reach their ends.
Inputs may be any that keep to these rules, and one draw needn't show every extreme that they name: `present`: each device's 2 consecutive slots hold its images first and empty slots after; every device holds 1 to 2 images, and some device holds 2, another 1.
All inputs are finite; a program needn't handle non-finite values.
Results may differ from the reference program's by a relative error of at most 0.012.
The reference program's roundings to bfloat16 on the way count: a program that leaves them out, or rounds other values in their place, can miss the bound.
Values may be sent and summed in bfloat16 or wider, within the bound.
No kernel may reach another device: no remote copies, remote signals or barrier semaphores. Data moves between devices by JAX's collectives and lax.ppermute only.
A program may use at most 320 MiB of HBM per device.

```python
import math
from functools import partial
import jax
import jax.numpy as jnp
from jax import lax

D = 2048
HEADS = 16
HEAD_DIM = 128
FF = 8192
SEQ = 256
BINS = 32
CAP = 2
SLOTS = 32


def draw_present(key, part):
    key = jax.random.fold_in(key, 7)
    key_counts, key_full, key_single = jax.random.split(key, 3)
    groups = SLOTS // CAP
    counts = jax.random.randint(key_counts, (groups,), 1, CAP + 1)
    full_at = jax.random.randint(key_full, (), 0, groups)
    single_at = jax.random.randint(key_single, (), 0, groups - 1)
    single_at = jnp.where(single_at >= full_at, single_at + 1, single_at)
    places = jnp.arange(groups)
    counts = jnp.where(places == single_at, 1, counts)
    counts = jnp.where(places == full_at, CAP, counts)
    filled = jnp.arange(CAP)[None, :] < counts[:, None]
    return filled.astype(jnp.int32).reshape(SLOTS)


def set_ends(entries, key, low, high):
    longest = entries.shape.index(max(entries.shape))
    spots = []
    for shift in (0, 1):
        where = [jax.random.randint(jax.random.fold_in(key, axis), (), 0, length) for axis, length in enumerate(entries.shape)]
        where[longest] = (where[longest] + shift) % entries.shape[longest]
        spots.append(tuple(where))
    return entries.at[spots[0]].set(low).at[spots[1]].set(high)


def block_scale(stream_key, dims, shards, smallest, top_value):
    def one(position, shards_of):
        steps = jax.random.uniform(jax.random.fold_in(jax.random.fold_in(stream_key, 6), position), (shards_of,), jnp.float32, smallest / len(shards), top_value / len(shards))
        return jnp.repeat(jnp.exp(steps), dims[position] // shards_of).reshape((-1,) + (1,) * (len(dims) - position - 1))

    level = one(*shards[0])
    for cut in shards[1:]:
        level = level * one(*cut)
    return level


def bell_draw(rng, extent, scale, most, shards=(), kind=jnp.bfloat16):
    entries = scale * jax.random.normal(rng, extent, jnp.float32)
    if shards:
        entries = entries * block_scale(rng, extent, shards, -0.22, 0.18)
    return jnp.clip(entries, -most, most).astype(kind)


def setup_inputs(seed: int = 0) -> dict:
    streams_of = jax.random.split(jax.random.key(seed), 10)
    tokens = bell_draw(streams_of[0], (SLOTS, SEQ, D), 1.0, 6.0, ((0, 16),))
    mod_table = bell_draw(streams_of[1], (BINS, 6, D), 0.5, 3.0, (), jnp.float32)
    w_qkv = bell_draw(streams_of[2], (3, D, D), D ** -0.5, 0.125, ((1, 16), (2, 2)))
    w_out_t = bell_draw(streams_of[3], (D, D), (D // 64) ** -0.5, 1.0, ((0, 16), (1, 2)))
    w_up = bell_draw(streams_of[4], (D, FF), D ** -0.5, 0.125, ((0, 16), (1, 2)))
    w_down = bell_draw(streams_of[5], (D, FF), FF ** -0.5, 0.0625, ((0, 16), (1, 2)))
    bins = set_ends(jax.random.randint(streams_of[6], (SLOTS,), 0, BINS), jax.random.fold_in(streams_of[6], 1), 0, BINS - 1).astype(jnp.int32)
    present = draw_present(jax.random.fold_in(streams_of[9], 71), 0)
    cotangent = bell_draw(streams_of[8], (SLOTS, SEQ, D), 1.0, 6.0, ((0, 16),))
    return dict(tokens=tokens, mod_table=mod_table, w_qkv=w_qkv, w_out_t=w_out_t, w_up=w_up, w_down=w_down, bins=bins, present=present, cotangent=cotangent)


@jax.custom_vjp
def low(v):
    return lax.optimization_barrier(v.astype(jnp.bfloat16)).astype(jnp.float32)

@jax.custom_vjp
def low_back(v):
    return v

def low_keep(v):
    return (low(v), None)

def low_pass(kept, grad):
    return (grad,)

def back_keep(v):
    return (v, None)

def back_low(kept, grad):
    return (low(grad),)
low.defvjp(low_keep, low_pass)
low_back.defvjp(back_keep, back_low)
EPS = 1e-06
HIGH = lax.Precision.HIGHEST

def layer_norm(value):
    centre = value - lax.optimization_barrier(jnp.mean(value, axis=-1, keepdims=True))
    spread = lax.optimization_barrier(jnp.mean(centre * centre, axis=-1, keepdims=True))
    return centre * lax.rsqrt(spread + EPS)

def modulate(value, shift, scale):
    return layer_norm(value) * (1.0 + scale) + shift

def forward(onehot, inputs, table, w_qkv, w_out_t, w_up, w_down):
    count, length, width = inputs.shape
    rows = jnp.einsum('gb,btd->gtd', onehot, table, precision=HIGH)
    shift1, scale1, gate1 = (rows[:, 0:1], rows[:, 1:2], rows[:, 2:3])
    shift2, scale2, gate2 = (rows[:, 3:4], rows[:, 4:5], rows[:, 5:6])
    normed = low(modulate(inputs, shift1, scale1))
    qkv = low(low_back(jnp.einsum('csd,tde->tcse', normed, w_qkv, precision=HIGH)))
    query = qkv[0].reshape(count, length, HEADS, HEAD_DIM)
    keys = qkv[1].reshape(count, length, HEADS, HEAD_DIM)
    values = qkv[2].reshape(count, length, HEADS, HEAD_DIM)
    scores = jnp.einsum('cqhe,ckhe->chqk', query, keys, precision=HIGH) * HEAD_DIM ** (-0.5)
    scores = low_back(scores)
    probs = low(jax.nn.softmax(scores, axis=-1))
    mixed = jnp.einsum('chqk,ckhe->cqhe', probs, values, precision=HIGH).reshape(count, length, width)
    mixed = low(low_back(mixed))
    att = low_back(jnp.einsum('cse,de->csd', mixed, w_out_t, precision=HIGH))
    hidden = inputs + gate1 * att
    second = low(modulate(hidden, shift2, scale2))
    up_val = low_back(jnp.einsum('csd,df->csf', second, w_up, precision=HIGH))
    act = low(jax.nn.gelu(up_val))
    mlp = low_back(jnp.einsum('csf,df->csd', act, w_down, precision=HIGH))
    return hidden + gate2 * mlp

def reference(tokens, mod_table, w_qkv, w_out_t, w_up, w_down, bins, present, cotangent):
    group = math.gcd(SLOTS, 16)
    steps_count = SLOTS // group
    weights = (w_qkv.astype(jnp.float32), w_out_t.astype(jnp.float32), w_up.astype(jnp.float32), w_down.astype(jnp.float32))
    xs = tokens.reshape(steps_count, group, SEQ, D)
    dys = cotangent.reshape(steps_count, group, SEQ, D)
    bs = bins.reshape(steps_count, group)
    ps = present.reshape(steps_count, group)

    def step(carry, items):
        block_x, block_dy, block_bins, block_present = items
        mask = block_present.astype(jnp.float32)[:, None, None]
        onehot = jax.nn.one_hot(block_bins, BINS, dtype=jnp.float32)
        result, pull = jax.vjp(partial(forward, onehot), block_x.astype(jnp.float32), mod_table, *weights)
        grads = pull(block_dy.astype(jnp.float32) * mask)
        new_carry = (carry[0] + grads[1], carry[1] + grads[2], carry[2] + grads[3], carry[3] + grads[4], carry[4] + grads[5])
        return (new_carry, ((result * mask).astype(jnp.bfloat16), grads[0]))
    start = (jnp.zeros((BINS, 6, D), jnp.float32), jnp.zeros((3, D, D), jnp.float32), jnp.zeros((D, D), jnp.float32), jnp.zeros((D, FF), jnp.float32), jnp.zeros((D, FF), jnp.float32))
    totals, outs = lax.scan(step, start, (xs, dys, bs, ps))
    block_out = outs[0].reshape(SLOTS, SEQ, D)
    input_grad = outs[1].reshape(SLOTS, SEQ, D)
    return (block_out, input_grad, totals[0], totals[1], totals[2], totals[3], totals[4])
```

```python
import jax
import jax.numpy as jnp
from jax import lax
from jax.experimental import pallas as pl
from jax.experimental.pallas import tpu as pltpu
from jax.sharding import PartitionSpec as P

HEAD_DIM = 128
EPS = 1e-06
HIGH = lax.Precision.HIGHEST
F32 = jnp.float32
BF16 = jnp.bfloat16


def layer_norm(value):
    centre = value - jnp.mean(value, axis=-1, keepdims=True)
    spread = jnp.mean(centre * centre, axis=-1, keepdims=True)
    return centre * lax.rsqrt(spread + EPS)


def modulate(value, shift, scale):
    return layer_norm(value) * (1.0 + scale) + shift


class Link:
    def __init__(self, name, perm, depth):
        self.name, self.perm, self.depth, self.done = name, perm, depth, []

    def send(self, value):
        if len(self.done) >= self.depth:
            value, _ = lax.optimization_barrier((value, self.done[-self.depth]))
        out = lax.ppermute(value, self.name, self.perm)
        self.done.append(out)
        return out


class Grid:
    def __init__(self, size):
        self.c = 2 if size % 2 == 0 else 1
        self.z = 4 if (size // self.c) % 4 == 0 else 1
        self.x = size // self.c // self.z
        self.size = size
        self.links = {
            "z": Link("dp", self.ring(1, 0, 0), 2),
            "x": Link("dp", self.ring(0, 1, 0), 2),
            "c": Link("dp", self.ring(0, 0, 1), 2),
        }
        me = lax.axis_index("dp")
        self.me = (me // (self.x * self.c), (me // self.c) % self.x, me % self.c)

    def index(self, z, x, c):
        return (z % self.z * self.x + x % self.x) * self.c + c % self.c

    def ring(self, dz, dx, dc):
        return [
            (self.index(z, x, c), self.index(z + dz, x + dx, c + dc))
            for z in range(self.z)
            for x in range(self.x)
            for c in range(self.c)
        ]

    def to_relative(self):
        z, x, c = self.me
        return jnp.stack(
            [
                self.index(z - kz + self.z, x - kx + self.x, c - kc + self.c)
                for kc in range(self.c)
                for kx in range(self.x)
                for kz in range(self.z)
            ]
        ).astype(jnp.int32)

    def to_absolute(self):
        z, x, c = self.me
        return jnp.stack(
            [
                ((c - oc) % self.c * self.x + (x - ox) % self.x) * self.z + (z - oz) % self.z
                for oz in range(self.z)
                for ox in range(self.x)
                for oc in range(self.c)
            ]
        ).astype(jnp.int32)

    def gather(self, shard, first):
        blocks = {(0, 0, 0): shard}
        place = {"c": 0, "x": 1, "z": 2}
        order = ("z", "x", "c") if first == "z" else ("x", "z", "c")
        for axis in order:
            at, count = place[axis], getattr(self, axis)
            base = list(blocks)
            for k in range(1, count):
                for key in base:
                    source = key[:at] + (k - 1,) + key[at + 1 :]
                    target = key[:at] + (k,) + key[at + 1 :]
                    blocks[target] = self.links[axis].send(blocks[source])
        return blocks

    def whole(self, blocks, axis):
        return jnp.concatenate([blocks[key] for key in sorted(blocks)], axis=axis)

    def reduce(self, lhs, rhs, first):
        width = lhs.shape[1] // (self.c * self.x)
        blk = width // self.z

        def product(kc, kx):
            at = (kc * self.x + kx) * width
            return lax.dot_general(
                lhs[:, at : at + width], rhs, (((0,), (0,)), ((), ())), preferred_element_type=F32
            )

        order = [kx for kx in range(self.x) if kx] + [0]
        kept = {}
        moving = {kx: None for kx in order}
        for kc in list(range(1, self.c)) + [0]:
            for kx in order:
                value = product(kc, kx)
                if moving[kx] is not None:
                    value = value + moving[kx].astype(F32)
                value = value.astype(BF16)
                if kc:
                    moving[kx] = self.links["c"].send(value)
                else:
                    kept[kx] = value
        part = lambda kx, kz: kept[kx][kz * blk : (kz + 1) * blk]
        zorder = list(range(1, self.z)) + [0]
        if first == "x":
            gone = {}
            for kz in zorder:
                gone[kz] = None
            for kx in order:
                for kz in zorder:
                    value = part(kx, kz)
                    if gone[kz] is not None:
                        value = value.astype(F32) + gone[kz].astype(F32)
                        value = value.astype(BF16) if kx else value
                    if kx:
                        gone[kz] = self.links["x"].send(value)
                    else:
                        gone[kz] = value.astype(F32)
            total = None
            for kz in zorder:
                value = gone[kz] if total is None else gone[kz] + total.astype(F32)
                if kz:
                    total = self.links["z"].send(value.astype(BF16))
            return value
        totals = {kx: None for kx in order}
        for kz in zorder:
            for kx in order:
                value = part(kx, kz).astype(F32)
                if totals[kx] is not None:
                    value = value + totals[kx].astype(F32)
                totals[kx] = self.links["z"].send(value.astype(BF16)) if kz else value
        total = None
        for kx in order:
            value = totals[kx] if total is None else totals[kx] + total.astype(F32)
            if kx:
                total = self.links["x"].send(value.astype(BF16))
        return value


def copy_block(order_ref, in_ref, out_ref):
    out_ref[...] = in_ref[...]


def reorder(value, order):
    count = order.shape[0]
    shape = value.shape
    flat = value.reshape(-1, shape[-1])
    blk = shape[-1] // count
    if blk % 128:
        return jnp.take(flat.reshape(-1, count, blk), order, axis=1).reshape(shape)
    out = pl.pallas_call(
        copy_block,
        grid_spec=pltpu.PrefetchScalarGridSpec(
            num_scalar_prefetch=1,
            grid=(count,),
            in_specs=[pl.BlockSpec((flat.shape[0], blk), lambda j, s: (0, s[j]))],
            out_specs=pl.BlockSpec((flat.shape[0], blk), lambda j, s: (0, j)),
        ),
        out_shape=jax.ShapeDtypeStruct(flat.shape, flat.dtype),
    )(order, flat)
    return out.reshape(shape)


def make_body(dp, mp):
    turn = [(i, (i + 1) % mp) for i in range(mp)]

    def across(part):
        total, moving = part.astype(F32), part
        for _ in range(mp - 1):
            moving = lax.ppermute(moving, "mp", turn)
            total = total + moving.astype(F32)
        return total

    def body(tokens, mod_table, w_qkv, w_out_t, w_up, w_down, bins, present, cotangent):
        count, length, width = tokens.shape
        rows_all = count * length
        grid = Grid(dp)
        relative, absolute = grid.to_relative(), grid.to_absolute()

        v_blocks = grid.gather(w_qkv[2], "x")
        o_blocks = grid.gather(w_out_t, "x")
        qk_blocks = grid.gather(w_qkv[:2], "z")
        u_blocks = grid.gather(w_up, "z")
        d_blocks = grid.gather(w_down, "z")
        w_qk, w_v, w_o, w_u, w_d = (
            grid.whole(qk_blocks, 1),
            grid.whole(v_blocks, 0),
            grid.whole(o_blocks, 0),
            grid.whole(u_blocks, 0),
            grid.whole(d_blocks, 0),
        )
        local_width = w_v.shape[1]
        local_heads = local_width // HEAD_DIM
        factor = HEAD_DIM ** (-0.5)

        bins_all = lax.all_gather(bins, "dp", axis=0, tiled=True)
        table_rows = jnp.arange(mod_table.shape[0])[None, :]
        onehot = (bins[:, None] == table_rows).astype(F32)
        onehot_all = (bins_all[:, None] == table_rows).astype(F32)
        mods = jnp.einsum("cb,btd->ctd", onehot, mod_table, precision=HIGH)
        mods = reorder(mods, relative)
        tokens = reorder(tokens, relative)
        cotangent = reorder(cotangent, relative)
        shift1, scale1, gate1 = (mods[:, 0:1], mods[:, 1:2], mods[:, 2:3])
        shift2, scale2, gate2 = (mods[:, 3:4], mods[:, 4:5], mods[:, 5:6])
        mask = present.astype(F32)[:, None, None]
        inputs = tokens.astype(F32)
        grad_dy = cotangent.astype(F32) * mask
        d_mlp = (gate2 * grad_dy).astype(BF16).reshape(rows_all, width)

        normed = modulate(inputs, shift1, scale1).astype(BF16).reshape(rows_all, width)
        qk = jnp.einsum("rd,tde->tre", normed, w_qk, preferred_element_type=F32).astype(BF16)
        val = jnp.einsum("rd,de->re", normed, w_v, preferred_element_type=F32).astype(BF16)
        query = qk[0].reshape(count, length, local_heads, HEAD_DIM)
        keys = qk[1].reshape(count, length, local_heads, HEAD_DIM)
        values = val.reshape(count, length, local_heads, HEAD_DIM)
        scores = jnp.einsum("cqhe,ckhe->chqk", query, keys, preferred_element_type=F32) * factor
        top = jnp.max(scores, axis=-1, keepdims=True)
        expo = jnp.exp(scores - top)
        total = jnp.sum(expo, axis=-1, keepdims=True)
        lse = top + jnp.log(total)
        probs_low = (expo / total).astype(BF16)
        mixed = jnp.einsum("chqk,ckhe->cqhe", probs_low, values, preferred_element_type=F32)
        mixed = mixed.astype(BF16).reshape(rows_all, local_width)
        att_part = jnp.einsum("re,de->rd", mixed, w_o, preferred_element_type=F32).astype(BF16)
        att = across(lax.optimization_barrier(att_part)).reshape(count, length, width)
        hidden = inputs + gate1 * att
        second = modulate(hidden, shift2, scale2).astype(BF16).reshape(rows_all, width)
        up_val = jnp.einsum("rd,df->rf", second, w_u, preferred_element_type=F32)
        act = jax.nn.gelu(up_val).astype(BF16)
        down_part = grid.reduce(d_mlp, act, "x")
        d_act = jnp.einsum("rd,df->rf", d_mlp, w_d, preferred_element_type=F32)
        _, gelu_pull = jax.vjp(jax.nn.gelu, up_val)
        d_up = gelu_pull(d_act)[0].astype(BF16)
        d_second_part = jnp.einsum("rf,df->rd", d_up, w_u, preferred_element_type=F32).astype(BF16)
        d_second = across(lax.optimization_barrier(d_second_part))
        up_part = grid.reduce(second, d_up, "x")
        mlp_part = jnp.einsum("rf,df->rd", act, w_d, preferred_element_type=F32).astype(BF16)
        mlp = across(lax.optimization_barrier(mlp_part)).reshape(count, length, width)
        block_out = (mask * (hidden + gate2 * mlp)).astype(BF16)
        block_out = reorder(block_out, absolute)
        g_gate2 = jnp.sum(grad_dy * mlp, axis=1)
        _, norm_pull2 = jax.vjp(modulate, hidden, shift2, scale2)
        d_hidden_n, g_shift2, g_scale2 = norm_pull2(d_second.reshape(count, length, width))
        d_hidden = grad_dy + d_hidden_n
        g_gate1 = jnp.sum(d_hidden * att, axis=1)
        d_att = (gate1 * d_hidden).astype(BF16).reshape(rows_all, width)
        d_mixed = jnp.einsum("rd,de->re", d_att, w_o, preferred_element_type=F32).astype(BF16)
        out_part = grid.reduce(d_att, mixed, "z")
        d_mixed = d_mixed.reshape(count, length, local_heads, HEAD_DIM)
        again = jnp.einsum("cqhe,ckhe->chqk", query, keys, preferred_element_type=F32) * factor
        probs = jnp.exp(again - lse)
        probs_again = probs.astype(BF16)
        d_probs = jnp.einsum("cqhe,ckhe->chqk", d_mixed, values, preferred_element_type=F32)
        d_values = jnp.einsum(
            "chqk,cqhe->ckhe", probs_again, d_mixed, preferred_element_type=F32
        ).astype(BF16)
        delta = jnp.sum(d_probs * probs, axis=-1, keepdims=True)
        d_scores = (probs * (d_probs - delta)).astype(BF16)
        d_query = (
            jnp.einsum("chqk,ckhe->cqhe", d_scores, keys, preferred_element_type=F32) * factor
        ).astype(BF16)
        d_keys = (
            jnp.einsum("chqk,cqhe->ckhe", d_scores, query, preferred_element_type=F32) * factor
        ).astype(BF16)
        d_query = d_query.reshape(rows_all, local_width)
        d_keys = d_keys.reshape(rows_all, local_width)
        d_values = d_values.reshape(rows_all, local_width)
        d_qk = jnp.stack([d_query, d_keys])
        d_normed_part = (
            jnp.einsum("tre,tde->rd", d_qk, w_qk, preferred_element_type=F32)
            + jnp.einsum("re,de->rd", d_values, w_v, preferred_element_type=F32)
        ).astype(BF16)
        d_normed = across(lax.optimization_barrier(d_normed_part))
        v_part = grid.reduce(normed, d_values, "z")
        qk_part = grid.reduce(normed, jnp.concatenate([d_query, d_keys], axis=1), "x")
        _, norm_pull1 = jax.vjp(modulate, inputs, shift1, scale1)
        d_input_n, g_shift1, g_scale1 = norm_pull1(d_normed.reshape(count, length, width))
        input_grad = reorder(d_hidden + d_input_n, absolute)
        d_mods = jnp.stack(
            [g_shift1[:, 0], g_scale1[:, 0], g_gate1, g_shift2[:, 0], g_scale2[:, 0], g_gate2],
            axis=1,
        )
        d_mods = reorder(d_mods, absolute)
        d_mods = lax.all_to_all(d_mods, "dp", split_axis=2, concat_axis=0, tiled=True)
        table_part = jnp.einsum("sb,std->btd", onehot_all, d_mods, precision=HIGH)
        qkv_part = jnp.stack(
            [qk_part[:, :local_width], qk_part[:, local_width:], v_part], axis=0
        )
        return (block_out, input_grad, table_part, qkv_part, out_part, up_part, down_part)

    return body


def solution(mesh):
    in_specs = (
        P("dp", None, None),
        P(),
        P(None, "dp", "mp"),
        P("dp", "mp"),
        P("dp", "mp"),
        P("dp", "mp"),
        P("dp"),
        P("dp"),
        P("dp", None, None),
    )
    out_specs = (
        P("dp", None, None),
        P("dp", None, None),
        P(None, None, "dp"),
        P(None, "dp", "mp"),
        P("dp", "mp"),
        P("dp", "mp"),
        P("dp", "mp"),
    )
    body = make_body(mesh.shape["dp"], mesh.shape["mp"])
    return jax.shard_map(body, mesh=mesh, in_specs=in_specs, out_specs=out_specs, check_vma=False)
```

```python
import jax
import jax.numpy as jnp
from jax import lax
from jax.experimental import pallas as pl
from jax.experimental.pallas import tpu as pltpu
from jax.sharding import PartitionSpec as P

HEAD_DIM = 128
EPS = 1e-06
HIGH = lax.Precision.HIGHEST
F32 = jnp.float32
BF16 = jnp.bfloat16
CORES = 2


def layer_norm(value):
    centre = value - jnp.mean(value, axis=-1, keepdims=True)
    spread = jnp.mean(centre * centre, axis=-1, keepdims=True)
    return centre * lax.rsqrt(spread + EPS)


def modulate(value, shift, scale):
    return layer_norm(value) * (1.0 + scale) + shift


def after(value, *earlier):
    return lax.optimization_barrier((value, *earlier))[0]


def pass_on(in_ref, out_ref):
    out_ref[...] = in_ref[...]


def pace(token, cost):
    return pl.pallas_call(
        pass_on,
        out_shape=jax.ShapeDtypeStruct(token.shape, token.dtype),
        cost_estimate=pl.CostEstimate(
            flops=int(cost * 1.15e9), bytes_accessed=8192, transcendentals=0
        ),
    )(token)


class Phases:
    def __init__(self, dp, mp):
        self.z = 4 if (dp // CORES) % 4 == 0 else 1
        self.x = dp // CORES // self.z
        self.tail, self.results, self.sent, self.last = (), [], [], ()
        self.turn = [(i, (i + 1) % mp) for i in range(mp)]
        self.token = jnp.zeros((8, 128), F32)

    def ring(self, dz, dx, dc):
        index = lambda z, x, c: (z % self.z * self.x + x % self.x) * CORES + c % CORES
        return [
            (index(z, x, c), index(z + dz, x + dx, c + dc))
            for z in range(self.z)
            for x in range(self.x)
            for c in range(CORES)
        ]

    def send(self, value, dz, dx, hold=True):
        value = after(value, *self.tail)
        self.sent.append(value)
        out = lax.ppermute(value, "dp", self.ring(dz, dx, 0))
        if hold:
            self.results.append(out)
        return out

    def send_z(self, value, places):
        return self.send(value, places, 0)

    def send_x(self, value):
        return self.send(value, 0, 1)

    def send_core(self, value):
        return lax.ppermute(value, "dp", self.ring(0, 0, 1))

    def across(self, part):
        out = [lax.optimization_barrier(part)]
        for _ in range(len(self.turn) - 1):
            out.append(lax.ppermute(out[-1], "mp", self.turn))
        return out

    def now(self, value):
        return after(value, *self.tail)

    def begin(self, value):
        return after(value, *self.tail, *self.sent, *self.last)

    def end(self, *values):
        self.last = values

    def close(self, cost=25.0):
        self.token = pace(after(self.token, *self.tail, *self.sent), cost)
        self.tail = (*self.results, *self.last, self.token)
        self.results, self.sent, self.last = [], [], ()

    def gather_x(self, piece):
        pieces = [piece]
        for _ in range(1, self.x):
            pieces.append(self.send_x(pieces[-1]))
        return pieces

    def reduce_x(self, blocks):
        moving = None
        for kx in range(1, self.x):
            value = blocks[kx]
            if moving is not None:
                value = value.astype(F32) + moving.astype(F32)
            moving = self.send_x(value.astype(BF16))
        return moving


def plus(first, *others):
    total = first.astype(F32)
    for other in others:
        if other is not None:
            total = total + other.astype(F32)
    return total


class Grid:
    def __init__(self, phases):
        self.z, self.x, self.phases = phases.z, phases.x, phases
        me = lax.axis_index("dp")
        self.at_z, self.at_x, self.core = (
            me // (self.x * CORES),
            (me // CORES) % self.x,
            me % CORES,
        )

    def to_relative(self):
        return jnp.stack(
            [
                (self.at_z - kz) % self.z * self.x + (self.at_x - kx) % self.x
                for kx in range(self.x)
                for kz in range(self.z)
            ]
        ).astype(jnp.int32)

    def to_absolute(self):
        return jnp.stack(
            [
                (self.at_x - ox) % self.x * self.z + (self.at_z - oz) % self.z
                for oz in range(self.z)
                for ox in range(self.x)
            ]
        ).astype(jnp.int32)

    def by_core(self, first, second, axis):
        return jnp.where(
            self.core == 0,
            jnp.concatenate([first, second], axis=axis),
            jnp.concatenate([second, first], axis=axis),
        )

    def halves(self, value, axis):
        half = value.shape[axis] // 2
        low = lax.slice_in_dim(value, 0, half, axis=axis)
        high = lax.slice_in_dim(value, half, 2 * half, axis=axis)
        return (
            jnp.where(self.core == 0, low, high),
            jnp.where(self.core == 0, high, low),
        )

    def chip_shard(self, shard):
        mine, theirs = self.halves(shard, 1)
        return self.by_core(mine, self.phases.send_core(theirs), 0)

    def own_rows(self, total):
        mine, theirs = self.halves(total, total.ndim - 2)
        return self.by_core(mine, self.phases.send_core(theirs), total.ndim - 1)

    def dots(self, lhs, rhs, kx):
        width = lhs.shape[1] // self.x
        return lax.dot_general(
            lhs[:, kx * width : (kx + 1) * width],
            rhs,
            (((0,), (0,)), ((), ())),
            preferred_element_type=F32,
        ).astype(BF16)


def copy_block(order_ref, in_ref, out_ref):
    out_ref[...] = in_ref[...]


def reorder(value, order):
    count = order.shape[0]
    shape = value.shape
    flat = value.reshape(-1, shape[-1])
    blk = shape[-1] // count
    if blk % 128:
        return jnp.take(flat.reshape(-1, count, blk), order, axis=1).reshape(shape)
    out = pl.pallas_call(
        copy_block,
        grid_spec=pltpu.PrefetchScalarGridSpec(
            num_scalar_prefetch=1,
            grid=(count,),
            in_specs=[pl.BlockSpec((flat.shape[0], blk), lambda j, s: (0, s[j]))],
            out_specs=pl.BlockSpec((flat.shape[0], blk), lambda j, s: (0, j)),
        ),
        out_shape=jax.ShapeDtypeStruct(flat.shape, flat.dtype),
    )(order, flat)
    return out.reshape(shape)


def matmul(lhs, rhs, turned=False):
    return lax.dot_general(
        lhs, rhs, (((1,), (1 if turned else 0,)), ((), ())), preferred_element_type=F32
    )


def make_body(dp, mp):
    def body(tokens, mod_table, w_qkv, w_out_t, w_up, w_down, bins, present, cotangent):
        count, length, width = tokens.shape
        rows = count * length
        ph = Phases(dp, mp)
        grid = Grid(ph)
        relative, absolute = grid.to_relative(), grid.to_absolute()
        turns = list(range(1, grid.x)) + [0]
        join = lambda own, theirs: jnp.concatenate([own, theirs], axis=0)

        def whole(*by_z):
            return jnp.concatenate(
                [by_z[kz][kx] for kx in range(grid.x) for kz in range(grid.z)], axis=0
            )

        def summed(value, weight, between=None):
            part = matmul(ph.begin(value[rows:]), weight, True).astype(BF16)
            ph.end(part)
            theirs = ph.send_core(part)
            if between is not None:
                between()
            part = matmul(ph.begin(value[:rows]), weight, True) + theirs.astype(F32)
            part = part.astype(BF16)
            ph.end(part)
            return ph.across(part)

        def from_both(theirs, value, weight, between=None):
            if between is not None:
                between()
            part = matmul(ph.begin(value[:rows]), weight, True) + theirs.astype(F32)
            part = part.astype(BF16)
            ph.end(part)
            return ph.across(part)

        def dots(lhs, rhs):
            kept = {}
            for kx in turns:
                kept[kx] = grid.dots(ph.begin(lhs), rhs, kx)
                ph.end(kept[kx])
            return kept

        def rows_of(kept, low, high):
            blk = width // grid.x // grid.z
            return {kx: kept[kx][low * blk : high * blk] for kx in kept}

        wide = w_qkv.reshape(3, -1, CORES, w_qkv.shape[2] // CORES).transpose(1, 2, 0, 3)
        s_q = grid.chip_shard(wide.reshape(w_qkv.shape[1], -1))
        z_q, x_q = {1: ph.send_z(s_q, 1)}, {0: ph.gather_x(s_q)}
        s_o = grid.chip_shard(ph.begin(w_out_t))
        ph.end(s_o)
        x_o = jnp.stack(ph.gather_x(s_o))
        table_rows = jnp.arange(mod_table.shape[0])[None, :]
        onehot = (bins[:, None] == table_rows).astype(F32)
        mods = jnp.einsum("cb,btd->ctd", ph.begin(onehot), mod_table, precision=HIGH)
        mods = reorder(mods, relative)
        ph.end(mods)
        ph.close()

        z_q[3] = ph.send_z(s_q, 3)
        x_q[1] = ph.gather_x(z_q[1])
        tokens = reorder(ph.begin(tokens), relative)
        shift1, scale1, gate1 = (mods[:, 0:1], mods[:, 1:2], mods[:, 2:3])
        shift2, scale2, gate2 = (mods[:, 3:4], mods[:, 4:5], mods[:, 5:6])
        mask = present.astype(F32)[:, None, None]
        inputs = tokens.astype(F32)
        normed_own = modulate(inputs, shift1, scale1).astype(BF16).reshape(rows, width)
        ph.end(normed_own)
        ph.close()

        z_q[2] = ph.send_z(z_q[1], 1)
        x_q[3] = ph.gather_x(z_q[3])
        normed_other = ph.send_core(ph.now(normed_own))
        s_u = grid.chip_shard(ph.begin(w_up))
        ph.end(s_u)
        normed = join(normed_own, ph.begin(normed_other))
        ph.end(normed)
        ph.close()

        z_o = {0: x_o, 1: ph.send_z(x_o, 1)}
        x_q[2] = ph.gather_x(z_q[2])
        s_d = grid.chip_shard(ph.begin(w_down))
        ph.end(s_d)
        ph.close()

        z_o[3] = ph.send_z(x_o, 3)
        z_o[2] = ph.send_z(z_o[1], 1)
        x_u = {0: ph.gather_x(s_u)}
        w_a = whole(x_q[0], x_q[1], x_q[2], x_q[3])
        local_width = s_o.shape[1]
        local_heads = local_width // HEAD_DIM
        factor = HEAD_DIM ** (-0.5)
        per_head = lambda value: value.reshape(CORES * count, length, local_heads, HEAD_DIM)
        qkv = matmul(ph.begin(normed), w_a).astype(BF16)
        ph.end(qkv)
        query, keys, values = (per_head(part) for part in jnp.split(ph.begin(qkv), 3, axis=1))
        scores = jnp.einsum("cqhe,ckhe->chqk", query, keys, preferred_element_type=F32) * factor
        top = jnp.max(scores, axis=-1, keepdims=True)
        expo = jnp.exp(scores - top)
        total = jnp.sum(expo, axis=-1, keepdims=True)
        lse = top + jnp.log(total)
        probs_low = (expo / total).astype(BF16)
        ph.end(probs_low)
        ph.close()

        z_u = {1: ph.send_z(s_u, 1)}
        x_d = {0: ph.gather_x(s_d)}
        w_o = jnp.concatenate([z_o[kz][kx] for kx in range(grid.x) for kz in range(grid.z)], axis=0)
        probs_low = ph.begin(probs_low)
        mixed = jnp.einsum("chqk,ckhe->cqhe", probs_low, values, preferred_element_type=F32)
        mixed = mixed.astype(BF16).reshape(CORES * rows, local_width)
        ph.end(mixed)
        att = summed(mixed, w_o)
        ph.close()

        z_u[3] = ph.send_z(s_u, 3)
        x_u[1] = ph.gather_x(z_u[1])
        cotangent = reorder(ph.begin(cotangent), relative)
        grad_dy = cotangent.astype(F32) * mask
        d_mlp_own = (gate2 * grad_dy).astype(BF16).reshape(rows, width)
        ph.end(d_mlp_own)
        ph.close()

        z_u[2] = ph.send_z(z_u[1], 1)
        x_u[3] = ph.gather_x(z_u[3])
        d_mlp = join(d_mlp_own, ph.begin(ph.send_core(ph.now(d_mlp_own))))
        ph.end(d_mlp)
        att[-1] = ph.begin(att[-1])
        att = plus(*att).reshape(count, length, width)
        hidden = inputs + gate1 * att
        second_own = modulate(hidden, shift2, scale2).astype(BF16).reshape(rows, width)
        ph.end(second_own)
        ph.close()

        z_d = {1: ph.send_z(s_d, 1)}
        x_u[2] = ph.gather_x(z_u[2])
        second = join(second_own, ph.begin(ph.send_core(ph.now(second_own))))
        ph.end(second)
        ph.close()

        z_d[3] = ph.send_z(s_d, 3)
        x_d[1] = ph.gather_x(z_d[1])
        w_u = whole(x_u[0], x_u[1], x_u[2], x_u[3])
        up_val = matmul(ph.begin(second), w_u)
        act = jax.nn.gelu(up_val).astype(BF16)
        ph.end(act)
        ph.close()

        z_d[2] = ph.send_z(z_d[1], 1)
        x_d[3] = ph.gather_x(z_d[3])
        down = dots(d_mlp, act)
        half = down[0].shape[1] // 2
        first = jnp.stack([down[kx][:, :half] for kx in range(grid.x)])
        other = {kx: down[kx][:, half:] for kx in down}
        ph.end(first)
        ph.close()

        blk = first.shape[1] // grid.z
        part = lambda stacked, kz: stacked[:, kz * blk : (kz + 1) * blk]
        x_d[2] = ph.gather_x(z_d[2])
        a_2 = ph.send_z(part(first, 2), 3)
        ph.close()

        x_b = {2: ph.reduce_x(rows_of(other, 2, 4))}
        a_3 = ph.send_z(part(first, 3), 1)
        w_d = whole(x_d[0], x_d[1], x_d[2], x_d[3])
        d_act = matmul(ph.begin(d_mlp), w_d)
        _, gelu_pull = jax.vjp(jax.nn.gelu, up_val)
        d_up = gelu_pull(d_act)[0].astype(BF16)
        ph.end(d_up)
        up = {}
        d_second_part = matmul(ph.begin(d_up)[rows:], w_u, True).astype(BF16)
        ph.end(d_second_part)
        ph.close()

        def up_dots(blocks):
            for kx in blocks:
                up[kx] = grid.dots(ph.begin(second), d_up, kx)
                ph.end(up[kx])

        x_b[0] = ph.reduce_x(rows_of(other, 0, 2))
        a_1 = ph.send_z(plus(part(first, 1), ph.now(a_2)).astype(BF16), 3)
        d_second = from_both(ph.send_core(ph.now(d_second_part)), d_up, w_u, lambda: up_dots(turns[:-1]))
        ph.close()

        up_rows = lambda kz: ph.reduce_x(rows_of(up, kz, kz + 1))
        x_up = {2: up_rows(2)}
        b_part = lambda kz: ph.now(x_b[kz // 2 * 2][(kz % 2) * blk : (kz % 2 + 1) * blk])
        b_sum = lambda kz: plus(rows_of(other, kz, kz + 1)[0], b_part(kz))
        b_2 = ph.send_z(b_sum(2).astype(BF16), 3)
        b_3 = ph.send_z(b_sum(3).astype(BF16), 1)
        up_dots(turns[-1:])
        mlp_part = matmul(ph.begin(act)[rows:], w_d, True).astype(BF16)
        ph.end(mlp_part)
        ph.close()

        x_up[3] = up_rows(3)
        up_sum = lambda kz: plus(rows_of(up, kz, kz + 1)[0], ph.now(x_up[kz]))
        u_2 = ph.send_z(up_sum(2).astype(BF16), 3)
        mlp = from_both(ph.send_core(ph.now(mlp_part)), act, w_d)
        d_second[-1] = ph.begin(d_second[-1])
        d_second = plus(*d_second)
        _, norm_pull2 = jax.vjp(modulate, hidden, shift2, scale2)
        d_hidden_n, g_shift2, g_scale2 = norm_pull2(d_second.reshape(count, length, width))
        d_hidden = grad_dy + d_hidden_n
        g_gate1 = jnp.sum(d_hidden * att, axis=1)
        d_att_own = (gate1 * d_hidden).astype(BF16).reshape(rows, width)
        ph.end(d_att_own)
        ph.close()

        x_up[1] = up_rows(1)
        u_3 = ph.send_z(up_sum(3).astype(BF16), 1)
        d_att = join(d_att_own, ph.begin(ph.send_core(ph.now(d_att_own))))
        d_mixed = matmul(d_att, w_o).astype(BF16)
        ph.end(d_mixed)
        d_mixed = per_head(ph.begin(d_mixed))
        again = jnp.einsum("cqhe,ckhe->chqk", query, keys, preferred_element_type=F32) * factor
        probs = jnp.exp(again - lse)
        probs_again = probs.astype(BF16)
        d_probs = jnp.einsum("cqhe,ckhe->chqk", d_mixed, values, preferred_element_type=F32)
        delta = jnp.sum(d_probs * probs, axis=-1, keepdims=True)
        d_scores = (probs * (d_probs - delta)).astype(BF16)
        d_values = jnp.einsum(
            "chqk,cqhe->ckhe", probs_again, d_mixed, preferred_element_type=F32
        ).astype(BF16)
        d_query = (
            jnp.einsum("chqk,ckhe->cqhe", d_scores, keys, preferred_element_type=F32) * factor
        ).astype(BF16)
        d_keys = (
            jnp.einsum("chqk,cqhe->ckhe", d_scores, query, preferred_element_type=F32) * factor
        ).astype(BF16)
        flat = lambda value: value.reshape(CORES * rows, local_width)
        d_qkv = jnp.concatenate([flat(d_query), flat(d_keys), flat(d_values)], axis=1)
        ph.end(d_qkv)
        ph.close()

        x_up[0] = up_rows(0)
        u_1 = ph.send_z((up_sum(1) + ph.now(u_2).astype(F32)).astype(BF16), 3)
        d_normed_part = matmul(ph.begin(d_qkv)[rows:], w_a, True).astype(BF16)
        ph.end(d_normed_part)
        out = {}

        def out_dots():
            out.update(dots(d_att, mixed))

        d_normed = from_both(ph.send_core(d_normed_part), d_qkv, w_a, out_dots)
        proj = dots(normed, d_qkv)
        ph.close()

        x_out = ph.reduce_x(out)
        b_1 = ph.send_z((b_sum(1) + ph.now(b_2).astype(F32)).astype(BF16), 3)
        mlp[-1] = ph.begin(mlp[-1])
        mlp = plus(*mlp).reshape(count, length, width)
        block_out = (mask * (hidden + gate2 * mlp)).astype(BF16)
        block_out = reorder(block_out, absolute)
        g_gate2 = jnp.sum(grad_dy * mlp, axis=1)
        ph.end(block_out, g_gate2)
        ph.close()

        p_rows = lambda kz: ph.reduce_x(rows_of(proj, kz, kz + 1))
        p_sum = lambda kz: plus(rows_of(proj, kz, kz + 1)[0], ph.now(x_p[kz]))
        out_sum = lambda kz: plus(
            rows_of(out, kz, kz + 1)[0], ph.now(x_out[kz * blk : (kz + 1) * blk])
        )
        x_p = {2: p_rows(2)}
        o_2 = ph.send_z(out_sum(2).astype(BF16), 3)
        o_3 = ph.send_z(out_sum(3).astype(BF16), 1)
        up_part = up_sum(0) + ph.now(u_3).astype(F32) + ph.now(u_1).astype(F32)
        up_part = grid.own_rows(ph.begin(up_part))
        ph.end(up_part)
        ph.close(20.0)

        x_p[3] = p_rows(3)
        p_2 = ph.send_z(p_sum(2).astype(BF16), 3)
        d_normed[-1] = ph.begin(d_normed[-1])
        d_normed = plus(*d_normed)
        _, norm_pull1 = jax.vjp(modulate, inputs, shift1, scale1)
        d_input_n, g_shift1, g_scale1 = norm_pull1(d_normed.reshape(count, length, width))
        input_grad = d_hidden + d_input_n
        ph.end(input_grad)
        ph.close(20.0)

        x_p[1] = p_rows(1)
        p_3 = ph.send_z(p_sum(3).astype(BF16), 1)
        input_grad = reorder(ph.begin(input_grad), absolute)
        d_mods = jnp.stack(
            [g_shift1[:, 0], g_scale1[:, 0], g_gate1, g_shift2[:, 0], g_scale2[:, 0], g_gate2],
            axis=1,
        )
        d_mods = reorder(d_mods, absolute)
        bin_row = jnp.broadcast_to(bins.astype(F32)[:, None, None], (count, 1, width))
        d_mods = jnp.concatenate([d_mods, bin_row], axis=1)
        ph.end(input_grad, d_mods)
        ph.close(20.0)

        x_p[0] = p_rows(0)
        p_1 = ph.send_z((p_sum(1) + ph.now(p_2).astype(F32)).astype(BF16), 3)
        d_mods = lax.all_to_all(ph.now(d_mods), "dp", split_axis=2, concat_axis=0, tiled=True)
        d_mods = ph.begin(d_mods)
        onehot_all = (d_mods[:, 6, :1] == table_rows.astype(F32)).astype(F32)
        table_part = jnp.einsum("sb,std->btd", onehot_all, d_mods[:, :6], precision=HIGH)
        ph.end(table_part)
        ph.close(20.0)

        first_sum = plus(part(first, 0), a_3, a_1)
        x_first = ph.reduce_x(first_sum.astype(BF16))
        o_1 = ph.send_z((out_sum(1) + ph.now(o_2).astype(F32)).astype(BF16), 3)
        qkv_part = p_sum(0) + ph.now(p_3).astype(F32) + ph.now(p_1).astype(F32)
        qkv_part = qkv_part.reshape(-1, 3, local_width).transpose(1, 0, 2)
        qkv_part = grid.own_rows(ph.begin(qkv_part))
        ph.end(qkv_part)
        ph.close(15.0)

        down_low = plus(ph.now(first_sum)[0], x_first)
        down_high = b_sum(0) + ph.now(b_3).astype(F32) + ph.now(b_1).astype(F32)
        down_part = grid.own_rows(jnp.concatenate([down_low, down_high], axis=1))
        out_part = grid.own_rows(out_sum(0) + ph.now(o_3).astype(F32) + ph.now(o_1).astype(F32))
        return (block_out, input_grad, table_part, qkv_part, out_part, up_part, down_part)

    return body


def solution(mesh):
    in_specs = (
        P("dp", None, None),
        P(),
        P(None, "dp", "mp"),
        P("dp", "mp"),
        P("dp", "mp"),
        P("dp", "mp"),
        P("dp"),
        P("dp"),
        P("dp", None, None),
    )
    out_specs = (
        P("dp", None, None),
        P("dp", None, None),
        P(None, None, "dp"),
        P(None, "dp", "mp"),
        P("dp", "mp"),
        P("dp", "mp"),
        P("dp", "mp"),
    )
    body = make_body(mesh.shape["dp"], mesh.shape["mp"])
    return jax.shard_map(body, mesh=mesh, in_specs=in_specs, out_specs=out_specs, check_vma=False)
```

```python
import functools

import jax
import jax.numpy as jnp
from jax import lax
from jax.experimental import pallas as pl
from jax.experimental.pallas import tpu as pltpu
from jax.sharding import PartitionSpec as P

HEAD_DIM = 128
EPS = 1e-06
HIGH = lax.Precision.HIGHEST
F32 = jnp.float32
BF16 = jnp.bfloat16
CORES = 2
TILE = 128
CHUNK = 16


def after(value, *earlier):
    return lax.optimization_barrier((value, *earlier))[0]


def pass_on(in_ref, out_ref):
    out_ref[...] = in_ref[...]


def pace(token, cost):
    return pl.pallas_call(
        pass_on,
        out_shape=jax.ShapeDtypeStruct(token.shape, token.dtype),
        cost_estimate=pl.CostEstimate(
            flops=int(cost * 1.15e9), bytes_accessed=8192, transcendentals=0
        ),
    )(token)


class Phases:
    def __init__(self, dp, mp):
        self.z = 4 if (dp // CORES) % 4 == 0 else 1
        self.x = dp // CORES // self.z
        self.tail, self.results, self.sent, self.last = (), [], [], ()
        self.turn = [(i, (i + 1) % mp) for i in range(mp)]
        self.token = jnp.zeros((8, 128), F32)

    def ring(self, dz, dx, dc):
        index = lambda z, x, c: (z % self.z * self.x + x % self.x) * CORES + c % CORES
        return [
            (index(z, x, c), index(z + dz, x + dx, c + dc))
            for z in range(self.z)
            for x in range(self.x)
            for c in range(CORES)
        ]

    def send(self, value, dz, dx, hold=True):
        value = after(value, *self.tail)
        self.sent.append(value)
        out = lax.ppermute(value, "dp", self.ring(dz, dx, 0))
        if hold:
            self.results.append(out)
        return out

    def send_z(self, value, places):
        return self.send(value, places, 0)

    def send_x(self, value):
        return self.send(value, 0, 1)

    def send_core(self, value):
        return lax.ppermute(value, "dp", self.ring(0, 0, 1))

    def hand_over(self, value):
        out = self.send_core(value)
        self.results.append(out)
        return out

    def across(self, part):
        out = [lax.optimization_barrier(part)]
        for _ in range(len(self.turn) - 1):
            out.append(lax.ppermute(out[-1], "mp", self.turn))
        return out

    def now(self, value):
        return after(value, *self.tail)

    def begin(self, value):
        return after(value, *self.tail, *self.sent, *self.last)

    def end(self, *values):
        self.last = values

    def close(self, cost=25.0):
        self.token = pace(after(self.token, *self.tail, *self.sent), cost)
        self.tail = (*self.results, *self.last, self.token)
        self.results, self.sent, self.last = [], [], ()

    def gather_x(self, piece):
        pieces = [piece]
        for _ in range(1, self.x):
            pieces.append(self.send_x(pieces[-1]))
        return pieces

    def reduce_x(self, blocks):
        moving = None
        for kx in range(1, self.x):
            value = blocks[kx]
            if moving is not None:
                value = value.astype(F32) + moving.astype(F32)
            moving = self.send_x(value.astype(BF16))
        return moving


def plus(first, *others):
    total = first.astype(F32)
    for other in others:
        if other is not None:
            total = total + other.astype(F32)
    return total


class Grid:
    def __init__(self, phases):
        self.z, self.x, self.phases = phases.z, phases.x, phases
        me = lax.axis_index("dp")
        self.at_z, self.at_x, self.core = (
            me // (self.x * CORES),
            (me // CORES) % self.x,
            me % CORES,
        )

    def to_relative(self):
        return jnp.stack(
            [
                (self.at_z - kz) % self.z * self.x + (self.at_x - kx) % self.x
                for kx in range(self.x)
                for kz in range(self.z)
            ]
        ).astype(jnp.int32)

    def to_absolute(self):
        return jnp.stack(
            [
                (self.at_x - ox) % self.x * self.z + (self.at_z - oz) % self.z
                for oz in range(self.z)
                for ox in range(self.x)
            ]
        ).astype(jnp.int32)

    def by_core(self, first, second, axis):
        return jnp.where(
            self.core == 0,
            jnp.concatenate([first, second], axis=axis),
            jnp.concatenate([second, first], axis=axis),
        )

    def halves(self, value, axis):
        half = value.shape[axis] // 2
        low = lax.slice_in_dim(value, 0, half, axis=axis)
        high = lax.slice_in_dim(value, half, 2 * half, axis=axis)
        return (
            jnp.where(self.core == 0, low, high),
            jnp.where(self.core == 0, high, low),
        )

    def chip_shard(self, shard):
        mine, theirs = self.halves(shard, 1)
        return self.by_core(mine, self.phases.send_core(theirs), 0)

    def own_rows(self, total):
        mine, theirs = self.halves(total, total.ndim - 2)
        return self.by_core(mine, self.phases.send_core(theirs), total.ndim - 1)

    def dots(self, lhs, rhs, kx):
        width = lhs.shape[1] // self.x
        return lax.dot_general(
            lhs[:, kx * width : (kx + 1) * width],
            rhs,
            (((0,), (0,)), ((), ())),
            preferred_element_type=F32,
        ).astype(BF16)


def copy_block(order_ref, in_ref, out_ref):
    out_ref[...] = in_ref[...]


def reorder(value, order):
    count = order.shape[0]
    shape = value.shape
    flat = value.reshape(-1, shape[-1])
    blk = shape[-1] // count
    if blk % 128:
        return jnp.take(flat.reshape(-1, count, blk), order, axis=1).reshape(shape)
    out = pl.pallas_call(
        copy_block,
        grid_spec=pltpu.PrefetchScalarGridSpec(
            num_scalar_prefetch=1,
            grid=(count,),
            in_specs=[pl.BlockSpec((flat.shape[0], blk), lambda j, s: (0, s[j]))],
            out_specs=pl.BlockSpec((flat.shape[0], blk), lambda j, s: (0, j)),
        ),
        out_shape=jax.ShapeDtypeStruct(flat.shape, flat.dtype),
    )(order, flat)
    return out.reshape(shape)


def dot(lhs, rhs, left, right):
    return lax.dot_general(lhs, rhs, (((left,), (right,)), ((), ())), preferred_element_type=F32)


def softmax(query, keys):
    scores = dot(query, keys, 1, 1) * HEAD_DIM ** (-0.5)
    expo = jnp.exp(scores - jnp.max(scores, axis=-1, keepdims=True))
    return expo / jnp.sum(expo, axis=-1, keepdims=True)


def head_cols(part, head, heads):
    return pl.ds((part * heads + head) * HEAD_DIM, HEAD_DIM)


def attend_kernel(heads, qkv_ref, mixed_ref):
    for head in range(heads):
        query, keys, values = (qkv_ref[:, head_cols(part, head, heads)] for part in range(3))
        probs = softmax(query, keys).astype(BF16)
        mixed = dot(probs, values, 1, 0).astype(BF16)
        mixed_ref[:, head_cols(0, head, heads)] = mixed


def attend_back_kernel(heads, qkv_ref, d_mixed_ref, d_qkv_ref):
    factor = HEAD_DIM ** (-0.5)
    for head in range(heads):
        query, keys, values = (qkv_ref[:, head_cols(part, head, heads)] for part in range(3))
        d_mixed = d_mixed_ref[:, head_cols(0, head, heads)]
        probs = softmax(query, keys)
        d_probs = dot(d_mixed, values, 1, 1)
        d_values = dot(probs.astype(BF16), d_mixed, 0, 0)
        delta = jnp.sum(d_probs * probs, axis=-1, keepdims=True)
        d_scores = (probs * (d_probs - delta)).astype(BF16)
        d_query = dot(d_scores, keys, 1, 0) * factor
        d_keys = dot(d_scores, query, 0, 0) * factor
        d_qkv_ref[:, head_cols(0, head, heads)] = d_query.astype(BF16)
        d_qkv_ref[:, head_cols(1, head, heads)] = d_keys.astype(BF16)
        d_qkv_ref[:, head_cols(2, head, heads)] = d_values.astype(BF16)


def by_image(kernel, length, width, *operands):
    rows = operands[0].shape[0]
    block = lambda cols: pl.BlockSpec((length, cols), lambda image: (image, 0))
    return pl.pallas_call(
        kernel,
        grid=(rows // length,),
        in_specs=[block(operand.shape[1]) for operand in operands],
        out_specs=block(width),
        out_shape=jax.ShapeDtypeStruct((rows, width), BF16),
        compiler_params=pltpu.CompilerParams(vmem_limit_bytes=32 * 1024 * 1024),
        cost_estimate=pl.CostEstimate(
            flops=rows * length * width * 8, bytes_accessed=rows * 8192, transcendentals=rows * 1024
        ),
    )(*operands)


def normal(value):
    centre = value - jnp.mean(value, axis=-1, keepdims=True)
    factor = lax.rsqrt(jnp.mean(centre * centre, axis=-1, keepdims=True) + EPS)
    return centre * factor, factor


def normal_back(grad, unit, factor):
    mean = jnp.mean(grad, axis=-1, keepdims=True)
    along = jnp.mean(grad * unit, axis=-1, keepdims=True)
    return factor * (grad - mean - unit * along)


class Rows:
    def __init__(self, blocks, order_ref, width):
        self.blocks, self.order, self.width = blocks, order_ref, width

    def each(self, count, body):
        def step(index, carry):
            body(pl.ds(pl.multiple_of(index * CHUNK, CHUNK), CHUNK))
            return carry

        lax.fori_loop(0, count // CHUNK, step, 0)

    def places(self):
        if not self.blocks:
            return [(slice(0, self.width), slice(0, self.width))]
        blk = self.width // self.blocks
        return [
            (
                slice(k * blk, (k + 1) * blk),
                pl.ds(pl.multiple_of(self.order[k] * blk, blk), blk),
            )
            for k in range(self.blocks)
        ]


def clear_sums(sums_ref):
    @pl.when(pl.program_id(1) == 0)
    def _():
        sums_ref[...] = jnp.zeros_like(sums_ref)


def add_sums(sums_ref, places, *terms):
    for index, term in enumerate(terms):
        low, high = term[:8], term[8:]
        for here, there in places:
            sums_ref[0, index * 8 : index * 8 + 8, there] += low[:, here] + high[:, here]


def first_norm_kernel(blocks, order_ref, present_ref, tokens_ref, mods_ref, kept_ref, normed_ref):
    rows = Rows(blocks, order_ref, tokens_ref.shape[1])
    for here, there in rows.places():
        kept_ref[:, here] = tokens_ref[:, there]

    def body(some):
        unit, _ = normal(kept_ref[some, :].astype(F32))
        value = unit * (1.0 + mods_ref[0, 1:2, :]) + mods_ref[0, 0:1, :]
        normed_ref[some, :] = value.astype(BF16)

    rows.each(tokens_ref.shape[0], body)


def cotangent_kernel(blocks, order_ref, present_ref, cotangent_ref, mods_ref, dy_ref, d_mlp_ref):
    rows = Rows(blocks, order_ref, cotangent_ref.shape[1])
    mask = present_ref[pl.program_id(0)].astype(F32)
    for here, there in rows.places():
        dy = cotangent_ref[:, there].astype(F32) * mask
        dy_ref[:, here] = dy.astype(BF16)
        d_mlp_ref[:, here] = (mods_ref[0, 5:6, here] * dy).astype(BF16)


def second_norm_kernel(
    blocks, order_ref, present_ref, tokens_ref, att_a, att_b, mods_ref, hidden_ref, second_ref
):
    rows = Rows(blocks, order_ref, tokens_ref.shape[1])

    def body(some):
        att = att_a[some, :].astype(F32) + att_b[some, :].astype(F32)
        hidden = tokens_ref[some, :].astype(F32) + mods_ref[0, 2:3, :] * att
        hidden_ref[some, :] = hidden
        unit, _ = normal(hidden)
        value = unit * (1.0 + mods_ref[0, 4:5, :]) + mods_ref[0, 3:4, :]
        second_ref[some, :] = value.astype(BF16)

    rows.each(tokens_ref.shape[0], body)


def second_back_kernel(
    blocks, order_ref, present_ref, hidden_ref, att_a, att_b, d_a, d_b, dy_ref, mods_ref,
    d_hidden_ref, d_att_ref, sums_ref,
):
    rows = Rows(blocks, order_ref, hidden_ref.shape[1])
    places = rows.places()
    clear_sums(sums_ref)

    def body(some):
        grad = d_a[some, :].astype(F32) + d_b[some, :].astype(F32)
        unit, factor = normal(hidden_ref[some, :])
        add_sums(sums_ref, places, grad, grad * unit)
        d_hidden = normal_back(grad * (1.0 + mods_ref[0, 4:5, :]), unit, factor)
        d_hidden = dy_ref[some, :].astype(F32) + d_hidden
        d_hidden_ref[some, :] = d_hidden
        d_att_ref[some, :] = (mods_ref[0, 2:3, :] * d_hidden).astype(BF16)
        att = att_a[some, :].astype(F32) + att_b[some, :].astype(F32)
        add_sums(sums_ref.at[:, 16:24], places, d_hidden * att)

    rows.each(hidden_ref.shape[0], body)


def first_back_kernel(
    blocks, order_ref, present_ref, tokens_ref, d_a, d_b, d_hidden_ref, mods_ref,
    input_grad_ref, sums_ref,
):
    rows = Rows(blocks, order_ref, tokens_ref.shape[1])
    places = rows.places()
    clear_sums(sums_ref)

    def body(some):
        grad = d_a[some, :].astype(F32) + d_b[some, :].astype(F32)
        unit, factor = normal(tokens_ref[some, :].astype(F32))
        add_sums(sums_ref, places, grad, grad * unit)
        value = normal_back(grad * (1.0 + mods_ref[0, 1:2, :]), unit, factor)
        value = d_hidden_ref[some, :] + value
        for here, there in places:
            input_grad_ref[some, there] = value[:, here]

    rows.each(tokens_ref.shape[0], body)


def block_out_kernel(
    blocks, order_ref, present_ref, hidden_ref, mlp_a, mlp_b, dy_ref, mods_ref,
    block_out_ref, sums_ref,
):
    rows = Rows(blocks, order_ref, hidden_ref.shape[1])
    places = rows.places()
    mask = present_ref[pl.program_id(0)].astype(F32)
    clear_sums(sums_ref)

    def body(some):
        mlp = mlp_a[some, :].astype(F32) + mlp_b[some, :].astype(F32)
        add_sums(sums_ref, places, dy_ref[some, :].astype(F32) * mlp)
        value = mask * (hidden_ref[some, :] + mods_ref[0, 5:6, :] * mlp)
        for here, there in places:
            block_out_ref[some, there] = value[:, here].astype(BF16)

    rows.each(hidden_ref.shape[0], body)


def by_rows(kernel, order, present, operands, mods, kinds, sums=0):
    images, kinds_of_mods, width = mods.shape
    tiles = operands[0].shape[0] // images // TILE
    row = pl.BlockSpec((TILE, width), lambda i, t, *s: (i * tiles + t, 0))
    whole = lambda count: pl.BlockSpec((1, count, width), lambda i, t, *s: (i, 0, 0))
    shapes = [jax.ShapeDtypeStruct(operands[0].shape, kind) for kind in kinds]
    specs = [row] * len(kinds)
    if sums:
        shapes.append(jax.ShapeDtypeStruct((images, 8 * sums, width), F32))
        specs.append(whole(8 * sums))
    blocks = 0 if width // order.shape[0] % 128 else order.shape[0]
    return pl.pallas_call(
        functools.partial(kernel, blocks),
        grid_spec=pltpu.PrefetchScalarGridSpec(
            num_scalar_prefetch=2,
            grid=(images, tiles),
            in_specs=[row] * len(operands) + [whole(kinds_of_mods)],
            out_specs=specs,
        ),
        out_shape=shapes,
        compiler_params=pltpu.CompilerParams(vmem_limit_bytes=40 * 1024 * 1024),
        cost_estimate=pl.CostEstimate(
            flops=operands[0].size * 6000, bytes_accessed=operands[0].size * 8, transcendentals=0
        ),
    )(order, present, *operands, mods)


def matmul(lhs, rhs, turned=False):
    return lax.dot_general(
        lhs, rhs, (((1,), (1 if turned else 0,)), ((), ())), preferred_element_type=F32
    )


def make_body(dp, mp):
    def body(tokens, mod_table, w_qkv, w_out_t, w_up, w_down, bins, present, cotangent):
        count, length, width = tokens.shape
        rows = count * length
        ph = Phases(dp, mp)
        grid = Grid(ph)
        relative, absolute = grid.to_relative(), grid.to_absolute()
        turns = list(range(1, grid.x)) + [0]
        outside = width // relative.shape[0] % 128
        turn_in = lambda value: reorder(value, relative) if outside else value
        turn_out = lambda value: reorder(value, absolute) if outside else value
        flat = lambda value: value.reshape(rows, width)
        join = lambda own, theirs: jnp.concatenate([own, theirs], axis=0)

        def whole(*by_z):
            return jnp.concatenate(
                [by_z[kz][kx] for kx in range(grid.x) for kz in range(grid.z)], axis=0
            )

        def summed(value, weight, between=None):
            part = matmul(ph.begin(value[rows:]), weight, True).astype(BF16)
            ph.end(part)
            theirs = ph.send_core(part)
            if between is not None:
                between()
            part = matmul(ph.begin(value[:rows]), weight, True) + theirs.astype(F32)
            part = part.astype(BF16)
            ph.end(part)
            return ph.across(part)

        def from_both(theirs, value, weight, between=None):
            if between is not None:
                between()
            part = matmul(ph.begin(value[:rows]), weight, True) + theirs.astype(F32)
            part = part.astype(BF16)
            ph.end(part)
            return ph.across(part)

        def two(parts):
            return parts if len(parts) == 2 else [plus(*parts), jnp.zeros_like(parts[0])]

        def dots(lhs, rhs):
            kept = {}
            for kx in turns:
                kept[kx] = grid.dots(ph.begin(lhs), rhs, kx)
                ph.end(kept[kx])
            return kept

        def rows_of(kept, low, high):
            blk = width // grid.x // grid.z
            return {kx: kept[kx][low * blk : high * blk] for kx in kept}

        wide = w_qkv.reshape(3, -1, CORES, w_qkv.shape[2] // CORES).transpose(1, 2, 0, 3)
        s_q = grid.chip_shard(wide.reshape(w_qkv.shape[1], -1))
        z_q, x_q = {1: ph.send_z(s_q, 1)}, {0: ph.gather_x(s_q)}
        s_o = grid.chip_shard(ph.begin(w_out_t))
        ph.end(s_o)
        x_o = jnp.stack(ph.gather_x(s_o))
        table_rows = jnp.arange(mod_table.shape[0])[None, :]
        onehot = (bins[:, None] == table_rows).astype(F32)
        mods = jnp.einsum("cb,btd->ctd", ph.begin(onehot), mod_table, precision=HIGH)
        mods = reorder(mods, relative)
        ph.end(mods)
        ph.close()

        z_q[3] = ph.send_z(s_q, 3)
        x_q[1] = ph.gather_x(z_q[1])
        tokens, normed_own = by_rows(
            first_norm_kernel, relative, present, [flat(turn_in(ph.begin(tokens)))], mods, [BF16, BF16]
        )
        ph.end(normed_own)
        normed_other = ph.hand_over(normed_own)
        ph.close()

        z_q[2] = ph.send_z(z_q[1], 1)
        x_q[3] = ph.gather_x(z_q[3])
        s_u = grid.chip_shard(ph.begin(w_up))
        ph.end(s_u)
        normed = join(normed_own, ph.begin(normed_other))
        ph.end(normed)
        ph.close()

        z_o = {0: x_o, 1: ph.send_z(x_o, 1)}
        x_q[2] = ph.gather_x(z_q[2])
        s_d = grid.chip_shard(ph.begin(w_down))
        ph.end(s_d)
        ph.close()

        z_o[3] = ph.send_z(x_o, 3)
        z_o[2] = ph.send_z(z_o[1], 1)
        x_u = {0: ph.gather_x(s_u)}
        w_a = whole(x_q[0], x_q[1], x_q[2], x_q[3])
        local_width = s_o.shape[1]
        local_heads = local_width // HEAD_DIM
        qkv = matmul(ph.begin(normed), w_a).astype(BF16)
        ph.end(qkv)
        attend = functools.partial(attend_kernel, local_heads)
        mixed = by_image(attend, length, local_width, ph.begin(qkv))
        ph.end(mixed)
        ph.close()

        z_u = {1: ph.send_z(s_u, 1)}
        x_d = {0: ph.gather_x(s_d)}
        w_o = jnp.concatenate([z_o[kz][kx] for kx in range(grid.x) for kz in range(grid.z)], axis=0)
        from_cotangent = []

        def take_cotangent():
            from_cotangent.extend(
                by_rows(
                    cotangent_kernel, relative, present, [flat(turn_in(ph.begin(cotangent)))], mods,
                    [BF16, BF16],
                )
            )
            ph.end(from_cotangent[1])

        att = summed(mixed, w_o, take_cotangent)
        dy, d_mlp_own = from_cotangent
        ph.close()

        z_u[3] = ph.send_z(s_u, 3)
        x_u[1] = ph.gather_x(z_u[1])
        d_mlp_other = ph.hand_over(ph.now(d_mlp_own))
        ph.close()

        z_u[2] = ph.send_z(z_u[1], 1)
        x_u[3] = ph.gather_x(z_u[3])
        att[-1] = ph.begin(att[-1])
        hidden, second_own = by_rows(
            second_norm_kernel, relative, present, [tokens, *two(att)], mods, [F32, BF16]
        )
        ph.end(second_own)
        second_other = ph.hand_over(second_own)
        ph.close()

        z_d = {1: ph.send_z(s_d, 1)}
        x_u[2] = ph.gather_x(z_u[2])
        second = join(second_own, ph.begin(second_other))
        ph.end(second)
        d_mlp = join(d_mlp_own, ph.begin(d_mlp_other))
        ph.end(d_mlp)
        ph.close()

        z_d[3] = ph.send_z(s_d, 3)
        x_d[1] = ph.gather_x(z_d[1])
        w_u = whole(x_u[0], x_u[1], x_u[2], x_u[3])
        up_val = matmul(ph.begin(second), w_u)
        act = jax.nn.gelu(up_val).astype(BF16)
        ph.end(act)
        ph.close()

        z_d[2] = ph.send_z(z_d[1], 1)
        x_d[3] = ph.gather_x(z_d[3])
        down = dots(d_mlp, act)
        half = down[0].shape[1] // 2
        first = jnp.stack([down[kx][:, :half] for kx in range(grid.x)])
        other = {kx: down[kx][:, half:] for kx in down}
        ph.end(first)
        ph.close()

        blk = first.shape[1] // grid.z
        part = lambda stacked, kz: stacked[:, kz * blk : (kz + 1) * blk]
        x_d[2] = ph.gather_x(z_d[2])
        a_2 = ph.send_z(part(first, 2), 3)
        up_val = ph.begin(up_val)
        _, gelu_pull = jax.vjp(jax.nn.gelu, up_val)
        slope = gelu_pull(jnp.ones_like(up_val))[0]
        ph.end(slope)
        ph.close()

        x_b = {2: ph.reduce_x(rows_of(other, 2, 4))}
        a_3 = ph.send_z(part(first, 3), 1)
        w_d = whole(x_d[0], x_d[1], x_d[2], x_d[3])
        d_up = (matmul(ph.begin(d_mlp), w_d) * slope).astype(BF16)
        ph.end(d_up)
        up = {}
        d_second_part = matmul(ph.begin(d_up)[rows:], w_u, True).astype(BF16)
        ph.end(d_second_part)
        d_second_part = ph.hand_over(d_second_part)
        ph.close()

        def up_dots(blocks):
            for kx in blocks:
                up[kx] = grid.dots(ph.begin(second), d_up, kx)
                ph.end(up[kx])

        x_b[0] = ph.reduce_x(rows_of(other, 0, 2))
        a_1 = ph.send_z(plus(part(first, 1), ph.now(a_2)).astype(BF16), 3)
        d_second = from_both(d_second_part, d_up, w_u)
        up_dots(turns[:-1])
        ph.close()

        up_rows = lambda kz: ph.reduce_x(rows_of(up, kz, kz + 1))
        x_up = {2: up_rows(2)}
        b_part = lambda kz: ph.now(x_b[kz // 2 * 2][(kz % 2) * blk : (kz % 2 + 1) * blk])
        b_sum = lambda kz: plus(rows_of(other, kz, kz + 1)[0], b_part(kz))
        b_2 = ph.send_z(b_sum(2).astype(BF16), 3)
        b_3 = ph.send_z(b_sum(3).astype(BF16), 1)
        up_dots(turns[-1:])
        mlp_part = matmul(ph.begin(act)[rows:], w_d, True).astype(BF16)
        ph.end(mlp_part)
        mlp_part = ph.hand_over(mlp_part)
        ph.close()

        x_up[3] = up_rows(3)
        up_sum = lambda kz: plus(rows_of(up, kz, kz + 1)[0], ph.now(x_up[kz]))
        u_2 = ph.send_z(up_sum(2).astype(BF16), 3)
        mlp = from_both(mlp_part, act, w_d)
        d_second[-1] = ph.begin(d_second[-1])
        d_hidden, d_att_own, sums2 = by_rows(
            second_back_kernel, relative, present, [hidden, *two(att), *two(d_second), dy], mods,
            [F32, BF16], 3,
        )
        ph.end(d_att_own)
        d_att_other = ph.hand_over(d_att_own)
        ph.close()

        x_up[1] = up_rows(1)
        first_sum = plus(part(first, 0), a_3, ph.now(a_1))
        x_first = ph.reduce_x(first_sum.astype(BF16))
        u_3 = ph.send_z(up_sum(3).astype(BF16), 1)
        b_1 = ph.send_z((b_sum(1) + ph.now(b_2).astype(F32)).astype(BF16), 3)
        d_att = join(d_att_own, ph.begin(d_att_other))
        d_mixed = matmul(d_att, w_o).astype(BF16)
        ph.end(d_mixed)
        attend_back = functools.partial(attend_back_kernel, local_heads)
        d_qkv = by_image(attend_back, length, 3 * local_width, qkv, ph.begin(d_mixed))
        ph.end(d_qkv)
        d_normed_part = matmul(ph.begin(d_qkv)[rows:], w_a, True).astype(BF16)
        ph.end(d_normed_part)
        d_normed_part = ph.hand_over(d_normed_part)
        ph.close()

        x_up[0] = up_rows(0)
        u_1 = ph.send_z((up_sum(1) + ph.now(u_2).astype(F32)).astype(BF16), 3)
        d_normed = from_both(d_normed_part, d_qkv, w_a)
        mlp[-1] = ph.begin(mlp[-1])
        ph.end(mlp[-1])
        out = dots(d_att, mixed)
        proj = dots(normed, d_qkv)
        ph.close()

        x_out = ph.reduce_x(out)
        mlp[-1] = ph.begin(mlp[-1])
        block_out, sums3 = by_rows(
            block_out_kernel, relative, present, [hidden, *two(mlp), dy], mods, [BF16], 1
        )
        ph.end(block_out)
        up_total = up_sum(0) + ph.now(u_3).astype(F32) + ph.now(u_1).astype(F32)
        up_mine, up_theirs = grid.halves(ph.begin(up_total), 0)
        ph.end(up_mine)
        up_theirs = ph.hand_over(up_theirs)
        ph.close()

        p_rows = lambda kz: ph.reduce_x(rows_of(proj, kz, kz + 1))
        p_sum = lambda kz: plus(rows_of(proj, kz, kz + 1)[0], ph.now(x_p[kz]))
        out_sum = lambda kz: plus(
            rows_of(out, kz, kz + 1)[0], ph.now(x_out[kz * blk : (kz + 1) * blk])
        )
        x_p = {2: p_rows(2)}
        o_2 = ph.send_z(out_sum(2).astype(BF16), 3)
        o_3 = ph.send_z(out_sum(3).astype(BF16), 1)
        d_normed[-1] = ph.begin(d_normed[-1])
        input_grad, sums1 = by_rows(
            first_back_kernel, relative, present, [tokens, *two(d_normed), d_hidden], mods, [F32], 2
        )
        ph.end(input_grad)
        ph.close(20.0)

        x_p[3] = p_rows(3)
        p_2 = ph.send_z(p_sum(2).astype(BF16), 3)
        o_1 = ph.send_z((out_sum(1) + ph.now(o_2).astype(F32)).astype(BF16), 3)
        row_sums = [jnp.sum(v.reshape(count, -1, 8, width), axis=2) for v in (sums1, sums2, sums3)]
        bin_row = jnp.broadcast_to(bins.astype(F32)[:, None, None], (count, 1, width))
        d_mods = ph.begin(turn_out(jnp.concatenate(row_sums, axis=1)))
        d_mods = jnp.concatenate([d_mods, bin_row], axis=1)
        ph.end(d_mods)
        down_low = plus(ph.now(first_sum)[0], x_first)
        down_high = b_sum(0) + ph.now(b_3).astype(F32) + ph.now(b_1).astype(F32)
        down_total = ph.begin(jnp.concatenate([down_low, down_high], axis=1))
        down_mine, down_theirs = grid.halves(down_total, 0)
        ph.end(down_mine, d_mods)
        down_theirs = ph.hand_over(down_theirs)
        ph.close(20.0)

        x_p[1] = p_rows(1)
        p_3 = ph.send_z(p_sum(3).astype(BF16), 1)
        d_mods = lax.all_to_all(ph.now(d_mods), "dp", split_axis=2, concat_axis=0, tiled=True)
        ph.results.append(d_mods)
        up_part = grid.by_core(ph.begin(up_mine), up_theirs, 1)
        ph.end(up_part)
        ph.close(20.0)

        x_p[0] = p_rows(0)
        p_1 = ph.send_z((p_sum(1) + ph.now(p_2).astype(F32)).astype(BF16), 3)
        d_mods = ph.begin(d_mods)
        rows_in_order = jnp.stack([d_mods[:, k] for k in (0, 1, 4, 2, 3, 5)], axis=1)
        onehot_all = (d_mods[:, 6, :1] == table_rows.astype(F32)).astype(F32)
        table_part = jnp.einsum("sb,std->btd", onehot_all, rows_in_order, precision=HIGH)
        ph.end(table_part)
        down_part = grid.by_core(ph.begin(down_mine), down_theirs, 1)
        ph.end(down_part)
        out_total = out_sum(0) + ph.now(o_3).astype(F32) + ph.now(o_1).astype(F32)
        out_mine, out_theirs = grid.halves(ph.begin(out_total), 0)
        ph.end(out_mine)
        out_theirs = ph.hand_over(out_theirs)
        ph.close(20.0)

        out_part = grid.by_core(out_mine, ph.begin(out_theirs), 1)
        qkv_part = p_sum(0) + ph.now(p_3).astype(F32) + ph.now(p_1).astype(F32)
        qkv_part = qkv_part.reshape(-1, 3, local_width).transpose(1, 0, 2)
        qkv_part = grid.own_rows(qkv_part)
        block_out, input_grad = (
            turn_out(value).reshape(count, length, width) for value in (block_out, input_grad)
        )
        return (block_out, input_grad, table_part, qkv_part, out_part, up_part, down_part)

    return body


def solution(mesh):
    in_specs = (
        P("dp", None, None),
        P(),
        P(None, "dp", "mp"),
        P("dp", "mp"),
        P("dp", "mp"),
        P("dp", "mp"),
        P("dp"),
        P("dp"),
        P("dp", None, None),
    )
    out_specs = (
        P("dp", None, None),
        P("dp", None, None),
        P(None, None, "dp"),
        P(None, "dp", "mp"),
        P("dp", "mp"),
        P("dp", "mp"),
        P("dp", "mp"),
    )
    body = make_body(mesh.shape["dp"], mesh.shape["mp"])
    return jax.shard_map(body, mesh=mesh, in_specs=in_specs, out_specs=out_specs, check_vma=False)
```

```python
import functools

import jax
import jax.numpy as jnp
from jax import lax
from jax.experimental import pallas as pl
from jax.experimental.pallas import tpu as pltpu
from jax.sharding import PartitionSpec as P

HEAD_DIM = 128
EPS = 1e-06
HIGH = lax.Precision.HIGHEST
F32 = jnp.float32
BF16 = jnp.bfloat16
CORES = 2
TILE = 128
CHUNK = 16


def after(value, *earlier):
    return lax.optimization_barrier((value, *earlier))[0]


def pass_on(in_ref, out_ref):
    out_ref[...] = in_ref[...]


def pace(token, cost):
    return pl.pallas_call(
        pass_on,
        out_shape=jax.ShapeDtypeStruct(token.shape, token.dtype),
        cost_estimate=pl.CostEstimate(
            flops=int(cost * 1.15e9), bytes_accessed=8192, transcendentals=0
        ),
    )(token)


class Phases:
    def __init__(self, dp, mp):
        self.z = 4 if (dp // CORES) % 4 == 0 else 1
        self.x = dp // CORES // self.z
        self.tail, self.results, self.sent, self.last = (), [], [], ()
        self.turn = [(i, (i + 1) % mp) for i in range(mp)]
        self.token = jnp.zeros((8, 128), F32)

    def ring(self, dz, dx, dc):
        index = lambda z, x, c: (z % self.z * self.x + x % self.x) * CORES + c % CORES
        return [
            (index(z, x, c), index(z + dz, x + dx, c + dc))
            for z in range(self.z)
            for x in range(self.x)
            for c in range(CORES)
        ]

    def send(self, value, dz, dx, hold=True):
        value = after(value, *self.tail)
        self.sent.append(value)
        out = lax.ppermute(value, "dp", self.ring(dz, dx, 0))
        if hold:
            self.results.append(out)
        return out

    def send_z(self, value, places):
        return self.send(value, places, 0)

    def send_x(self, value):
        return self.send(value, 0, 1)

    def send_core(self, value):
        return lax.ppermute(value, "dp", self.ring(0, 0, 1))

    def hand_over(self, value):
        out = self.send_core(value)
        self.results.append(out)
        return out

    def across(self, part):
        out = [lax.optimization_barrier(part)]
        for _ in range(len(self.turn) - 1):
            out.append(lax.ppermute(out[-1], "mp", self.turn))
        return out

    def now(self, value):
        return after(value, *self.tail)

    def begin(self, value):
        return after(value, *self.tail, *self.sent, *self.last)

    def end(self, *values):
        self.last = values

    def close(self, cost=25.0):
        self.token = pace(after(self.token, *self.tail, *self.sent), cost)
        self.tail = (*self.results, *self.last, self.token)
        self.results, self.sent, self.last = [], [], ()

    def gather_x(self, piece):
        pieces = [piece]
        for _ in range(1, self.x):
            pieces.append(self.send_x(pieces[-1]))
        return pieces

    def reduce_x(self, blocks):
        moving = None
        for kx in range(1, self.x):
            value = blocks[kx]
            if moving is not None:
                value = value.astype(F32) + moving.astype(F32)
            moving = self.send_x(value.astype(BF16))
        return moving


def plus(first, *others):
    total = first.astype(F32)
    for other in others:
        if other is not None:
            total = total + other.astype(F32)
    return total


class Grid:
    def __init__(self, phases):
        self.z, self.x, self.phases = phases.z, phases.x, phases
        me = lax.axis_index("dp")
        self.at_z, self.at_x, self.core = (
            me // (self.x * CORES),
            (me // CORES) % self.x,
            me % CORES,
        )

    def to_relative(self):
        return jnp.stack(
            [
                (self.at_z - kz) % self.z * self.x + (self.at_x - kx) % self.x
                for kx in range(self.x)
                for kz in range(self.z)
            ]
        ).astype(jnp.int32)

    def to_absolute(self):
        return jnp.stack(
            [
                (self.at_x - ox) % self.x * self.z + (self.at_z - oz) % self.z
                for oz in range(self.z)
                for ox in range(self.x)
            ]
        ).astype(jnp.int32)

    def by_core(self, first, second, axis):
        return jnp.where(
            self.core == 0,
            jnp.concatenate([first, second], axis=axis),
            jnp.concatenate([second, first], axis=axis),
        )

    def halves(self, value, axis):
        half = value.shape[axis] // 2
        low = lax.slice_in_dim(value, 0, half, axis=axis)
        high = lax.slice_in_dim(value, half, 2 * half, axis=axis)
        return (
            jnp.where(self.core == 0, low, high),
            jnp.where(self.core == 0, high, low),
        )

    def chip_shard(self, shard):
        mine, theirs = self.halves(shard, 1)
        return self.by_core(mine, self.phases.send_core(theirs), 0)

    def own_rows(self, total):
        mine, theirs = self.halves(total, total.ndim - 2)
        return self.by_core(mine, self.phases.send_core(theirs), total.ndim - 1)

    def dots(self, lhs, rhs, kx):
        width = lhs.shape[1] // self.x
        return lax.dot_general(
            lhs[:, kx * width : (kx + 1) * width],
            rhs,
            (((0,), (0,)), ((), ())),
            preferred_element_type=F32,
        ).astype(BF16)


def copy_block(order_ref, in_ref, out_ref):
    out_ref[...] = in_ref[...]


def reorder(value, order):
    count = order.shape[0]
    shape = value.shape
    flat = value.reshape(-1, shape[-1])
    blk = shape[-1] // count
    if blk % 128:
        return jnp.take(flat.reshape(-1, count, blk), order, axis=1).reshape(shape)
    out = pl.pallas_call(
        copy_block,
        grid_spec=pltpu.PrefetchScalarGridSpec(
            num_scalar_prefetch=1,
            grid=(count,),
            in_specs=[pl.BlockSpec((flat.shape[0], blk), lambda j, s: (0, s[j]))],
            out_specs=pl.BlockSpec((flat.shape[0], blk), lambda j, s: (0, j)),
        ),
        out_shape=jax.ShapeDtypeStruct(flat.shape, flat.dtype),
    )(order, flat)
    return out.reshape(shape)


def dot(lhs, rhs, left, right):
    return lax.dot_general(lhs, rhs, (((left,), (right,)), ((), ())), preferred_element_type=F32)


def softmax(query, keys):
    scores = dot(query, keys, 1, 1) * HEAD_DIM ** (-0.5)
    expo = jnp.exp(scores - jnp.max(scores, axis=-1, keepdims=True))
    return expo / jnp.sum(expo, axis=-1, keepdims=True)


def head_cols(part, head, heads):
    return pl.ds((part * heads + head) * HEAD_DIM, HEAD_DIM)


def attend_kernel(heads, qkv_ref, mixed_ref):
    for head in range(heads):
        query, keys, values = (qkv_ref[:, head_cols(part, head, heads)] for part in range(3))
        probs = softmax(query, keys).astype(BF16)
        mixed = dot(probs, values, 1, 0).astype(BF16)
        mixed_ref[:, head_cols(0, head, heads)] = mixed


def attend_back_kernel(heads, qkv_ref, d_mixed_ref, d_qkv_ref):
    factor = HEAD_DIM ** (-0.5)
    for head in range(heads):
        query, keys, values = (qkv_ref[:, head_cols(part, head, heads)] for part in range(3))
        d_mixed = d_mixed_ref[:, head_cols(0, head, heads)]
        probs = softmax(query, keys)
        d_probs = dot(d_mixed, values, 1, 1)
        d_values = dot(probs.astype(BF16), d_mixed, 0, 0)
        delta = jnp.sum(d_probs * probs, axis=-1, keepdims=True)
        d_scores = (probs * (d_probs - delta)).astype(BF16)
        d_query = dot(d_scores, keys, 1, 0) * factor
        d_keys = dot(d_scores, query, 0, 0) * factor
        d_qkv_ref[:, head_cols(0, head, heads)] = d_query.astype(BF16)
        d_qkv_ref[:, head_cols(1, head, heads)] = d_keys.astype(BF16)
        d_qkv_ref[:, head_cols(2, head, heads)] = d_values.astype(BF16)


def by_image(kernel, length, width, *operands):
    rows = operands[0].shape[0]
    block = lambda cols: pl.BlockSpec((length, cols), lambda image: (image, 0))
    return pl.pallas_call(
        kernel,
        grid=(rows // length,),
        in_specs=[block(operand.shape[1]) for operand in operands],
        out_specs=block(width),
        out_shape=jax.ShapeDtypeStruct((rows, width), BF16),
        compiler_params=pltpu.CompilerParams(vmem_limit_bytes=32 * 1024 * 1024),
        cost_estimate=pl.CostEstimate(
            flops=rows * length * width * 8, bytes_accessed=rows * 8192, transcendentals=rows * 1024
        ),
    )(*operands)


def normal(value):
    centre = value - jnp.mean(value, axis=-1, keepdims=True)
    factor = lax.rsqrt(jnp.mean(centre * centre, axis=-1, keepdims=True) + EPS)
    return centre * factor, factor


def normal_back(grad, unit, factor):
    mean = jnp.mean(grad, axis=-1, keepdims=True)
    along = jnp.mean(grad * unit, axis=-1, keepdims=True)
    return factor * (grad - mean - unit * along)


class Rows:
    def __init__(self, blocks, order_ref, width):
        self.blocks, self.order, self.width = blocks, order_ref, width

    def each(self, count, body):
        def step(index, carry):
            body(pl.ds(pl.multiple_of(index * CHUNK, CHUNK), CHUNK))
            return carry

        lax.fori_loop(0, count // CHUNK, step, 0)

    def places(self):
        if not self.blocks:
            return [(slice(0, self.width), slice(0, self.width))]
        blk = self.width // self.blocks
        return [
            (
                slice(k * blk, (k + 1) * blk),
                pl.ds(pl.multiple_of(self.order[k] * blk, blk), blk),
            )
            for k in range(self.blocks)
        ]


def clear_sums(sums_ref):
    @pl.when(pl.program_id(1) == 0)
    def _():
        sums_ref[...] = jnp.zeros_like(sums_ref)


def add_sums(sums_ref, places, *terms):
    for index, term in enumerate(terms):
        low, high = term[:8], term[8:]
        for here, there in places:
            sums_ref[0, index * 8 : index * 8 + 8, there] += low[:, here] + high[:, here]


def first_norm_kernel(blocks, order_ref, present_ref, tokens_ref, mods_ref, kept_ref, normed_ref):
    rows = Rows(blocks, order_ref, tokens_ref.shape[1])
    for here, there in rows.places():
        kept_ref[:, here] = tokens_ref[:, there]

    def body(some):
        unit, _ = normal(kept_ref[some, :].astype(F32))
        value = unit * (1.0 + mods_ref[0, 1:2, :]) + mods_ref[0, 0:1, :]
        normed_ref[some, :] = value.astype(BF16)

    rows.each(tokens_ref.shape[0], body)


def cotangent_kernel(blocks, order_ref, present_ref, cotangent_ref, mods_ref, dy_ref, d_mlp_ref):
    rows = Rows(blocks, order_ref, cotangent_ref.shape[1])
    mask = present_ref[pl.program_id(0)].astype(F32)
    for here, there in rows.places():
        dy = cotangent_ref[:, there].astype(F32) * mask
        dy_ref[:, here] = dy.astype(BF16)
        d_mlp_ref[:, here] = (mods_ref[0, 5:6, here] * dy).astype(BF16)


def second_norm_kernel(
    blocks, order_ref, present_ref, tokens_ref, att_a, att_b, mods_ref, hidden_ref, second_ref
):
    rows = Rows(blocks, order_ref, tokens_ref.shape[1])

    def body(some):
        att = att_a[some, :].astype(F32) + att_b[some, :].astype(F32)
        hidden = tokens_ref[some, :].astype(F32) + mods_ref[0, 2:3, :] * att
        hidden_ref[some, :] = hidden
        unit, _ = normal(hidden)
        value = unit * (1.0 + mods_ref[0, 4:5, :]) + mods_ref[0, 3:4, :]
        second_ref[some, :] = value.astype(BF16)

    rows.each(tokens_ref.shape[0], body)


def second_back_kernel(
    blocks, order_ref, present_ref, hidden_ref, att_a, att_b, d_a, d_b, dy_ref, mods_ref,
    d_hidden_ref, d_att_ref, sums_ref,
):
    rows = Rows(blocks, order_ref, hidden_ref.shape[1])
    places = rows.places()
    clear_sums(sums_ref)

    def body(some):
        grad = d_a[some, :].astype(F32) + d_b[some, :].astype(F32)
        unit, factor = normal(hidden_ref[some, :])
        add_sums(sums_ref, places, grad, grad * unit)
        d_hidden = normal_back(grad * (1.0 + mods_ref[0, 4:5, :]), unit, factor)
        d_hidden = dy_ref[some, :].astype(F32) + d_hidden
        d_hidden_ref[some, :] = d_hidden
        d_att_ref[some, :] = (mods_ref[0, 2:3, :] * d_hidden).astype(BF16)
        att = att_a[some, :].astype(F32) + att_b[some, :].astype(F32)
        add_sums(sums_ref.at[:, 16:24], places, d_hidden * att)

    rows.each(hidden_ref.shape[0], body)


def first_back_kernel(
    blocks, order_ref, present_ref, tokens_ref, d_a, d_b, d_hidden_ref, mods_ref,
    input_grad_ref, sums_ref,
):
    rows = Rows(blocks, order_ref, tokens_ref.shape[1])
    places = rows.places()
    clear_sums(sums_ref)

    def body(some):
        grad = d_a[some, :].astype(F32) + d_b[some, :].astype(F32)
        unit, factor = normal(tokens_ref[some, :].astype(F32))
        add_sums(sums_ref, places, grad, grad * unit)
        value = normal_back(grad * (1.0 + mods_ref[0, 1:2, :]), unit, factor)
        value = d_hidden_ref[some, :] + value
        for here, there in places:
            input_grad_ref[some, there] = value[:, here]

    rows.each(tokens_ref.shape[0], body)


def block_out_kernel(
    blocks, order_ref, present_ref, hidden_ref, mlp_a, mlp_b, dy_ref, mods_ref,
    block_out_ref, sums_ref,
):
    rows = Rows(blocks, order_ref, hidden_ref.shape[1])
    places = rows.places()
    mask = present_ref[pl.program_id(0)].astype(F32)
    clear_sums(sums_ref)

    def body(some):
        mlp = mlp_a[some, :].astype(F32) + mlp_b[some, :].astype(F32)
        add_sums(sums_ref, places, dy_ref[some, :].astype(F32) * mlp)
        value = mask * (hidden_ref[some, :] + mods_ref[0, 5:6, :] * mlp)
        for here, there in places:
            block_out_ref[some, there] = value[:, here].astype(BF16)

    rows.each(hidden_ref.shape[0], body)


def by_rows(kernel, order, present, operands, mods, kinds, sums=0):
    images, kinds_of_mods, width = mods.shape
    tiles = operands[0].shape[0] // images // TILE
    row = pl.BlockSpec((TILE, width), lambda i, t, *s: (i * tiles + t, 0))
    whole = lambda count: pl.BlockSpec((1, count, width), lambda i, t, *s: (i, 0, 0))
    shapes = [jax.ShapeDtypeStruct(operands[0].shape, kind) for kind in kinds]
    specs = [row] * len(kinds)
    if sums:
        shapes.append(jax.ShapeDtypeStruct((images, 8 * sums, width), F32))
        specs.append(whole(8 * sums))
    blocks = 0 if width // order.shape[0] % 128 else order.shape[0]
    return pl.pallas_call(
        functools.partial(kernel, blocks),
        grid_spec=pltpu.PrefetchScalarGridSpec(
            num_scalar_prefetch=2,
            grid=(images, tiles),
            in_specs=[row] * len(operands) + [whole(kinds_of_mods)],
            out_specs=specs,
        ),
        out_shape=shapes,
        compiler_params=pltpu.CompilerParams(vmem_limit_bytes=40 * 1024 * 1024),
        cost_estimate=pl.CostEstimate(
            flops=operands[0].size * 6000, bytes_accessed=operands[0].size * 8, transcendentals=0
        ),
    )(order, present, *operands, mods)


def matmul(lhs, rhs, turned=False):
    return lax.dot_general(
        lhs, rhs, (((1,), (1 if turned else 0,)), ((), ())), preferred_element_type=F32
    )


def make_body(dp, mp):
    def body(tokens, mod_table, w_qkv, w_out_t, w_up, w_down, bins, present, cotangent):
        count, length, width = tokens.shape
        rows = count * length
        ph = Phases(dp, mp)
        grid = Grid(ph)
        relative, absolute = grid.to_relative(), grid.to_absolute()
        turns = list(range(1, grid.x)) + [0]
        outside = width // relative.shape[0] % 128
        turn_in = lambda value: reorder(value, relative) if outside else value
        turn_out = lambda value: reorder(value, absolute) if outside else value
        flat = lambda value: value.reshape(rows, width)
        join = lambda own, theirs: jnp.concatenate([own, theirs], axis=0)

        def whole(*by_z):
            return jnp.concatenate(
                [by_z[kz][kx] for kx in range(grid.x) for kz in range(grid.z)], axis=0
            )

        def from_both(theirs, value, weight, between=None):
            if between is not None:
                between()
            part = matmul(ph.begin(value[:rows]), weight, True) + theirs.astype(F32)
            part = part.astype(BF16)
            ph.end(part)
            return ph.across(part)

        def two(parts):
            return parts if len(parts) == 2 else [plus(*parts), jnp.zeros_like(parts[0])]

        def dots(lhs, rhs):
            kept = {}
            for kx in turns:
                kept[kx] = grid.dots(ph.begin(lhs), rhs, kx)
                ph.end(kept[kx])
            return kept

        def rows_of(kept, low, high):
            blk = width // grid.x // grid.z
            return {kx: kept[kx][low * blk : high * blk] for kx in kept}

        wide = w_qkv.reshape(3, -1, CORES, w_qkv.shape[2] // CORES).transpose(1, 2, 0, 3)
        s_q = grid.chip_shard(wide.reshape(w_qkv.shape[1], -1))
        z_q, x_q = {1: ph.send_z(s_q, 1)}, {0: ph.gather_x(s_q)}
        s_o = grid.chip_shard(ph.begin(w_out_t))
        ph.end(s_o)
        x_o = jnp.stack(ph.gather_x(s_o))
        table_rows = jnp.arange(mod_table.shape[0])[None, :]
        onehot = (bins[:, None] == table_rows).astype(F32)
        mods = jnp.einsum("cb,btd->ctd", ph.begin(onehot), mod_table, precision=HIGH)
        mods = reorder(mods, relative)
        ph.end(mods)
        ph.close()

        z_q[3] = ph.send_z(s_q, 3)
        x_q[1] = ph.gather_x(z_q[1])
        tokens, normed_own = by_rows(
            first_norm_kernel, relative, present, [flat(turn_in(ph.begin(tokens)))], mods, [BF16, BF16]
        )
        ph.end(normed_own)
        normed_other = ph.hand_over(normed_own)
        ph.close()

        z_q[2] = ph.send_z(z_q[1], 1)
        x_q[3] = ph.gather_x(z_q[3])
        s_u = grid.chip_shard(ph.begin(w_up))
        ph.end(s_u)
        normed = join(normed_own, ph.begin(normed_other))
        ph.end(normed)
        ph.close()

        z_o = {0: x_o, 1: ph.send_z(x_o, 1)}
        x_q[2] = ph.gather_x(z_q[2])
        s_d = grid.chip_shard(ph.begin(w_down))
        ph.end(s_d)
        ph.close()

        z_o[3] = ph.send_z(x_o, 3)
        z_o[2] = ph.send_z(z_o[1], 1)
        x_u = {0: ph.gather_x(s_u)}
        w_a = whole(x_q[0], x_q[1], x_q[2], x_q[3])
        local_width = s_o.shape[1]
        local_heads = local_width // HEAD_DIM
        qkv = matmul(ph.begin(normed), w_a).astype(BF16)
        ph.end(qkv)
        attend = functools.partial(attend_kernel, local_heads)
        mixed = by_image(attend, length, local_width, ph.begin(qkv))
        ph.end(mixed)
        w_o = jnp.concatenate([z_o[kz][kx] for kx in range(grid.x) for kz in range(grid.z)], axis=0)
        att_part = matmul(ph.begin(mixed)[rows:], w_o, True).astype(BF16)
        ph.end(att_part)
        att_part = ph.hand_over(att_part)
        ph.close()

        z_u = {1: ph.send_z(s_u, 1)}
        x_d = {0: ph.gather_x(s_d)}
        att = from_both(att_part, mixed, w_o)
        dy, d_mlp_own = by_rows(
            cotangent_kernel, relative, present, [flat(turn_in(ph.begin(cotangent)))], mods, [BF16, BF16]
        )
        ph.end(d_mlp_own)
        ph.close()

        z_u[3] = ph.send_z(s_u, 3)
        x_u[1] = ph.gather_x(z_u[1])
        d_mlp_other = ph.hand_over(ph.now(d_mlp_own))
        ph.close()

        z_u[2] = ph.send_z(z_u[1], 1)
        x_u[3] = ph.gather_x(z_u[3])
        att[-1] = ph.begin(att[-1])
        hidden, second_own = by_rows(
            second_norm_kernel, relative, present, [tokens, *two(att)], mods, [F32, BF16]
        )
        ph.end(second_own)
        second_other = ph.hand_over(second_own)
        ph.close()

        z_d = {1: ph.send_z(s_d, 1)}
        x_u[2] = ph.gather_x(z_u[2])
        second = join(second_own, ph.begin(second_other))
        ph.end(second)
        d_mlp = join(d_mlp_own, ph.begin(d_mlp_other))
        ph.end(d_mlp)
        ph.close()

        z_d[3] = ph.send_z(s_d, 3)
        x_d[1] = ph.gather_x(z_d[1])
        w_u = whole(x_u[0], x_u[1], x_u[2], x_u[3])
        up_val = matmul(ph.begin(second), w_u)
        act = jax.nn.gelu(up_val).astype(BF16)
        ph.end(act)
        ph.close()

        z_d[2] = ph.send_z(z_d[1], 1)
        x_d[3] = ph.gather_x(z_d[3])
        down = dots(d_mlp, act)
        half = down[0].shape[1] // 2
        first = jnp.stack([down[kx][:, :half] for kx in range(grid.x)])
        other = {kx: down[kx][:, half:] for kx in down}
        ph.end(first)
        ph.close()

        blk = first.shape[1] // grid.z
        part = lambda stacked, kz: stacked[:, kz * blk : (kz + 1) * blk]
        x_d[2] = ph.gather_x(z_d[2])
        a_2 = ph.send_z(part(first, 2), 3)
        up_val = ph.begin(up_val)
        _, gelu_pull = jax.vjp(jax.nn.gelu, up_val)
        slope = gelu_pull(jnp.ones_like(up_val))[0]
        ph.end(slope)
        ph.close()

        x_b = {2: ph.reduce_x(rows_of(other, 2, 4))}
        a_3 = ph.send_z(part(first, 3), 1)
        w_d = whole(x_d[0], x_d[1], x_d[2], x_d[3])
        d_up = (matmul(ph.begin(d_mlp), w_d) * slope).astype(BF16)
        ph.end(d_up)
        d_second_part = matmul(ph.begin(d_up)[rows:], w_u, True).astype(BF16)
        ph.end(d_second_part)
        d_second_part = ph.hand_over(d_second_part)
        a_1 = ph.begin(plus(part(first, 1), ph.now(a_2)).astype(BF16))
        ph.end(a_1)
        ph.close()

        x_b[0] = ph.reduce_x(rows_of(other, 0, 2))
        a_1 = ph.send_z(a_1, 3)
        d_second = from_both(d_second_part, d_up, w_u)
        up = {}

        def up_dots(blocks):
            for kx in blocks:
                up[kx] = grid.dots(ph.begin(second), d_up, kx)
                ph.end(up[kx])

        up_dots(turns[:-1])
        b_part = lambda kz: ph.now(x_b[kz // 2 * 2][(kz % 2) * blk : (kz % 2 + 1) * blk])
        b_sum = lambda kz: plus(rows_of(other, kz, kz + 1)[0], b_part(kz))
        b_2, b_3 = (ph.begin(b_sum(kz).astype(BF16)) for kz in (2, 3))
        ph.end(b_2, b_3)
        ph.close()

        up_rows = lambda kz: ph.reduce_x(rows_of(up, kz, kz + 1))
        x_up = {2: up_rows(2)}
        b_2 = ph.send_z(b_2, 3)
        b_3 = ph.send_z(b_3, 1)
        up_dots(turns[-1:])
        first_sum = ph.begin(plus(part(first, 0), ph.now(a_3), ph.now(a_1)))
        ph.end(first_sum)
        ph.close()

        x_up[3] = up_rows(3)
        up_sum = lambda kz: plus(rows_of(up, kz, kz + 1)[0], ph.now(x_up[kz]))
        u_2 = ph.send_z(up_sum(2).astype(BF16), 3)
        b_1 = ph.begin((b_sum(1) + ph.now(b_2).astype(F32)).astype(BF16))
        ph.end(b_1)
        d_second[-1] = ph.begin(d_second[-1])
        d_hidden, d_att_own, sums2 = by_rows(
            second_back_kernel, relative, present, [hidden, *two(att), *two(d_second), dy], mods,
            [F32, BF16], 3,
        )
        ph.end(d_att_own)
        d_att_other = ph.hand_over(d_att_own)
        ph.close()

        x_up[1] = up_rows(1)
        x_first = ph.reduce_x(first_sum.astype(BF16))
        u_3 = ph.send_z(up_sum(3).astype(BF16), 1)
        b_1 = ph.send_z(b_1, 3)
        d_att = join(d_att_own, ph.begin(d_att_other))
        d_mixed = matmul(d_att, w_o).astype(BF16)
        ph.end(d_mixed)
        attend_back = functools.partial(attend_back_kernel, local_heads)
        d_qkv = by_image(attend_back, length, 3 * local_width, qkv, ph.begin(d_mixed))
        ph.end(d_qkv)
        d_normed_part = matmul(ph.begin(d_qkv)[rows:], w_a, True).astype(BF16)
        ph.end(d_normed_part)
        d_normed_part = ph.hand_over(d_normed_part)
        ph.close()

        x_up[0] = up_rows(0)
        u_1 = ph.send_z((up_sum(1) + ph.now(u_2).astype(F32)).astype(BF16), 3)
        d_normed = from_both(d_normed_part, d_qkv, w_a)
        out = dots(d_att, mixed)
        proj = dots(normed, d_qkv)
        ph.close()

        x_out = ph.reduce_x(out)
        mlp_part = matmul(ph.begin(act)[rows:], w_d, True).astype(BF16)
        ph.end(mlp_part)
        mlp_part = ph.send_core(mlp_part)
        up_total = up_sum(0) + ph.now(u_3).astype(F32) + ph.now(u_1).astype(F32)
        up_mine, up_theirs = grid.halves(ph.begin(up_total), 0)
        ph.end(up_mine)
        mlp = from_both(mlp_part, act, w_d)
        up_theirs = ph.hand_over(up_theirs)
        ph.close()

        p_rows = lambda kz: ph.reduce_x(rows_of(proj, kz, kz + 1))
        p_sum = lambda kz: plus(rows_of(proj, kz, kz + 1)[0], ph.now(x_p[kz]))
        out_sum = lambda kz: plus(
            rows_of(out, kz, kz + 1)[0], ph.now(x_out[kz * blk : (kz + 1) * blk])
        )
        x_p = {2: p_rows(2)}
        o_2 = ph.send_z(out_sum(2).astype(BF16), 3)
        o_3 = ph.send_z(out_sum(3).astype(BF16), 1)
        d_normed[-1] = ph.begin(d_normed[-1])
        input_grad, sums1 = by_rows(
            first_back_kernel, relative, present, [tokens, *two(d_normed), d_hidden], mods, [F32], 2
        )
        ph.end(input_grad)
        ph.close(20.0)

        x_p[3] = p_rows(3)
        p_2 = ph.send_z(p_sum(2).astype(BF16), 3)
        o_1 = ph.send_z((out_sum(1) + ph.now(o_2).astype(F32)).astype(BF16), 3)
        down_low = plus(ph.now(first_sum)[0], x_first)
        down_high = b_sum(0) + ph.now(b_3).astype(F32) + ph.now(b_1).astype(F32)
        down_total = ph.begin(jnp.concatenate([down_low, down_high], axis=1))
        down_mine, down_theirs = grid.halves(down_total, 0)
        ph.end(down_mine)
        down_theirs = ph.hand_over(down_theirs)
        ph.close(20.0)

        x_p[1] = p_rows(1)
        p_3 = ph.send_z(p_sum(3).astype(BF16), 1)
        mlp[-1] = ph.begin(mlp[-1])
        block_out, sums3 = by_rows(
            block_out_kernel, relative, present, [hidden, *two(mlp), dy], mods, [BF16], 1
        )
        row_sums = [jnp.sum(v.reshape(count, -1, 8, width), axis=2) for v in (sums1, sums2, sums3)]
        bin_row = jnp.broadcast_to(bins.astype(F32)[:, None, None], (count, 1, width))
        d_mods = turn_out(jnp.concatenate(row_sums, axis=1))
        d_mods = jnp.concatenate([d_mods, bin_row], axis=1)
        ph.end(d_mods)
        d_mods = lax.all_to_all(d_mods, "dp", split_axis=2, concat_axis=0, tiled=True)
        up_part = grid.by_core(ph.begin(up_mine), up_theirs, 1)
        ph.end(up_part)
        ph.close(20.0)

        x_p[0] = p_rows(0)
        p_1 = ph.send_z((p_sum(1) + ph.now(p_2).astype(F32)).astype(BF16), 3)
        d_mods = ph.begin(d_mods)
        rows_in_order = jnp.stack([d_mods[:, k] for k in (0, 1, 4, 2, 3, 5)], axis=1)
        onehot_all = (d_mods[:, 6, :1] == table_rows.astype(F32)).astype(F32)
        table_part = jnp.einsum("sb,std->btd", onehot_all, rows_in_order, precision=HIGH)
        ph.end(table_part)
        down_part = grid.by_core(ph.begin(down_mine), down_theirs, 1)
        ph.end(down_part)
        out_total = out_sum(0) + ph.now(o_3).astype(F32) + ph.now(o_1).astype(F32)
        out_mine, out_theirs = grid.halves(ph.begin(out_total), 0)
        ph.end(out_mine)
        out_theirs = ph.hand_over(out_theirs)
        ph.close(20.0)

        out_part = grid.by_core(out_mine, ph.begin(out_theirs), 1)
        qkv_part = p_sum(0) + ph.now(p_3).astype(F32) + ph.now(p_1).astype(F32)
        qkv_part = qkv_part.reshape(-1, 3, local_width).transpose(1, 0, 2)
        qkv_part = grid.own_rows(qkv_part)
        block_out, input_grad = (
            turn_out(value).reshape(count, length, width) for value in (block_out, input_grad)
        )
        return (block_out, input_grad, table_part, qkv_part, out_part, up_part, down_part)

    return body


def solution(mesh):
    in_specs = (
        P("dp", None, None),
        P(),
        P(None, "dp", "mp"),
        P("dp", "mp"),
        P("dp", "mp"),
        P("dp", "mp"),
        P("dp"),
        P("dp"),
        P("dp", None, None),
    )
    out_specs = (
        P("dp", None, None),
        P("dp", None, None),
        P(None, None, "dp"),
        P(None, "dp", "mp"),
        P("dp", "mp"),
        P("dp", "mp"),
        P("dp", "mp"),
    )
    body = make_body(mesh.shape["dp"], mesh.shape["mp"])
    return jax.shard_map(body, mesh=mesh, in_specs=in_specs, out_specs=out_specs, check_vma=False)
```

```python
import functools

import jax
import jax.numpy as jnp
from jax import lax
from jax.experimental import pallas as pl
from jax.experimental.pallas import tpu as pltpu
from jax.sharding import PartitionSpec as P

HEAD_DIM = 128
EPS = 1e-06
HIGH = lax.Precision.HIGHEST
F32 = jnp.float32
BF16 = jnp.bfloat16
CORES = 2
TILE = 128
CHUNK = 16


def after(value, *earlier):
    return lax.optimization_barrier((value, *earlier))[0]


def pass_on(in_ref, out_ref):
    out_ref[...] = in_ref[...]


def pace(token, cost):
    return pl.pallas_call(
        pass_on,
        out_shape=jax.ShapeDtypeStruct(token.shape, token.dtype),
        cost_estimate=pl.CostEstimate(
            flops=int(cost * 1.15e9), bytes_accessed=8192, transcendentals=0
        ),
    )(token)


class Phases:
    def __init__(self, dp, mp):
        self.z = 4 if (dp // CORES) % 4 == 0 else 1
        self.x = dp // CORES // self.z
        self.tail, self.results, self.sent, self.last = (), [], [], ()
        self.turn = [(i, (i + 1) % mp) for i in range(mp)]
        self.token = jnp.zeros((8, 128), F32)

    def ring(self, dz, dx, dc):
        index = lambda z, x, c: (z % self.z * self.x + x % self.x) * CORES + c % CORES
        return [
            (index(z, x, c), index(z + dz, x + dx, c + dc))
            for z in range(self.z)
            for x in range(self.x)
            for c in range(CORES)
        ]

    def send(self, value, dz, dx, hold=True):
        value = after(value, *self.tail)
        self.sent.append(value)
        out = lax.ppermute(value, "dp", self.ring(dz, dx, 0))
        if hold:
            self.results.append(out)
        return out

    def send_z(self, value, places):
        return self.send(value, places, 0)

    def send_x(self, value):
        return self.send(value, 0, 1)

    def send_core(self, value):
        return lax.ppermute(value, "dp", self.ring(0, 0, 1))

    def hand_over(self, value):
        out = self.send_core(value)
        self.results.append(out)
        return out

    def across(self, part):
        out = [lax.optimization_barrier(part)]
        for _ in range(len(self.turn) - 1):
            out.append(lax.ppermute(out[-1], "mp", self.turn))
        return out

    def now(self, value):
        return after(value, *self.tail)

    def begin(self, value):
        return after(value, *self.tail, *self.sent, *self.last)

    def end(self, *values):
        self.last = values

    def close(self, cost=25.0):
        self.token = pace(after(self.token, *self.tail, *self.sent), cost)
        self.tail = (*self.results, *self.last, self.token)
        self.results, self.sent, self.last = [], [], ()

    def gather_x(self, piece):
        pieces = [piece]
        for _ in range(1, self.x):
            pieces.append(self.send_x(pieces[-1]))
        return pieces

    def reduce_x(self, blocks):
        moving = None
        for kx in range(1, self.x):
            value = blocks[kx]
            if moving is not None:
                value = value.astype(F32) + moving.astype(F32)
            moving = self.send_x(value.astype(BF16))
        return moving


def plus(first, *others):
    total = first.astype(F32)
    for other in others:
        if other is not None:
            total = total + other.astype(F32)
    return total


class Grid:
    def __init__(self, phases):
        self.z, self.x, self.phases = phases.z, phases.x, phases
        me = lax.axis_index("dp")
        self.at_z, self.at_x, self.core = (
            me // (self.x * CORES),
            (me // CORES) % self.x,
            me % CORES,
        )

    def to_relative(self):
        return jnp.stack(
            [
                (self.at_z - kz) % self.z * self.x + (self.at_x - kx) % self.x
                for kx in range(self.x)
                for kz in range(self.z)
            ]
        ).astype(jnp.int32)

    def to_absolute(self):
        return jnp.stack(
            [
                (self.at_x - ox) % self.x * self.z + (self.at_z - oz) % self.z
                for oz in range(self.z)
                for ox in range(self.x)
            ]
        ).astype(jnp.int32)

    def by_core(self, first, second, axis):
        return jnp.where(
            self.core == 0,
            jnp.concatenate([first, second], axis=axis),
            jnp.concatenate([second, first], axis=axis),
        )

    def halves(self, value, axis):
        half = value.shape[axis] // 2
        low = lax.slice_in_dim(value, 0, half, axis=axis)
        high = lax.slice_in_dim(value, half, 2 * half, axis=axis)
        return (
            jnp.where(self.core == 0, low, high),
            jnp.where(self.core == 0, high, low),
        )

    def chip_shard(self, shard):
        mine, theirs = self.halves(shard, 1)
        return self.by_core(mine, self.phases.send_core(theirs), 0)

    def own_rows(self, total):
        mine, theirs = self.halves(total, total.ndim - 2)
        return self.by_core(mine, self.phases.send_core(theirs), total.ndim - 1)

    def dots(self, lhs, rhs, kx):
        width = lhs.shape[1] // self.x
        return lax.dot_general(
            lhs[:, kx * width : (kx + 1) * width],
            rhs,
            (((0,), (0,)), ((), ())),
            preferred_element_type=F32,
        ).astype(BF16)


def copy_block(order_ref, in_ref, out_ref):
    out_ref[...] = in_ref[...]


def reorder(value, order):
    count = order.shape[0]
    shape = value.shape
    flat = value.reshape(-1, shape[-1])
    blk = shape[-1] // count
    if blk % 128:
        return jnp.take(flat.reshape(-1, count, blk), order, axis=1).reshape(shape)
    out = pl.pallas_call(
        copy_block,
        grid_spec=pltpu.PrefetchScalarGridSpec(
            num_scalar_prefetch=1,
            grid=(count,),
            in_specs=[pl.BlockSpec((flat.shape[0], blk), lambda j, s: (0, s[j]))],
            out_specs=pl.BlockSpec((flat.shape[0], blk), lambda j, s: (0, j)),
        ),
        out_shape=jax.ShapeDtypeStruct(flat.shape, flat.dtype),
    )(order, flat)
    return out.reshape(shape)


def dot(lhs, rhs, left, right):
    return lax.dot_general(lhs, rhs, (((left,), (right,)), ((), ())), preferred_element_type=F32)


def softmax(query, keys):
    scores = dot(query, keys, 1, 1) * HEAD_DIM ** (-0.5)
    expo = jnp.exp(scores - jnp.max(scores, axis=-1, keepdims=True))
    return expo / jnp.sum(expo, axis=-1, keepdims=True)


def head_cols(part, head, heads):
    return pl.ds((part * heads + head) * HEAD_DIM, HEAD_DIM)


def attend_kernel(heads, qkv_ref, mixed_ref):
    for head in range(heads):
        query, keys, values = (qkv_ref[:, head_cols(part, head, heads)] for part in range(3))
        probs = softmax(query, keys).astype(BF16)
        mixed = dot(probs, values, 1, 0).astype(BF16)
        mixed_ref[:, head_cols(0, head, heads)] = mixed


def attend_back_kernel(heads, qkv_ref, d_mixed_ref, d_qkv_ref):
    factor = HEAD_DIM ** (-0.5)
    for head in range(heads):
        query, keys, values = (qkv_ref[:, head_cols(part, head, heads)] for part in range(3))
        d_mixed = d_mixed_ref[:, head_cols(0, head, heads)]
        probs = softmax(query, keys)
        d_probs = dot(d_mixed, values, 1, 1)
        d_values = dot(probs.astype(BF16), d_mixed, 0, 0)
        delta = jnp.sum(d_probs * probs, axis=-1, keepdims=True)
        d_scores = (probs * (d_probs - delta)).astype(BF16)
        d_query = dot(d_scores, keys, 1, 0) * factor
        d_keys = dot(d_scores, query, 0, 0) * factor
        d_qkv_ref[:, head_cols(0, head, heads)] = d_query.astype(BF16)
        d_qkv_ref[:, head_cols(1, head, heads)] = d_keys.astype(BF16)
        d_qkv_ref[:, head_cols(2, head, heads)] = d_values.astype(BF16)


def by_image(kernel, length, width, *operands):
    rows = operands[0].shape[0]
    block = lambda cols: pl.BlockSpec((length, cols), lambda image: (image, 0))
    return pl.pallas_call(
        kernel,
        grid=(rows // length,),
        in_specs=[block(operand.shape[1]) for operand in operands],
        out_specs=block(width),
        out_shape=jax.ShapeDtypeStruct((rows, width), BF16),
        compiler_params=pltpu.CompilerParams(vmem_limit_bytes=32 * 1024 * 1024),
        cost_estimate=pl.CostEstimate(
            flops=rows * length * width * 8, bytes_accessed=rows * 8192, transcendentals=rows * 1024
        ),
    )(*operands)


def normal(value):
    centre = value - jnp.mean(value, axis=-1, keepdims=True)
    factor = lax.rsqrt(jnp.mean(centre * centre, axis=-1, keepdims=True) + EPS)
    return centre * factor, factor


def normal_back(grad, unit, factor):
    mean = jnp.mean(grad, axis=-1, keepdims=True)
    along = jnp.mean(grad * unit, axis=-1, keepdims=True)
    return factor * (grad - mean - unit * along)


class Rows:
    def __init__(self, blocks, order_ref, width):
        self.blocks, self.order, self.width = blocks, order_ref, width

    def each(self, count, body):
        def step(index, carry):
            body(pl.ds(pl.multiple_of(index * CHUNK, CHUNK), CHUNK))
            return carry

        lax.fori_loop(0, count // CHUNK, step, 0)

    def places(self):
        if not self.blocks:
            return [(slice(0, self.width), slice(0, self.width))]
        blk = self.width // self.blocks
        return [
            (
                slice(k * blk, (k + 1) * blk),
                pl.ds(pl.multiple_of(self.order[k] * blk, blk), blk),
            )
            for k in range(self.blocks)
        ]


def clear_sums(sums_ref):
    @pl.when(pl.program_id(1) == 0)
    def _():
        sums_ref[...] = jnp.zeros_like(sums_ref)


def add_sums(sums_ref, places, *terms):
    for index, term in enumerate(terms):
        low, high = term[:8], term[8:]
        for here, there in places:
            sums_ref[0, index * 8 : index * 8 + 8, there] += low[:, here] + high[:, here]


def first_norm_kernel(blocks, order_ref, present_ref, tokens_ref, mods_ref, kept_ref, normed_ref):
    rows = Rows(blocks, order_ref, tokens_ref.shape[1])
    for here, there in rows.places():
        kept_ref[:, here] = tokens_ref[:, there]

    def body(some):
        unit, _ = normal(kept_ref[some, :].astype(F32))
        value = unit * (1.0 + mods_ref[0, 1:2, :]) + mods_ref[0, 0:1, :]
        normed_ref[some, :] = value.astype(BF16)

    rows.each(tokens_ref.shape[0], body)


def cotangent_kernel(blocks, order_ref, present_ref, cotangent_ref, mods_ref, dy_ref, d_mlp_ref):
    rows = Rows(blocks, order_ref, cotangent_ref.shape[1])
    mask = present_ref[pl.program_id(0)].astype(F32)
    for here, there in rows.places():
        dy = cotangent_ref[:, there].astype(F32) * mask
        dy_ref[:, here] = dy.astype(BF16)
        d_mlp_ref[:, here] = (mods_ref[0, 5:6, here] * dy).astype(BF16)


def second_norm_kernel(
    blocks, order_ref, present_ref, tokens_ref, att_a, att_b, mods_ref, hidden_ref, second_ref
):
    rows = Rows(blocks, order_ref, tokens_ref.shape[1])

    def body(some):
        att = att_a[some, :].astype(F32) + att_b[some, :].astype(F32)
        hidden = tokens_ref[some, :].astype(F32) + mods_ref[0, 2:3, :] * att
        hidden_ref[some, :] = hidden
        unit, _ = normal(hidden)
        value = unit * (1.0 + mods_ref[0, 4:5, :]) + mods_ref[0, 3:4, :]
        second_ref[some, :] = value.astype(BF16)

    rows.each(tokens_ref.shape[0], body)


def second_back_kernel(
    blocks, order_ref, present_ref, hidden_ref, att_a, att_b, d_a, d_b, dy_ref, mods_ref,
    d_hidden_ref, d_att_ref, sums_ref,
):
    rows = Rows(blocks, order_ref, hidden_ref.shape[1])
    places = rows.places()
    clear_sums(sums_ref)

    def body(some):
        grad = d_a[some, :].astype(F32) + d_b[some, :].astype(F32)
        unit, factor = normal(hidden_ref[some, :])
        add_sums(sums_ref, places, grad, grad * unit)
        d_hidden = normal_back(grad * (1.0 + mods_ref[0, 4:5, :]), unit, factor)
        d_hidden = dy_ref[some, :].astype(F32) + d_hidden
        d_hidden_ref[some, :] = d_hidden
        d_att_ref[some, :] = (mods_ref[0, 2:3, :] * d_hidden).astype(BF16)
        att = att_a[some, :].astype(F32) + att_b[some, :].astype(F32)
        add_sums(sums_ref.at[:, 16:24], places, d_hidden * att)

    rows.each(hidden_ref.shape[0], body)


def first_back_kernel(
    blocks, order_ref, present_ref, tokens_ref, d_a, d_b, d_hidden_ref, mods_ref,
    input_grad_ref, sums_ref,
):
    rows = Rows(blocks, order_ref, tokens_ref.shape[1])
    places = rows.places()
    clear_sums(sums_ref)

    def body(some):
        grad = d_a[some, :].astype(F32) + d_b[some, :].astype(F32)
        unit, factor = normal(tokens_ref[some, :].astype(F32))
        add_sums(sums_ref, places, grad, grad * unit)
        value = normal_back(grad * (1.0 + mods_ref[0, 1:2, :]), unit, factor)
        value = d_hidden_ref[some, :] + value
        for here, there in places:
            input_grad_ref[some, there] = value[:, here]

    rows.each(tokens_ref.shape[0], body)


def block_out_kernel(
    blocks, order_ref, present_ref, hidden_ref, mlp_a, mlp_b, dy_ref, mods_ref,
    block_out_ref, sums_ref,
):
    rows = Rows(blocks, order_ref, hidden_ref.shape[1])
    places = rows.places()
    mask = present_ref[pl.program_id(0)].astype(F32)
    clear_sums(sums_ref)

    def body(some):
        mlp = mlp_a[some, :].astype(F32) + mlp_b[some, :].astype(F32)
        add_sums(sums_ref, places, dy_ref[some, :].astype(F32) * mlp)
        value = mask * (hidden_ref[some, :] + mods_ref[0, 5:6, :] * mlp)
        for here, there in places:
            block_out_ref[some, there] = value[:, here].astype(BF16)

    rows.each(hidden_ref.shape[0], body)


def by_rows(kernel, order, present, operands, mods, kinds, sums=0):
    images, kinds_of_mods, width = mods.shape
    tiles = operands[0].shape[0] // images // TILE
    row = pl.BlockSpec((TILE, width), lambda i, t, *s: (i * tiles + t, 0))
    whole = lambda count: pl.BlockSpec((1, count, width), lambda i, t, *s: (i, 0, 0))
    shapes = [jax.ShapeDtypeStruct(operands[0].shape, kind) for kind in kinds]
    specs = [row] * len(kinds)
    if sums:
        shapes.append(jax.ShapeDtypeStruct((images, 8 * sums, width), F32))
        specs.append(whole(8 * sums))
    blocks = 0 if width // order.shape[0] % 128 else order.shape[0]
    return pl.pallas_call(
        functools.partial(kernel, blocks),
        grid_spec=pltpu.PrefetchScalarGridSpec(
            num_scalar_prefetch=2,
            grid=(images, tiles),
            in_specs=[row] * len(operands) + [whole(kinds_of_mods)],
            out_specs=specs,
        ),
        out_shape=shapes,
        compiler_params=pltpu.CompilerParams(vmem_limit_bytes=40 * 1024 * 1024),
        cost_estimate=pl.CostEstimate(
            flops=operands[0].size * 6000, bytes_accessed=operands[0].size * 8, transcendentals=0
        ),
    )(order, present, *operands, mods)


def matmul(lhs, rhs, turned=False):
    return lax.dot_general(
        lhs, rhs, (((1,), (1 if turned else 0,)), ((), ())), preferred_element_type=F32
    )


def make_body(dp, mp):
    def body(tokens, mod_table, w_qkv, w_out_t, w_up, w_down, bins, present, cotangent):
        count, length, width = tokens.shape
        rows = count * length
        ph = Phases(dp, mp)
        grid = Grid(ph)
        relative, absolute = grid.to_relative(), grid.to_absolute()
        turns = list(range(1, grid.x)) + [0]
        outside = width // relative.shape[0] % 128
        turn_in = lambda value: reorder(value, relative) if outside else value
        turn_out = lambda value: reorder(value, absolute) if outside else value
        flat = lambda value: value.reshape(rows, width)
        join = lambda own, theirs: jnp.concatenate([own, theirs], axis=0)

        def whole(*by_z):
            return jnp.concatenate(
                [by_z[kz][kx] for kx in range(grid.x) for kz in range(grid.z)], axis=0
            )

        def from_both(theirs, value, weight, between=None):
            if between is not None:
                between()
            part = matmul(ph.begin(value[:rows]), weight, True) + theirs.astype(F32)
            part = part.astype(BF16)
            ph.end(part)
            return ph.across(part)

        def two(parts):
            return parts if len(parts) == 2 else [plus(*parts), jnp.zeros_like(parts[0])]

        def dots(lhs, rhs):
            kept = {}
            for kx in turns:
                kept[kx] = grid.dots(ph.begin(lhs), rhs, kx)
                ph.end(kept[kx])
            return kept

        def rows_of(kept, low, high):
            blk = width // grid.x // grid.z
            return {kx: kept[kx][low * blk : high * blk] for kx in kept}

        wide = w_qkv.reshape(3, -1, CORES, w_qkv.shape[2] // CORES).transpose(1, 2, 0, 3)
        s_q = grid.chip_shard(wide.reshape(w_qkv.shape[1], -1))
        z_q, x_q = {1: ph.send_z(s_q, 1)}, {0: ph.gather_x(s_q)}
        s_o = grid.chip_shard(ph.begin(w_out_t))
        ph.end(s_o)
        x_o = jnp.stack(ph.gather_x(s_o))
        table_rows = jnp.arange(mod_table.shape[0])[None, :]
        onehot = (bins[:, None] == table_rows).astype(F32)
        mods = jnp.einsum("cb,btd->ctd", ph.begin(onehot), mod_table, precision=HIGH)
        mods = reorder(mods, relative)
        ph.end(mods)
        ph.close()

        z_q[3] = ph.send_z(s_q, 3)
        x_q[1] = ph.gather_x(z_q[1])
        tokens, normed_own = by_rows(
            first_norm_kernel, relative, present, [flat(turn_in(ph.begin(tokens)))], mods, [BF16, BF16]
        )
        ph.end(normed_own)
        normed_other = ph.hand_over(normed_own)
        ph.close()

        z_q[2] = ph.send_z(z_q[1], 1)
        x_q[3] = ph.gather_x(z_q[3])
        s_u = grid.chip_shard(ph.begin(w_up))
        ph.end(s_u)
        normed = join(normed_own, ph.begin(normed_other))
        ph.end(normed)
        ph.close()

        z_o = {0: x_o, 1: ph.send_z(x_o, 1)}
        x_q[2] = ph.gather_x(z_q[2])
        s_d = grid.chip_shard(ph.begin(w_down))
        ph.end(s_d)
        ph.close()

        z_o[3] = ph.send_z(x_o, 3)
        z_o[2] = ph.send_z(z_o[1], 1)
        x_u = {0: ph.gather_x(s_u)}
        w_a = whole(x_q[0], x_q[1], x_q[2], x_q[3])
        local_width = s_o.shape[1]
        local_heads = local_width // HEAD_DIM
        qkv = matmul(ph.begin(normed), w_a).astype(BF16)
        ph.end(qkv)
        attend = functools.partial(attend_kernel, local_heads)
        mixed = by_image(attend, length, local_width, ph.begin(qkv))
        ph.end(mixed)
        w_o = jnp.concatenate([z_o[kz][kx] for kx in range(grid.x) for kz in range(grid.z)], axis=0)
        att_part = matmul(ph.begin(mixed)[rows:], w_o, True).astype(BF16)
        ph.end(att_part)
        att_part = ph.hand_over(att_part)
        ph.close()

        z_u = {1: ph.send_z(s_u, 1)}
        x_d = {0: ph.gather_x(s_d)}
        att = from_both(att_part, mixed, w_o)
        dy, d_mlp_own = by_rows(
            cotangent_kernel, relative, present, [flat(turn_in(ph.begin(cotangent)))], mods, [BF16, BF16]
        )
        ph.end(d_mlp_own)
        ph.close()

        z_u[3] = ph.send_z(s_u, 3)
        x_u[1] = ph.gather_x(z_u[1])
        d_mlp_other = ph.hand_over(ph.now(d_mlp_own))
        ph.close()

        z_u[2] = ph.send_z(z_u[1], 1)
        x_u[3] = ph.gather_x(z_u[3])
        att[-1] = ph.begin(att[-1])
        hidden, second_own = by_rows(
            second_norm_kernel, relative, present, [tokens, *two(att)], mods, [F32, BF16]
        )
        ph.end(second_own)
        second_other = ph.hand_over(second_own)
        ph.close()

        z_d = {1: ph.send_z(s_d, 1)}
        x_u[2] = ph.gather_x(z_u[2])
        second = join(second_own, ph.begin(second_other))
        ph.end(second)
        d_mlp = join(d_mlp_own, ph.begin(d_mlp_other))
        ph.end(d_mlp)
        ph.close()

        z_d[3] = ph.send_z(s_d, 3)
        x_d[1] = ph.gather_x(z_d[1])
        w_u = whole(x_u[0], x_u[1], x_u[2], x_u[3])
        up_val = matmul(ph.begin(second), w_u)
        act = jax.nn.gelu(up_val).astype(BF16)
        ph.end(act)
        ph.close()

        z_d[2] = ph.send_z(z_d[1], 1)
        x_d[3] = ph.gather_x(z_d[3])
        down = dots(d_mlp, act)
        half = down[0].shape[1] // 2
        first = jnp.stack([down[kx][:, :half] for kx in range(grid.x)])
        other = {kx: down[kx][:, half:] for kx in down}
        ph.end(first)
        up_val = ph.begin(up_val)
        _, gelu_pull = jax.vjp(jax.nn.gelu, up_val)
        slope = gelu_pull(jnp.ones_like(up_val))[0]
        ph.end(slope)
        ph.close()

        blk = first.shape[1] // grid.z
        part = lambda stacked, kz: stacked[:, kz * blk : (kz + 1) * blk]
        x_d[2] = ph.gather_x(z_d[2])
        a_2 = ph.send_z(part(first, 2), 3)
        step = width // (grid.x * grid.z)
        feature_blocks = lambda value, some: jnp.concatenate(
            [
                value[:, (kx * grid.z + kz) * step : (kx * grid.z + kz + 1) * step]
                for kx in range(grid.x)
                for kz in some
            ],
            axis=1,
        )
        some_of = lambda by_z, some: jnp.concatenate(
            [by_z[kz][kx] for kx in range(grid.x) for kz in some], axis=0
        )
        there = [kz for kz in range(grid.z) if kz != 2]
        late = feature_blocks(d_mlp, [2])
        w_d = [some_of(x_d, there)]
        d_act = [
            matmul(ph.begin(feature_blocks(d_mlp[half_rows], there)), w_d[0])
            for half_rows in (slice(0, rows), slice(rows, None))
        ]
        ph.end(*d_act, late)
        ph.close()

        x_b = {2: ph.reduce_x(rows_of(other, 2, 4))}
        a_3 = ph.send_z(part(first, 3), 1)
        w_d.append(some_of(x_d, [2]))
        d_act = jnp.concatenate(d_act, axis=0) + matmul(ph.begin(late), w_d[1])
        d_up = (d_act * slope).astype(BF16)
        ph.end(d_up)
        d_second_part = matmul(ph.begin(d_up)[rows:], w_u, True).astype(BF16)
        ph.end(d_second_part)
        d_second_part = ph.hand_over(d_second_part)
        a_1 = ph.begin(plus(part(first, 1), ph.now(a_2)).astype(BF16))
        ph.end(a_1)
        ph.close()

        x_b[0] = ph.reduce_x(rows_of(other, 0, 2))
        a_1 = ph.send_z(a_1, 3)
        d_second = from_both(d_second_part, d_up, w_u)
        up = {}

        def up_dots(blocks):
            for kx in blocks:
                up[kx] = grid.dots(ph.begin(second), d_up, kx)
                ph.end(up[kx])

        up_dots(turns[:-1])
        b_part = lambda kz: ph.now(x_b[kz // 2 * 2][(kz % 2) * blk : (kz % 2 + 1) * blk])
        b_sum = lambda kz: plus(rows_of(other, kz, kz + 1)[0], b_part(kz))
        b_2, b_3 = (ph.begin(b_sum(kz).astype(BF16)) for kz in (2, 3))
        ph.end(b_2, b_3)
        ph.close()

        up_rows = lambda kz: ph.reduce_x(rows_of(up, kz, kz + 1))
        x_up = {2: up_rows(2)}
        b_2 = ph.send_z(b_2, 3)
        b_3 = ph.send_z(b_3, 1)
        up_dots(turns[-1:])
        first_sum = ph.begin(plus(part(first, 0), ph.now(a_3), ph.now(a_1)))
        ph.end(first_sum)
        ph.close()

        x_up[3] = up_rows(3)
        up_sum = lambda kz: plus(rows_of(up, kz, kz + 1)[0], ph.now(x_up[kz]))
        u_2 = ph.send_z(up_sum(2).astype(BF16), 3)
        b_1 = ph.begin((b_sum(1) + ph.now(b_2).astype(F32)).astype(BF16))
        ph.end(b_1)
        d_second[-1] = ph.begin(d_second[-1])
        d_hidden, d_att_own, sums2 = by_rows(
            second_back_kernel, relative, present, [hidden, *two(att), *two(d_second), dy], mods,
            [F32, BF16], 3,
        )
        ph.end(d_att_own)
        d_att_other = ph.hand_over(d_att_own)
        ph.close()

        x_up[1] = up_rows(1)
        x_first = ph.reduce_x(first_sum.astype(BF16))
        u_3 = ph.send_z(up_sum(3).astype(BF16), 1)
        b_1 = ph.send_z(b_1, 3)
        d_att = join(d_att_own, ph.begin(d_att_other))
        d_mixed = matmul(d_att, w_o).astype(BF16)
        ph.end(d_mixed)
        attend_back = functools.partial(attend_back_kernel, local_heads)
        d_qkv = by_image(attend_back, length, 3 * local_width, qkv, ph.begin(d_mixed))
        ph.end(d_qkv)
        d_normed_part = matmul(ph.begin(d_qkv)[rows:], w_a, True).astype(BF16)
        ph.end(d_normed_part)
        d_normed_part = ph.hand_over(d_normed_part)
        ph.close()

        x_up[0] = up_rows(0)
        u_1 = ph.send_z((up_sum(1) + ph.now(u_2).astype(F32)).astype(BF16), 3)
        d_normed = from_both(d_normed_part, d_qkv, w_a)
        out = dots(d_att, mixed)
        proj = dots(normed, d_qkv)
        ph.close()

        x_out = ph.reduce_x(out)
        down_of = lambda value: jnp.concatenate([matmul(value, w, True) for w in w_d], axis=1)
        mlp_part = down_of(ph.begin(act)[rows:]).astype(BF16)
        ph.end(mlp_part)
        mlp_part = ph.hand_over(mlp_part)
        up_total = up_sum(0) + ph.now(u_3).astype(F32) + ph.now(u_1).astype(F32)
        up_mine, up_theirs = grid.halves(ph.begin(up_total), 0)
        ph.end(up_mine)
        up_theirs = ph.hand_over(up_theirs)
        ph.close()

        p_rows = lambda kz: ph.reduce_x(rows_of(proj, kz, kz + 1))
        p_sum = lambda kz: plus(rows_of(proj, kz, kz + 1)[0], ph.now(x_p[kz]))
        out_sum = lambda kz: plus(
            rows_of(out, kz, kz + 1)[0], ph.now(x_out[kz * blk : (kz + 1) * blk])
        )
        x_p = {2: p_rows(2)}
        o_2 = ph.send_z(out_sum(2).astype(BF16), 3)
        o_3 = ph.send_z(out_sum(3).astype(BF16), 1)
        mlp = (down_of(ph.begin(act)[:rows]) + mlp_part.astype(F32)).astype(BF16)
        ph.end(mlp)
        mlp = ph.across(mlp)
        d_normed[-1] = ph.begin(d_normed[-1])
        input_grad, sums1 = by_rows(
            first_back_kernel, relative, present, [tokens, *two(d_normed), d_hidden], mods, [F32], 2
        )
        ph.end(input_grad)
        up_part = grid.by_core(ph.begin(up_mine), up_theirs, 1)
        ph.end(up_part)
        ph.close(20.0)

        x_p[3] = p_rows(3)
        p_2 = ph.send_z(p_sum(2).astype(BF16), 3)
        o_1 = ph.send_z((out_sum(1) + ph.now(o_2).astype(F32)).astype(BF16), 3)
        row_sums = [jnp.sum(v.reshape(count, -1, 8, width), axis=2) for v in (sums1, sums2)]
        row_sums = ph.begin(jnp.concatenate(row_sums, axis=1))
        down_low = plus(ph.now(first_sum)[0], x_first)
        down_high = b_sum(0) + ph.now(b_3).astype(F32) + ph.now(b_1).astype(F32)
        down_total = jnp.concatenate([down_low, down_high], axis=1)
        down_mine, down_theirs = grid.halves(ph.begin(down_total), 0)
        ph.end(down_mine, row_sums)
        down_theirs = ph.hand_over(down_theirs)
        ph.close(20.0)

        x_p[1] = p_rows(1)
        p_3 = ph.send_z(p_sum(3).astype(BF16), 1)
        down_part = grid.by_core(ph.begin(down_mine), down_theirs, 1)
        ph.end(down_part)
        mlp[-1] = ph.begin(mlp[-1])
        places = [(kx, kz) for some in (there, [2]) for kx in range(grid.x) for kz in some]
        in_order = [places.index((kx, kz)) for kx in range(grid.x) for kz in range(grid.z)]
        mlp = [
            jnp.concatenate([v[:, k * step : (k + 1) * step] for k in in_order], axis=1) for v in mlp
        ]
        block_out, sums3 = by_rows(
            block_out_kernel, relative, present, [hidden, *two(mlp), dy], mods, [BF16], 1
        )
        ph.end(block_out)
        ph.close(20.0)

        x_p[0] = p_rows(0)
        p_1 = ph.send_z((p_sum(1) + ph.now(p_2).astype(F32)).astype(BF16), 3)
        sums3 = jnp.sum(sums3.reshape(count, -1, 8, width), axis=2)
        bin_row = jnp.broadcast_to(bins.astype(F32)[:, None, None], (count, 1, width))
        d_mods = turn_out(jnp.concatenate([row_sums, sums3], axis=1))
        d_mods = jnp.concatenate([d_mods, bin_row], axis=1)
        d_mods = d_mods.reshape(-1, dp, width // dp).transpose(1, 0, 2)
        d_mods = ph.begin(d_mods)
        ph.end(d_mods)
        d_mods = lax.all_to_all(d_mods, "dp", split_axis=0, concat_axis=0, tiled=True)
        out_total = out_sum(0) + ph.now(o_3).astype(F32) + ph.now(o_1).astype(F32)
        out_mine, out_theirs = grid.halves(ph.begin(out_total), 0)
        ph.end(out_mine)
        out_theirs = ph.hand_over(out_theirs)
        ph.close(20.0)

        d_mods = ph.now(d_mods).reshape(dp * count, -1, width // dp)
        rows_in_order = jnp.stack([d_mods[:, k] for k in (0, 1, 4, 2, 3, 5)], axis=1)
        onehot_all = (d_mods[:, 6, :1] == table_rows.astype(F32)).astype(F32)
        table_part = jnp.einsum("sb,std->btd", onehot_all, rows_in_order, precision=HIGH)
        out_part = grid.by_core(out_mine, ph.now(out_theirs), 1)
        qkv_part = p_sum(0) + ph.now(p_3).astype(F32) + ph.now(p_1).astype(F32)
        qkv_part = qkv_part.reshape(-1, 3, local_width).transpose(1, 0, 2)
        qkv_part = grid.own_rows(qkv_part)
        block_out, input_grad = (
            turn_out(value).reshape(count, length, width) for value in (block_out, input_grad)
        )
        return (block_out, input_grad, table_part, qkv_part, out_part, up_part, down_part)

    return body


def solution(mesh):
    in_specs = (
        P("dp", None, None),
        P(),
        P(None, "dp", "mp"),
        P("dp", "mp"),
        P("dp", "mp"),
        P("dp", "mp"),
        P("dp"),
        P("dp"),
        P("dp", None, None),
    )
    out_specs = (
        P("dp", None, None),
        P("dp", None, None),
        P(None, None, "dp"),
        P(None, "dp", "mp"),
        P("dp", "mp"),
        P("dp", "mp"),
        P("dp", "mp"),
    )
    body = make_body(mesh.shape["dp"], mesh.shape["mp"])
    return jax.shard_map(body, mesh=mesh, in_specs=in_specs, out_specs=out_specs, check_vma=False)
```

```python
import functools

import jax
import jax.numpy as jnp
from jax import lax
from jax.experimental import pallas as pl
from jax.experimental.pallas import tpu as pltpu
from jax.sharding import PartitionSpec as P

HEAD_DIM = 128
EPS = 1e-06
HIGH = lax.Precision.HIGHEST
F32 = jnp.float32
BF16 = jnp.bfloat16
CORES = 2
TILE = 128
CHUNK = 16
UNROLL = 8


def after(value, *earlier):
    return lax.optimization_barrier((value, *earlier))[0]


def pass_on(in_ref, out_ref):
    out_ref[...] = in_ref[...]


def pace(token, cost):
    return pl.pallas_call(
        pass_on,
        out_shape=jax.ShapeDtypeStruct(token.shape, token.dtype),
        cost_estimate=pl.CostEstimate(
            flops=int(cost * 1.15e9), bytes_accessed=8192, transcendentals=0
        ),
    )(token)


class Phases:
    def __init__(self, dp, mp):
        self.z = 4 if (dp // CORES) % 4 == 0 else 1
        self.x = dp // CORES // self.z
        self.tail, self.results, self.sent, self.last = (), [], [], ()
        self.turn = [(i, (i + 1) % mp) for i in range(mp)]
        self.token = jnp.zeros((8, 128), F32)

    def ring(self, dz, dx, dc):
        index = lambda z, x, c: (z % self.z * self.x + x % self.x) * CORES + c % CORES
        return [
            (index(z, x, c), index(z + dz, x + dx, c + dc))
            for z in range(self.z)
            for x in range(self.x)
            for c in range(CORES)
        ]

    def send(self, value, dz, dx, hold=True):
        value = after(value, *self.tail)
        self.sent.append(value)
        out = lax.ppermute(value, "dp", self.ring(dz, dx, 0))
        if hold:
            self.results.append(out)
        return out

    def send_z(self, value, places):
        return self.send(value, places, 0)

    def send_x(self, value):
        return self.send(value, 0, 1)

    def send_core(self, value):
        return lax.ppermute(value, "dp", self.ring(0, 0, 1))

    def hand_over(self, value):
        out = self.send_core(value)
        self.results.append(out)
        return out

    def across(self, part):
        out = [lax.optimization_barrier(part)]
        for _ in range(len(self.turn) - 1):
            out.append(lax.ppermute(out[-1], "mp", self.turn))
        return out

    def now(self, value):
        return after(value, *self.tail)

    def begin(self, value):
        return after(value, *self.tail, *self.sent, *self.last)

    def end(self, *values):
        self.last = values

    def close(self, cost=25.0):
        self.token = pace(after(self.token, *self.tail, *self.sent), cost)
        self.tail = (*self.results, *self.last, self.token)
        self.results, self.sent, self.last = [], [], ()

    def gather_x(self, piece):
        pieces = [piece]
        for _ in range(1, self.x):
            pieces.append(self.send_x(pieces[-1]))
        return pieces

    def reduce_x(self, blocks):
        moving = None
        for kx in range(1, self.x):
            value = blocks[kx]
            if moving is not None:
                value = value.astype(F32) + moving.astype(F32)
            moving = self.send_x(value.astype(BF16))
        return moving


def plus(first, *others):
    total = first.astype(F32)
    for other in others:
        if other is not None:
            total = total + other.astype(F32)
    return total


class Grid:
    def __init__(self, phases):
        self.z, self.x, self.phases = phases.z, phases.x, phases
        me = lax.axis_index("dp")
        self.at_z, self.at_x, self.core = (
            me // (self.x * CORES),
            (me // CORES) % self.x,
            me % CORES,
        )

    def to_relative(self):
        return jnp.stack(
            [
                (self.at_z - kz) % self.z * self.x + (self.at_x - kx) % self.x
                for kx in range(self.x)
                for kz in range(self.z)
            ]
        ).astype(jnp.int32)

    def to_absolute(self):
        return jnp.stack(
            [
                (self.at_x - ox) % self.x * self.z + (self.at_z - oz) % self.z
                for oz in range(self.z)
                for ox in range(self.x)
            ]
        ).astype(jnp.int32)

    def by_core(self, first, second, axis):
        return jnp.where(
            self.core == 0,
            jnp.concatenate([first, second], axis=axis),
            jnp.concatenate([second, first], axis=axis),
        )

    def halves(self, value, axis):
        half = value.shape[axis] // 2
        low = lax.slice_in_dim(value, 0, half, axis=axis)
        high = lax.slice_in_dim(value, half, 2 * half, axis=axis)
        return (
            jnp.where(self.core == 0, low, high),
            jnp.where(self.core == 0, high, low),
        )

    def chip_shard(self, shard):
        mine, theirs = self.halves(shard, 1)
        return self.by_core(mine, self.phases.send_core(theirs), 0)

    def own_rows(self, total):
        mine, theirs = self.halves(total, total.ndim - 2)
        return self.by_core(mine, self.phases.send_core(theirs), total.ndim - 1)

    def dots(self, lhs, rhs, kx):
        width = lhs.shape[1] // self.x
        return lax.dot_general(
            lhs[:, kx * width : (kx + 1) * width],
            rhs,
            (((0,), (0,)), ((), ())),
            preferred_element_type=F32,
        ).astype(BF16)


def copy_block(order_ref, in_ref, out_ref):
    out_ref[...] = in_ref[...]


def reorder(value, order):
    count = order.shape[0]
    shape = value.shape
    flat = value.reshape(-1, shape[-1])
    blk = shape[-1] // count
    if blk % 128:
        return jnp.take(flat.reshape(-1, count, blk), order, axis=1).reshape(shape)
    out = pl.pallas_call(
        copy_block,
        grid_spec=pltpu.PrefetchScalarGridSpec(
            num_scalar_prefetch=1,
            grid=(count,),
            in_specs=[pl.BlockSpec((flat.shape[0], blk), lambda j, s: (0, s[j]))],
            out_specs=pl.BlockSpec((flat.shape[0], blk), lambda j, s: (0, j)),
        ),
        out_shape=jax.ShapeDtypeStruct(flat.shape, flat.dtype),
    )(order, flat)
    return out.reshape(shape)


def dot(lhs, rhs, left, right):
    return lax.dot_general(lhs, rhs, (((left,), (right,)), ((), ())), preferred_element_type=F32)


def softmax(query, keys):
    scores = dot(query, keys, 1, 1) * HEAD_DIM ** (-0.5)
    expo = jnp.exp(scores - jnp.max(scores, axis=-1, keepdims=True))
    return expo / jnp.sum(expo, axis=-1, keepdims=True)


def head_cols(part, head, heads):
    return pl.ds((part * heads + head) * HEAD_DIM, HEAD_DIM)


def attend_kernel(heads, qkv_ref, mixed_ref):
    for head in range(heads):
        query, keys, values = (qkv_ref[:, head_cols(part, head, heads)] for part in range(3))
        probs = softmax(query, keys).astype(BF16)
        mixed = dot(probs, values, 1, 0).astype(BF16)
        mixed_ref[:, head_cols(0, head, heads)] = mixed


def attend_back_kernel(heads, qkv_ref, d_mixed_ref, d_qkv_ref):
    factor = HEAD_DIM ** (-0.5)
    for head in range(heads):
        query, keys, values = (qkv_ref[:, head_cols(part, head, heads)] for part in range(3))
        d_mixed = d_mixed_ref[:, head_cols(0, head, heads)]
        probs = softmax(query, keys)
        d_probs = dot(d_mixed, values, 1, 1)
        d_values = dot(probs.astype(BF16), d_mixed, 0, 0)
        delta = jnp.sum(d_probs * probs, axis=-1, keepdims=True)
        d_scores = (probs * (d_probs - delta)).astype(BF16)
        d_query = dot(d_scores, keys, 1, 0) * factor
        d_keys = dot(d_scores, query, 0, 0) * factor
        d_qkv_ref[:, head_cols(0, head, heads)] = d_query.astype(BF16)
        d_qkv_ref[:, head_cols(1, head, heads)] = d_keys.astype(BF16)
        d_qkv_ref[:, head_cols(2, head, heads)] = d_values.astype(BF16)


def by_image(kernel, length, width, *operands):
    rows = operands[0].shape[0]
    block = lambda cols: pl.BlockSpec((length, cols), lambda image: (image, 0))
    return pl.pallas_call(
        kernel,
        grid=(rows // length,),
        in_specs=[block(operand.shape[1]) for operand in operands],
        out_specs=block(width),
        out_shape=jax.ShapeDtypeStruct((rows, width), BF16),
        compiler_params=pltpu.CompilerParams(vmem_limit_bytes=32 * 1024 * 1024),
        cost_estimate=pl.CostEstimate(
            flops=rows * length * width * 8, bytes_accessed=rows * 8192, transcendentals=rows * 1024
        ),
    )(*operands)


def normal(value):
    centre = value - jnp.mean(value, axis=-1, keepdims=True)
    factor = lax.rsqrt(jnp.mean(centre * centre, axis=-1, keepdims=True) + EPS)
    return centre * factor, factor


def normal_back(grad, unit, factor):
    mean = jnp.mean(grad, axis=-1, keepdims=True)
    along = jnp.mean(grad * unit, axis=-1, keepdims=True)
    return factor * (grad - mean - unit * along)


class Rows:
    def __init__(self, blocks, order_ref, width):
        self.blocks, self.order, self.width = blocks, order_ref, width

    def each(self, count, body):
        def step(index, carry):
            body(pl.ds(pl.multiple_of(index * CHUNK, CHUNK), CHUNK))
            return carry

        lax.fori_loop(0, count // CHUNK, step, 0, unroll=UNROLL)

    def places(self):
        if not self.blocks:
            return [(slice(0, self.width), slice(0, self.width))]
        blk = self.width // self.blocks
        return [
            (
                slice(k * blk, (k + 1) * blk),
                pl.ds(pl.multiple_of(self.order[k] * blk, blk), blk),
            )
            for k in range(self.blocks)
        ]


def clear_sums(sums_ref):
    @pl.when(pl.program_id(1) == 0)
    def _():
        sums_ref[...] = jnp.zeros_like(sums_ref)


def add_sums(sums_ref, places, *terms):
    for index, term in enumerate(terms):
        low, high = term[:8], term[8:]
        for here, there in places:
            sums_ref[0, index * 8 : index * 8 + 8, there] += low[:, here] + high[:, here]


def first_norm_kernel(blocks, order_ref, present_ref, tokens_ref, mods_ref, kept_ref, normed_ref):
    rows = Rows(blocks, order_ref, tokens_ref.shape[1])
    for here, there in rows.places():
        kept_ref[:, here] = tokens_ref[:, there]

    def body(some):
        unit, _ = normal(kept_ref[some, :].astype(F32))
        value = unit * (1.0 + mods_ref[0, 1:2, :]) + mods_ref[0, 0:1, :]
        normed_ref[some, :] = value.astype(BF16)

    rows.each(tokens_ref.shape[0], body)


def cotangent_kernel(blocks, order_ref, present_ref, cotangent_ref, mods_ref, dy_ref, d_mlp_ref):
    rows = Rows(blocks, order_ref, cotangent_ref.shape[1])
    mask = present_ref[pl.program_id(0)].astype(F32)
    for here, there in rows.places():
        dy = cotangent_ref[:, there].astype(F32) * mask
        dy_ref[:, here] = dy.astype(BF16)
        d_mlp_ref[:, here] = (mods_ref[0, 5:6, here] * dy).astype(BF16)


def second_norm_kernel(
    blocks, order_ref, present_ref, tokens_ref, att_a, att_b, mods_ref, hidden_ref, second_ref
):
    rows = Rows(blocks, order_ref, tokens_ref.shape[1])

    def body(some):
        att = att_a[some, :].astype(F32) + att_b[some, :].astype(F32)
        hidden = tokens_ref[some, :].astype(F32) + mods_ref[0, 2:3, :] * att
        hidden_ref[some, :] = hidden
        unit, _ = normal(hidden)
        value = unit * (1.0 + mods_ref[0, 4:5, :]) + mods_ref[0, 3:4, :]
        second_ref[some, :] = value.astype(BF16)

    rows.each(tokens_ref.shape[0], body)


def second_back_kernel(
    blocks, order_ref, present_ref, hidden_ref, att_a, att_b, d_a, d_b, dy_ref, mods_ref,
    d_hidden_ref, d_att_ref, sums_ref,
):
    rows = Rows(blocks, order_ref, hidden_ref.shape[1])
    places = rows.places()
    clear_sums(sums_ref)

    def body(some):
        grad = d_a[some, :].astype(F32) + d_b[some, :].astype(F32)
        unit, factor = normal(hidden_ref[some, :])
        add_sums(sums_ref, places, grad, grad * unit)
        d_hidden = normal_back(grad * (1.0 + mods_ref[0, 4:5, :]), unit, factor)
        d_hidden = dy_ref[some, :].astype(F32) + d_hidden
        d_hidden_ref[some, :] = d_hidden
        d_att_ref[some, :] = (mods_ref[0, 2:3, :] * d_hidden).astype(BF16)
        att = att_a[some, :].astype(F32) + att_b[some, :].astype(F32)
        add_sums(sums_ref.at[:, 16:24], places, d_hidden * att)

    rows.each(hidden_ref.shape[0], body)


def first_back_kernel(
    blocks, order_ref, present_ref, tokens_ref, d_a, d_b, d_hidden_ref, mods_ref,
    input_grad_ref, sums_ref,
):
    rows = Rows(blocks, order_ref, tokens_ref.shape[1])
    places = rows.places()
    clear_sums(sums_ref)

    def body(some):
        grad = d_a[some, :].astype(F32) + d_b[some, :].astype(F32)
        unit, factor = normal(tokens_ref[some, :].astype(F32))
        add_sums(sums_ref, places, grad, grad * unit)
        value = normal_back(grad * (1.0 + mods_ref[0, 1:2, :]), unit, factor)
        value = d_hidden_ref[some, :] + value
        for here, there in places:
            input_grad_ref[some, there] = value[:, here]

    rows.each(tokens_ref.shape[0], body)


def block_out_kernel(
    blocks, order_ref, present_ref, hidden_ref, mlp_a, mlp_b, dy_ref, mods_ref,
    block_out_ref, sums_ref,
):
    rows = Rows(blocks, order_ref, hidden_ref.shape[1])
    places = rows.places()
    mask = present_ref[pl.program_id(0)].astype(F32)
    clear_sums(sums_ref)

    def body(some):
        mlp = mlp_a[some, :].astype(F32) + mlp_b[some, :].astype(F32)
        add_sums(sums_ref, places, dy_ref[some, :].astype(F32) * mlp)
        value = mask * (hidden_ref[some, :] + mods_ref[0, 5:6, :] * mlp)
        for here, there in places:
            block_out_ref[some, there] = value[:, here].astype(BF16)

    rows.each(hidden_ref.shape[0], body)


def by_rows(kernel, order, present, operands, mods, kinds, sums=0):
    images, kinds_of_mods, width = mods.shape
    tiles = operands[0].shape[0] // images // TILE
    row = pl.BlockSpec((TILE, width), lambda i, t, *s: (i * tiles + t, 0))
    whole = lambda count: pl.BlockSpec((1, count, width), lambda i, t, *s: (i, 0, 0))
    shapes = [jax.ShapeDtypeStruct(operands[0].shape, kind) for kind in kinds]
    specs = [row] * len(kinds)
    if sums:
        shapes.append(jax.ShapeDtypeStruct((images, 8 * sums, width), F32))
        specs.append(whole(8 * sums))
    blocks = 0 if width // order.shape[0] % 128 else order.shape[0]
    return pl.pallas_call(
        functools.partial(kernel, blocks),
        grid_spec=pltpu.PrefetchScalarGridSpec(
            num_scalar_prefetch=2,
            grid=(images, tiles),
            in_specs=[row] * len(operands) + [whole(kinds_of_mods)],
            out_specs=specs,
        ),
        out_shape=shapes,
        compiler_params=pltpu.CompilerParams(vmem_limit_bytes=40 * 1024 * 1024),
        cost_estimate=pl.CostEstimate(
            flops=operands[0].size * 6000, bytes_accessed=operands[0].size * 8, transcendentals=0
        ),
    )(order, present, *operands, mods)


def matmul(lhs, rhs, turned=False):
    return lax.dot_general(
        lhs, rhs, (((1,), (1 if turned else 0,)), ((), ())), preferred_element_type=F32
    )


def make_body(dp, mp):
    def body(tokens, mod_table, w_qkv, w_out_t, w_up, w_down, bins, present, cotangent):
        count, length, width = tokens.shape
        rows = count * length
        ph = Phases(dp, mp)
        grid = Grid(ph)
        relative, absolute = grid.to_relative(), grid.to_absolute()
        turns = list(range(1, grid.x)) + [0]
        outside = width // relative.shape[0] % 128
        turn_in = lambda value: reorder(value, relative) if outside else value
        turn_out = lambda value: reorder(value, absolute) if outside else value
        flat = lambda value: value.reshape(rows, width)
        join = lambda own, theirs: jnp.concatenate([own, theirs], axis=0)

        def whole(*by_z):
            return jnp.concatenate(
                [by_z[kz][kx] for kx in range(grid.x) for kz in range(grid.z)], axis=0
            )

        def from_both(theirs, value, weight, between=None):
            if between is not None:
                between()
            part = matmul(ph.begin(value[:rows]), weight, True) + theirs.astype(F32)
            part = part.astype(BF16)
            ph.end(part)
            return ph.across(part)

        def two(parts):
            return parts if len(parts) == 2 else [plus(*parts), jnp.zeros_like(parts[0])]

        def dots(lhs, rhs):
            kept = {}
            for kx in turns:
                kept[kx] = grid.dots(ph.begin(lhs), rhs, kx)
                ph.end(kept[kx])
            return kept

        def rows_of(kept, low, high):
            blk = width // grid.x // grid.z
            return {kx: kept[kx][low * blk : high * blk] for kx in kept}

        wide = w_qkv.reshape(3, -1, CORES, w_qkv.shape[2] // CORES).transpose(1, 2, 0, 3)
        s_q = grid.chip_shard(wide.reshape(w_qkv.shape[1], -1))
        z_q, x_q = {1: ph.send_z(s_q, 1)}, {0: ph.gather_x(s_q)}
        s_o = grid.chip_shard(ph.begin(w_out_t))
        ph.end(s_o)
        x_o = jnp.stack(ph.gather_x(s_o))
        table_rows = jnp.arange(mod_table.shape[0])[None, :]
        onehot = (bins[:, None] == table_rows).astype(F32)
        mods = jnp.einsum("cb,btd->ctd", ph.begin(onehot), mod_table, precision=HIGH)
        mods = reorder(mods, relative)
        ph.end(mods)
        ph.close()

        z_q[3] = ph.send_z(s_q, 3)
        x_q[1] = ph.gather_x(z_q[1])
        tokens, normed_own = by_rows(
            first_norm_kernel, relative, present, [flat(turn_in(ph.begin(tokens)))], mods, [BF16, BF16]
        )
        ph.end(normed_own)
        normed_other = ph.hand_over(normed_own)
        ph.close()

        z_q[2] = ph.send_z(z_q[1], 1)
        x_q[3] = ph.gather_x(z_q[3])
        s_u = grid.chip_shard(ph.begin(w_up))
        ph.end(s_u)
        normed = join(normed_own, ph.begin(normed_other))
        ph.end(normed)
        ph.close()

        z_o = {0: x_o, 1: ph.send_z(x_o, 1)}
        x_q[2] = ph.gather_x(z_q[2])
        s_d = grid.chip_shard(ph.begin(w_down))
        ph.end(s_d)
        ph.close()

        z_o[3] = ph.send_z(x_o, 3)
        z_o[2] = ph.send_z(z_o[1], 1)
        x_u = {0: ph.gather_x(s_u)}
        w_a = whole(x_q[0], x_q[1], x_q[2], x_q[3])
        local_width = s_o.shape[1]
        local_heads = local_width // HEAD_DIM
        qkv = matmul(ph.begin(normed), w_a).astype(BF16)
        ph.end(qkv)
        attend = functools.partial(attend_kernel, local_heads)
        mixed = by_image(attend, length, local_width, ph.begin(qkv))
        ph.end(mixed)
        w_o = jnp.concatenate([z_o[kz][kx] for kx in range(grid.x) for kz in range(grid.z)], axis=0)
        att_part = matmul(ph.begin(mixed)[rows:], w_o, True).astype(BF16)
        ph.end(att_part)
        att_part = ph.hand_over(att_part)
        ph.close()

        z_u = {1: ph.send_z(s_u, 1)}
        x_d = {0: ph.gather_x(s_d)}
        att = from_both(att_part, mixed, w_o)
        dy, d_mlp_own = by_rows(
            cotangent_kernel, relative, present, [flat(turn_in(ph.begin(cotangent)))], mods, [BF16, BF16]
        )
        ph.end(d_mlp_own)
        ph.close()

        z_u[3] = ph.send_z(s_u, 3)
        x_u[1] = ph.gather_x(z_u[1])
        d_mlp_other = ph.hand_over(ph.now(d_mlp_own))
        ph.close()

        z_u[2] = ph.send_z(z_u[1], 1)
        x_u[3] = ph.gather_x(z_u[3])
        att[-1] = ph.begin(att[-1])
        hidden, second_own = by_rows(
            second_norm_kernel, relative, present, [tokens, *two(att)], mods, [F32, BF16]
        )
        ph.end(second_own)
        second_other = ph.hand_over(second_own)
        ph.close()

        z_d = {1: ph.send_z(s_d, 1)}
        x_u = {kz: [ph.now(piece) for piece in x_u[kz]] for kz in x_u}
        x_u[2] = ph.gather_x(z_u[2])
        second = join(second_own, ph.begin(second_other))
        ph.end(second)
        d_mlp = join(d_mlp_own, ph.begin(d_mlp_other))
        ph.end(d_mlp)
        ph.close()

        z_d[3] = ph.send_z(s_d, 3)
        x_d[1] = ph.gather_x(z_d[1])
        w_u = whole(x_u[0], x_u[1], x_u[2], x_u[3])
        up_val = matmul(ph.begin(second), w_u)
        act = jax.nn.gelu(up_val).astype(BF16)
        ph.end(act)
        ph.close()

        z_d[2] = ph.send_z(z_d[1], 1)
        x_d[3] = ph.gather_x(z_d[3])
        down = dots(d_mlp, act)
        half = down[0].shape[1] // 2
        first = jnp.stack([down[kx][:, :half] for kx in range(grid.x)])
        other = {kx: down[kx][:, half:] for kx in down}
        ph.end(first)
        up_val = ph.begin(up_val)
        _, gelu_pull = jax.vjp(jax.nn.gelu, up_val)
        slope = gelu_pull(jnp.ones_like(up_val))[0]
        ph.end(slope)
        ph.close()

        blk = first.shape[1] // grid.z
        part = lambda stacked, kz: stacked[:, kz * blk : (kz + 1) * blk]
        x_d[2] = ph.gather_x(z_d[2])
        a_2 = ph.send_z(part(first, 2), 3)
        step = width // (grid.x * grid.z)
        feature_blocks = lambda value, some: jnp.concatenate(
            [
                value[:, (kx * grid.z + kz) * step : (kx * grid.z + kz + 1) * step]
                for kx in range(grid.x)
                for kz in some
            ],
            axis=1,
        )
        some_of = lambda by_z, some: jnp.concatenate(
            [by_z[kz][kx] for kx in range(grid.x) for kz in some], axis=0
        )
        there = [kz for kz in range(grid.z) if kz != 2]
        late = feature_blocks(d_mlp, [2])
        w_d = [some_of(x_d, there)]
        d_act = [
            matmul(ph.begin(feature_blocks(d_mlp[half_rows], there)), w_d[0])
            for half_rows in (slice(0, rows), slice(rows, None))
        ]
        ph.end(*d_act, late)
        ph.close()

        x_b = {2: ph.reduce_x(rows_of(other, 2, 4))}
        a_3 = ph.send_z(part(first, 3), 1)
        w_d.append(some_of(x_d, [2]))
        d_act = jnp.concatenate(d_act, axis=0) + matmul(ph.begin(late), w_d[1])
        d_up = (d_act * slope).astype(BF16)
        ph.end(d_up)
        d_second_part = matmul(ph.begin(d_up)[rows:], w_u, True).astype(BF16)
        ph.end(d_second_part)
        d_second_part = ph.hand_over(d_second_part)
        a_1 = ph.begin(plus(part(first, 1), ph.now(a_2)).astype(BF16))
        ph.end(a_1)
        ph.close()

        x_b[0] = ph.reduce_x(rows_of(other, 0, 2))
        a_1 = ph.send_z(a_1, 3)
        d_second = from_both(d_second_part, d_up, w_u)
        up = {}

        def up_dots(blocks):
            for kx in blocks:
                up[kx] = grid.dots(ph.begin(second), d_up, kx)
                ph.end(up[kx])

        up_dots(turns[:-1])
        b_part = lambda kz: ph.now(x_b[kz // 2 * 2][(kz % 2) * blk : (kz % 2 + 1) * blk])
        b_sum = lambda kz: plus(rows_of(other, kz, kz + 1)[0], b_part(kz))
        b_2, b_3 = (ph.begin(b_sum(kz).astype(BF16)) for kz in (2, 3))
        ph.end(b_2, b_3)
        ph.close()

        up_rows = lambda kz: ph.reduce_x(rows_of(up, kz, kz + 1))
        x_up = {2: up_rows(2)}
        b_2 = ph.send_z(b_2, 3)
        b_3 = ph.send_z(b_3, 1)
        up_dots(turns[-1:])
        first_sum = ph.begin(plus(part(first, 0), ph.now(a_3), ph.now(a_1)))
        ph.end(first_sum)
        ph.close()

        x_up[3] = up_rows(3)
        up_sum = lambda kz: plus(rows_of(up, kz, kz + 1)[0], ph.now(x_up[kz]))
        u_2 = ph.send_z(up_sum(2).astype(BF16), 3)
        b_1 = ph.begin((b_sum(1) + ph.now(b_2).astype(F32)).astype(BF16))
        ph.end(b_1)
        d_second[-1] = ph.begin(d_second[-1])
        d_hidden, d_att_own, sums2 = by_rows(
            second_back_kernel, relative, present, [hidden, *two(att), *two(d_second), dy], mods,
            [F32, BF16], 3,
        )
        ph.end(d_att_own)
        d_att_other = ph.hand_over(d_att_own)
        ph.close()

        x_up[1] = up_rows(1)
        x_first = ph.reduce_x(first_sum.astype(BF16))
        u_3 = ph.send_z(up_sum(3).astype(BF16), 1)
        b_1 = ph.send_z(b_1, 3)
        d_att = join(d_att_own, ph.begin(d_att_other))
        d_mixed = matmul(d_att, w_o).astype(BF16)
        ph.end(d_mixed)
        attend_back = functools.partial(attend_back_kernel, local_heads)
        d_qkv = by_image(attend_back, length, 3 * local_width, qkv, ph.begin(d_mixed))
        ph.end(d_qkv)
        d_normed_part = matmul(ph.begin(d_qkv)[rows:], w_a, True).astype(BF16)
        ph.end(d_normed_part)
        d_normed_part = ph.hand_over(d_normed_part)
        ph.close()

        x_up[0] = up_rows(0)
        u_1 = ph.send_z((up_sum(1) + ph.now(u_2).astype(F32)).astype(BF16), 3)
        d_normed = from_both(d_normed_part, d_qkv, w_a)
        out = dots(d_att, mixed)
        proj = dots(normed, d_qkv)
        ph.close()

        x_out = ph.reduce_x(out)
        down_of = lambda value: jnp.concatenate([matmul(value, w, True) for w in w_d], axis=1)
        mlp_part = down_of(ph.begin(act)[rows:]).astype(BF16)
        ph.end(mlp_part)
        mlp_part = ph.hand_over(mlp_part)
        up_total = up_sum(0) + ph.now(u_3).astype(F32) + ph.now(u_1).astype(F32)
        up_mine, up_theirs = grid.halves(ph.begin(up_total), 0)
        ph.end(up_mine)
        up_theirs = ph.hand_over(up_theirs)
        ph.close()

        p_rows = lambda kz: ph.reduce_x(rows_of(proj, kz, kz + 1))
        p_sum = lambda kz: plus(rows_of(proj, kz, kz + 1)[0], ph.now(x_p[kz]))
        out_sum = lambda kz: plus(
            rows_of(out, kz, kz + 1)[0], ph.now(x_out[kz * blk : (kz + 1) * blk])
        )
        x_p = {2: p_rows(2)}
        o_2 = ph.send_z(out_sum(2).astype(BF16), 3)
        o_3 = ph.send_z(out_sum(3).astype(BF16), 1)
        mlp = (down_of(ph.begin(act)[:rows]) + mlp_part.astype(F32)).astype(BF16)
        ph.end(mlp)
        mlp = ph.across(mlp)
        d_normed[-1] = ph.begin(d_normed[-1])
        input_grad, sums1 = by_rows(
            first_back_kernel, relative, present, [tokens, *two(d_normed), d_hidden], mods, [F32], 2
        )
        ph.end(input_grad)
        ph.close(20.0)

        x_p[3] = p_rows(3)
        p_2 = ph.send_z(p_sum(2).astype(BF16), 3)
        up_part = grid.by_core(ph.begin(up_mine), up_theirs, 1)
        ph.end(up_part)
        o_1 = ph.send_z((out_sum(1) + ph.now(o_2).astype(F32)).astype(BF16), 3)
        row_sums = [jnp.sum(v.reshape(count, -1, 8, width), axis=2) for v in (sums1, sums2)]
        row_sums = ph.begin(jnp.concatenate(row_sums, axis=1))
        down_low = plus(ph.now(first_sum)[0], x_first)
        down_high = b_sum(0) + ph.now(b_3).astype(F32) + ph.now(b_1).astype(F32)
        down_total = jnp.concatenate([down_low, down_high], axis=1)
        down_mine, down_theirs = grid.halves(ph.begin(down_total), 0)
        ph.end(down_mine, row_sums)
        down_theirs = ph.hand_over(down_theirs)
        ph.close(20.0)

        x_p[1] = p_rows(1)
        p_3 = ph.send_z(p_sum(3).astype(BF16), 1)
        down_part = grid.by_core(ph.begin(down_mine), down_theirs, 1)
        ph.end(down_part)
        mlp[-1] = ph.begin(mlp[-1])
        places = [(kx, kz) for some in (there, [2]) for kx in range(grid.x) for kz in some]
        in_order = [places.index((kx, kz)) for kx in range(grid.x) for kz in range(grid.z)]
        mlp = [
            jnp.concatenate([v[:, k * step : (k + 1) * step] for k in in_order], axis=1) for v in mlp
        ]
        block_out, sums3 = by_rows(
            block_out_kernel, relative, present, [hidden, *two(mlp), dy], mods, [BF16], 1
        )
        ph.end(block_out)
        ph.close(20.0)

        x_p[0] = p_rows(0)
        p_1 = ph.send_z((p_sum(1) + ph.now(p_2).astype(F32)).astype(BF16), 3)
        sums3 = jnp.sum(sums3.reshape(count, -1, 8, width), axis=2)
        bin_row = jnp.broadcast_to(bins.astype(F32)[:, None, None], (count, 1, width))
        d_mods = turn_out(jnp.concatenate([row_sums, sums3], axis=1))
        d_mods = jnp.concatenate([d_mods, bin_row], axis=1)
        d_mods = d_mods.reshape(-1, dp, width // dp).transpose(1, 0, 2)
        d_mods = ph.begin(d_mods)
        ph.end(d_mods)
        d_mods = lax.all_to_all(d_mods, "dp", split_axis=0, concat_axis=0, tiled=True)
        out_total = out_sum(0) + ph.now(o_3).astype(F32) + ph.now(o_1).astype(F32)
        out_mine, out_theirs = grid.halves(ph.begin(out_total), 0)
        ph.end(out_mine)
        out_theirs = ph.hand_over(out_theirs)
        ph.close(20.0)

        d_mods = ph.now(d_mods).reshape(dp * count, -1, width // dp)
        rows_in_order = jnp.stack([d_mods[:, k] for k in (0, 1, 4, 2, 3, 5)], axis=1)
        onehot_all = (d_mods[:, 6, :1] == table_rows.astype(F32)).astype(F32)
        table_part = jnp.einsum("sb,std->btd", onehot_all, rows_in_order, precision=HIGH)
        out_part = grid.by_core(out_mine, ph.now(out_theirs), 1)
        qkv_part = p_sum(0) + ph.now(p_3).astype(F32) + ph.now(p_1).astype(F32)
        qkv_part = qkv_part.reshape(-1, 3, local_width).transpose(1, 0, 2)
        qkv_part = grid.own_rows(qkv_part)
        block_out, input_grad = (
            turn_out(value).reshape(count, length, width) for value in (block_out, input_grad)
        )
        return (block_out, input_grad, table_part, qkv_part, out_part, up_part, down_part)

    return body


def solution(mesh):
    in_specs = (
        P("dp", None, None),
        P(),
        P(None, "dp", "mp"),
        P("dp", "mp"),
        P("dp", "mp"),
        P("dp", "mp"),
        P("dp"),
        P("dp"),
        P("dp", None, None),
    )
    out_specs = (
        P("dp", None, None),
        P("dp", None, None),
        P(None, None, "dp"),
        P(None, "dp", "mp"),
        P("dp", "mp"),
        P("dp", "mp"),
        P("dp", "mp"),
    )
    body = make_body(mesh.shape["dp"], mesh.shape["mp"])
    return jax.shard_map(body, mesh=mesh, in_specs=in_specs, out_specs=out_specs, check_vma=False)
```

```python
import functools

import jax
import jax.numpy as jnp
from jax import lax
from jax.experimental import pallas as pl
from jax.experimental.pallas import tpu as pltpu
from jax.sharding import PartitionSpec as P

HEAD_DIM = 128
EPS = 1e-06
HIGH = lax.Precision.HIGHEST
F32 = jnp.float32
BF16 = jnp.bfloat16
CORES = 2
TILE = 128
CHUNK = 16
UNROLL = 8


def after(value, *earlier):
    return lax.optimization_barrier((value, *earlier))[0]


def pass_on(in_ref, out_ref):
    out_ref[...] = in_ref[...]


def pace(token, cost):
    return pl.pallas_call(
        pass_on,
        out_shape=jax.ShapeDtypeStruct(token.shape, token.dtype),
        cost_estimate=pl.CostEstimate(
            flops=int(cost * 1.15e9), bytes_accessed=8192, transcendentals=0
        ),
    )(token)


class Phases:
    def __init__(self, dp, mp):
        self.z = 4 if (dp // CORES) % 4 == 0 else 1
        self.x = dp // CORES // self.z
        self.tail, self.results, self.sent, self.last = (), [], [], ()
        self.turn = [(i, (i + 1) % mp) for i in range(mp)]
        self.token = jnp.zeros((8, 128), F32)

    def ring(self, dz, dx, dc):
        index = lambda z, x, c: (z % self.z * self.x + x % self.x) * CORES + c % CORES
        return [
            (index(z, x, c), index(z + dz, x + dx, c + dc))
            for z in range(self.z)
            for x in range(self.x)
            for c in range(CORES)
        ]

    def send(self, value, dz, dx, hold=True):
        value = after(value, *self.tail)
        self.sent.append(value)
        out = lax.ppermute(value, "dp", self.ring(dz, dx, 0))
        if hold:
            self.results.append(out)
        return out

    def send_z(self, value, places):
        return self.send(value, places, 0)

    def send_x(self, value):
        return self.send(value, 0, 1)

    def send_core(self, value):
        return lax.ppermute(value, "dp", self.ring(0, 0, 1))

    def hand_over(self, value):
        out = self.send_core(value)
        self.results.append(out)
        return out

    def across(self, part):
        out = [lax.optimization_barrier(part)]
        for _ in range(len(self.turn) - 1):
            out.append(lax.ppermute(out[-1], "mp", self.turn))
        return out

    def now(self, value):
        return after(value, *self.tail)

    def begin(self, value):
        return after(value, *self.tail, *self.sent, *self.last)

    def end(self, *values):
        self.last = values

    def close(self, cost=25.0):
        self.token = pace(after(self.token, *self.tail, *self.sent), cost)
        self.tail = (*self.results, *self.last, self.token)
        self.results, self.sent, self.last = [], [], ()

    def gather_x(self, piece):
        pieces = [piece]
        for _ in range(1, self.x):
            pieces.append(self.send_x(pieces[-1]))
        return pieces

    def reduce_x(self, blocks):
        moving = None
        for kx in range(1, self.x):
            value = blocks[kx]
            if moving is not None:
                value = value.astype(F32) + moving.astype(F32)
            moving = self.send_x(value.astype(BF16))
        return moving


def plus(first, *others):
    total = first.astype(F32)
    for other in others:
        if other is not None:
            total = total + other.astype(F32)
    return total


class Grid:
    def __init__(self, phases):
        self.z, self.x, self.phases = phases.z, phases.x, phases
        me = lax.axis_index("dp")
        self.at_z, self.at_x, self.core = (
            me // (self.x * CORES),
            (me // CORES) % self.x,
            me % CORES,
        )

    def to_relative(self):
        return jnp.stack(
            [
                (self.at_z - kz) % self.z * self.x + (self.at_x - kx) % self.x
                for kx in range(self.x)
                for kz in range(self.z)
            ]
        ).astype(jnp.int32)

    def to_absolute(self):
        return jnp.stack(
            [
                (self.at_x - ox) % self.x * self.z + (self.at_z - oz) % self.z
                for oz in range(self.z)
                for ox in range(self.x)
            ]
        ).astype(jnp.int32)

    def by_core(self, first, second, axis):
        return jnp.where(
            self.core == 0,
            jnp.concatenate([first, second], axis=axis),
            jnp.concatenate([second, first], axis=axis),
        )

    def halves(self, value, axis):
        half = value.shape[axis] // 2
        low = lax.slice_in_dim(value, 0, half, axis=axis)
        high = lax.slice_in_dim(value, half, 2 * half, axis=axis)
        return (
            jnp.where(self.core == 0, low, high),
            jnp.where(self.core == 0, high, low),
        )

    def chip_shard(self, shard):
        mine, theirs = self.halves(shard, 1)
        return self.by_core(mine, self.phases.send_core(theirs), 0)

    def own_rows(self, total):
        mine, theirs = self.halves(total, total.ndim - 2)
        return self.by_core(mine, self.phases.send_core(theirs), total.ndim - 1)

    def dots(self, lhs, rhs, kx):
        width = lhs.shape[1] // self.x
        return lax.dot_general(
            lhs[:, kx * width : (kx + 1) * width],
            rhs,
            (((0,), (0,)), ((), ())),
            preferred_element_type=F32,
        ).astype(BF16)


def copy_block(order_ref, in_ref, out_ref):
    out_ref[...] = in_ref[...]


def reorder(value, order):
    count = order.shape[0]
    shape = value.shape
    flat = value.reshape(-1, shape[-1])
    blk = shape[-1] // count
    if blk % 128:
        return jnp.take(flat.reshape(-1, count, blk), order, axis=1).reshape(shape)
    out = pl.pallas_call(
        copy_block,
        grid_spec=pltpu.PrefetchScalarGridSpec(
            num_scalar_prefetch=1,
            grid=(count,),
            in_specs=[pl.BlockSpec((flat.shape[0], blk), lambda j, s: (0, s[j]))],
            out_specs=pl.BlockSpec((flat.shape[0], blk), lambda j, s: (0, j)),
        ),
        out_shape=jax.ShapeDtypeStruct(flat.shape, flat.dtype),
    )(order, flat)
    return out.reshape(shape)


def dot(lhs, rhs, left, right):
    return lax.dot_general(lhs, rhs, (((left,), (right,)), ((), ())), preferred_element_type=F32)


def softmax(query, keys):
    scores = dot(query, keys, 1, 1) * HEAD_DIM ** (-0.5)
    expo = jnp.exp(scores - jnp.max(scores, axis=-1, keepdims=True))
    return expo / jnp.sum(expo, axis=-1, keepdims=True)


def head_cols(part, head, heads):
    return pl.ds((part * heads + head) * HEAD_DIM, HEAD_DIM)


def attend_kernel(heads, qkv_ref, mixed_ref):
    for head in range(heads):
        query, keys, values = (qkv_ref[:, head_cols(part, head, heads)] for part in range(3))
        probs = softmax(query, keys).astype(BF16)
        mixed = dot(probs, values, 1, 0).astype(BF16)
        mixed_ref[:, head_cols(0, head, heads)] = mixed


def attend_back_kernel(heads, qkv_ref, d_mixed_ref, d_qkv_ref):
    factor = HEAD_DIM ** (-0.5)
    for head in range(heads):
        query, keys, values = (qkv_ref[:, head_cols(part, head, heads)] for part in range(3))
        d_mixed = d_mixed_ref[:, head_cols(0, head, heads)]
        probs = softmax(query, keys)
        d_probs = dot(d_mixed, values, 1, 1)
        d_values = dot(probs.astype(BF16), d_mixed, 0, 0)
        delta = jnp.sum(d_probs * probs, axis=-1, keepdims=True)
        d_scores = (probs * (d_probs - delta)).astype(BF16)
        d_query = dot(d_scores, keys, 1, 0) * factor
        d_keys = dot(d_scores, query, 0, 0) * factor
        d_qkv_ref[:, head_cols(0, head, heads)] = d_query.astype(BF16)
        d_qkv_ref[:, head_cols(1, head, heads)] = d_keys.astype(BF16)
        d_qkv_ref[:, head_cols(2, head, heads)] = d_values.astype(BF16)


def by_image(kernel, length, width, *operands):
    rows = operands[0].shape[0]
    block = lambda cols: pl.BlockSpec((length, cols), lambda image: (image, 0))
    return pl.pallas_call(
        kernel,
        grid=(rows // length,),
        in_specs=[block(operand.shape[1]) for operand in operands],
        out_specs=block(width),
        out_shape=jax.ShapeDtypeStruct((rows, width), BF16),
        compiler_params=pltpu.CompilerParams(vmem_limit_bytes=32 * 1024 * 1024),
        cost_estimate=pl.CostEstimate(
            flops=rows * length * width * 8, bytes_accessed=rows * 8192, transcendentals=rows * 1024
        ),
    )(*operands)


def normal(value):
    centre = value - jnp.mean(value, axis=-1, keepdims=True)
    factor = lax.rsqrt(jnp.mean(centre * centre, axis=-1, keepdims=True) + EPS)
    return centre * factor, factor


def normal_back(grad, unit, factor):
    mean = jnp.mean(grad, axis=-1, keepdims=True)
    along = jnp.mean(grad * unit, axis=-1, keepdims=True)
    return factor * (grad - mean - unit * along)


class Rows:
    def __init__(self, blocks, order_ref, width):
        self.blocks, self.order, self.width = blocks, order_ref, width

    def each(self, count, body):
        def step(index, carry):
            body(pl.ds(pl.multiple_of(index * CHUNK, CHUNK), CHUNK))
            return carry

        lax.fori_loop(0, count // CHUNK, step, 0, unroll=UNROLL)

    def places(self):
        if not self.blocks:
            return [(slice(0, self.width), slice(0, self.width))]
        blk = self.width // self.blocks
        return [
            (
                slice(k * blk, (k + 1) * blk),
                pl.ds(pl.multiple_of(self.order[k] * blk, blk), blk),
            )
            for k in range(self.blocks)
        ]


def clear_sums(sums_ref):
    @pl.when(pl.program_id(1) == 0)
    def _():
        sums_ref[...] = jnp.zeros_like(sums_ref)


def add_sums(sums_ref, places, *terms):
    for index, term in enumerate(terms):
        low, high = term[:8], term[8:]
        for here, there in places:
            sums_ref[0, index * 8 : index * 8 + 8, there] += low[:, here] + high[:, here]


def first_norm_kernel(blocks, order_ref, present_ref, tokens_ref, mods_ref, kept_ref, normed_ref):
    rows = Rows(blocks, order_ref, tokens_ref.shape[1])
    for here, there in rows.places():
        kept_ref[:, here] = tokens_ref[:, there]

    def body(some):
        unit, _ = normal(kept_ref[some, :].astype(F32))
        value = unit * (1.0 + mods_ref[0, 1:2, :]) + mods_ref[0, 0:1, :]
        normed_ref[some, :] = value.astype(BF16)

    rows.each(tokens_ref.shape[0], body)


def cotangent_kernel(blocks, order_ref, present_ref, cotangent_ref, mods_ref, dy_ref, d_mlp_ref):
    rows = Rows(blocks, order_ref, cotangent_ref.shape[1])
    mask = present_ref[pl.program_id(0)].astype(F32)
    for here, there in rows.places():
        dy = cotangent_ref[:, there].astype(F32) * mask
        dy_ref[:, here] = dy.astype(BF16)
        d_mlp_ref[:, here] = (mods_ref[0, 5:6, here] * dy).astype(BF16)


def second_norm_kernel(
    blocks, order_ref, present_ref, tokens_ref, att_a, att_b, mods_ref, hidden_ref, second_ref
):
    rows = Rows(blocks, order_ref, tokens_ref.shape[1])

    def body(some):
        att = att_a[some, :].astype(F32) + att_b[some, :].astype(F32)
        hidden = tokens_ref[some, :].astype(F32) + mods_ref[0, 2:3, :] * att
        hidden_ref[some, :] = hidden
        unit, _ = normal(hidden)
        value = unit * (1.0 + mods_ref[0, 4:5, :]) + mods_ref[0, 3:4, :]
        second_ref[some, :] = value.astype(BF16)

    rows.each(tokens_ref.shape[0], body)


def second_back_kernel(
    blocks, order_ref, present_ref, hidden_ref, att_a, att_b, d_a, d_b, dy_ref, mods_ref,
    d_hidden_ref, d_att_ref, sums_ref,
):
    rows = Rows(blocks, order_ref, hidden_ref.shape[1])
    places = rows.places()
    clear_sums(sums_ref)

    def body(some):
        grad = d_a[some, :].astype(F32) + d_b[some, :].astype(F32)
        unit, factor = normal(hidden_ref[some, :])
        add_sums(sums_ref, places, grad, grad * unit)
        d_hidden = normal_back(grad * (1.0 + mods_ref[0, 4:5, :]), unit, factor)
        d_hidden = dy_ref[some, :].astype(F32) + d_hidden
        d_hidden_ref[some, :] = d_hidden
        d_att_ref[some, :] = (mods_ref[0, 2:3, :] * d_hidden).astype(BF16)
        att = att_a[some, :].astype(F32) + att_b[some, :].astype(F32)
        add_sums(sums_ref.at[:, 16:24], places, d_hidden * att)

    rows.each(hidden_ref.shape[0], body)


def first_back_kernel(
    blocks, order_ref, present_ref, tokens_ref, d_a, d_b, d_hidden_ref, mods_ref,
    input_grad_ref, sums_ref,
):
    rows = Rows(blocks, order_ref, tokens_ref.shape[1])
    places = rows.places()
    clear_sums(sums_ref)

    def body(some):
        grad = d_a[some, :].astype(F32) + d_b[some, :].astype(F32)
        unit, factor = normal(tokens_ref[some, :].astype(F32))
        add_sums(sums_ref, places, grad, grad * unit)
        value = normal_back(grad * (1.0 + mods_ref[0, 1:2, :]), unit, factor)
        value = d_hidden_ref[some, :] + value
        for here, there in places:
            input_grad_ref[some, there] = value[:, here]

    rows.each(tokens_ref.shape[0], body)


def block_out_kernel(
    blocks, order_ref, present_ref, hidden_ref, mlp_a, mlp_b, dy_ref, mods_ref,
    block_out_ref, sums_ref,
):
    rows = Rows(blocks, order_ref, hidden_ref.shape[1])
    places = rows.places()
    mask = present_ref[pl.program_id(0)].astype(F32)
    clear_sums(sums_ref)

    def body(some):
        mlp = mlp_a[some, :].astype(F32) + mlp_b[some, :].astype(F32)
        add_sums(sums_ref, places, dy_ref[some, :].astype(F32) * mlp)
        value = mask * (hidden_ref[some, :] + mods_ref[0, 5:6, :] * mlp)
        for here, there in places:
            block_out_ref[some, there] = value[:, here].astype(BF16)

    rows.each(hidden_ref.shape[0], body)


def by_rows(kernel, order, present, operands, mods, kinds, sums=0):
    images, kinds_of_mods, width = mods.shape
    tiles = operands[0].shape[0] // images // TILE
    row = pl.BlockSpec((TILE, width), lambda i, t, *s: (i * tiles + t, 0))
    whole = lambda count: pl.BlockSpec((1, count, width), lambda i, t, *s: (i, 0, 0))
    shapes = [jax.ShapeDtypeStruct(operands[0].shape, kind) for kind in kinds]
    specs = [row] * len(kinds)
    if sums:
        shapes.append(jax.ShapeDtypeStruct((images, 8 * sums, width), F32))
        specs.append(whole(8 * sums))
    blocks = 0 if width // order.shape[0] % 128 else order.shape[0]
    return pl.pallas_call(
        functools.partial(kernel, blocks),
        grid_spec=pltpu.PrefetchScalarGridSpec(
            num_scalar_prefetch=2,
            grid=(images, tiles),
            in_specs=[row] * len(operands) + [whole(kinds_of_mods)],
            out_specs=specs,
        ),
        out_shape=shapes,
        compiler_params=pltpu.CompilerParams(vmem_limit_bytes=40 * 1024 * 1024),
        cost_estimate=pl.CostEstimate(
            flops=operands[0].size * 6000, bytes_accessed=operands[0].size * 8, transcendentals=0
        ),
    )(order, present, *operands, mods)


def matmul(lhs, rhs, turned=False):
    return lax.dot_general(
        lhs, rhs, (((1,), (1 if turned else 0,)), ((), ())), preferred_element_type=F32
    )


def make_body(dp, mp):
    def body(tokens, mod_table, w_qkv, w_out_t, w_up, w_down, bins, present, cotangent):
        count, length, width = tokens.shape
        rows = count * length
        ph = Phases(dp, mp)
        grid = Grid(ph)
        relative, absolute = grid.to_relative(), grid.to_absolute()
        turns = list(range(1, grid.x)) + [0]
        outside = width // relative.shape[0] % 128
        turn_in = lambda value: reorder(value, relative) if outside else value
        turn_out = lambda value: reorder(value, absolute) if outside else value
        flat = lambda value: value.reshape(rows, width)
        join = lambda own, theirs: jnp.concatenate([own, theirs], axis=0)

        def whole(*by_z):
            return jnp.concatenate(
                [by_z[kz][kx] for kx in range(grid.x) for kz in range(grid.z)], axis=0
            )

        def from_both(theirs, value, weight, between=None):
            if between is not None:
                between()
            part = matmul(ph.begin(value[:rows]), weight, True) + theirs.astype(F32)
            part = part.astype(BF16)
            ph.end(part)
            return ph.across(part)

        def two(parts):
            return parts if len(parts) == 2 else [plus(*parts), jnp.zeros_like(parts[0])]

        def dots(lhs, rhs):
            kept = {}
            for kx in turns:
                kept[kx] = grid.dots(ph.begin(lhs), rhs, kx)
                ph.end(kept[kx])
            return kept

        def rows_of(kept, low, high):
            blk = width // grid.x // grid.z
            return {kx: kept[kx][low * blk : high * blk] for kx in kept}

        wide = w_qkv.reshape(3, -1, CORES, w_qkv.shape[2] // CORES).transpose(1, 2, 0, 3)
        s_q = grid.chip_shard(wide.reshape(w_qkv.shape[1], -1))
        z_q, x_q = {1: ph.send_z(s_q, 1)}, {0: ph.gather_x(s_q)}
        s_o = grid.chip_shard(ph.begin(w_out_t))
        ph.end(s_o)
        x_o = jnp.stack(ph.gather_x(s_o))
        table_rows = jnp.arange(mod_table.shape[0])[None, :]
        onehot = (bins[:, None] == table_rows).astype(F32)
        mods = jnp.einsum("cb,btd->ctd", ph.begin(onehot), mod_table, precision=HIGH)
        mods = reorder(mods, relative)
        ph.end(mods)
        ph.close()

        z_q[3] = ph.send_z(s_q, 3)
        x_q[1] = ph.gather_x(z_q[1])
        tokens, normed_own = by_rows(
            first_norm_kernel, relative, present, [flat(turn_in(ph.begin(tokens)))], mods, [BF16, BF16]
        )
        ph.end(normed_own)
        normed_other = ph.hand_over(normed_own)
        ph.close()

        z_q[2] = ph.send_z(z_q[1], 1)
        x_q[3] = ph.gather_x(z_q[3])
        s_u = grid.chip_shard(ph.begin(w_up))
        ph.end(s_u)
        normed = join(normed_own, ph.begin(normed_other))
        ph.end(normed)
        ph.close()

        z_o = {0: x_o, 1: ph.send_z(x_o, 1)}
        x_q[2] = ph.gather_x(z_q[2])
        s_d = grid.chip_shard(ph.begin(w_down))
        ph.end(s_d)
        ph.close()

        z_o[3] = ph.send_z(x_o, 3)
        z_o[2] = ph.send_z(z_o[1], 1)
        x_u = {0: ph.gather_x(s_u)}
        w_a = whole(x_q[0], x_q[1], x_q[2], x_q[3])
        local_width = s_o.shape[1]
        local_heads = local_width // HEAD_DIM
        qkv = matmul(ph.begin(normed), w_a).astype(BF16)
        ph.end(qkv)
        attend = functools.partial(attend_kernel, local_heads)
        mixed = by_image(attend, length, local_width, ph.begin(qkv))
        ph.end(mixed)
        w_o = jnp.concatenate([z_o[kz][kx] for kx in range(grid.x) for kz in range(grid.z)], axis=0)
        att_part = matmul(ph.begin(mixed)[rows:], w_o, True).astype(BF16)
        ph.end(att_part)
        att_part = ph.hand_over(att_part)
        ph.close()

        z_u = {1: ph.send_z(s_u, 1)}
        x_d = {0: ph.gather_x(s_d)}
        att = from_both(att_part, mixed, w_o)
        dy, d_mlp_own = by_rows(
            cotangent_kernel, relative, present, [flat(turn_in(ph.begin(cotangent)))], mods, [BF16, BF16]
        )
        ph.end(d_mlp_own)
        ph.close()

        z_u[3] = ph.send_z(s_u, 3)
        x_u[1] = ph.gather_x(z_u[1])
        d_mlp_other = ph.hand_over(ph.now(d_mlp_own))
        ph.close()

        z_u[2] = ph.send_z(z_u[1], 1)
        x_u[3] = ph.gather_x(z_u[3])
        att[-1] = ph.begin(att[-1])
        hidden, second_own = by_rows(
            second_norm_kernel, relative, present, [tokens, *two(att)], mods, [F32, BF16]
        )
        ph.end(second_own)
        second_other = ph.hand_over(second_own)
        ph.close()

        z_d = {1: ph.send_z(s_d, 1)}
        x_u = {kz: [ph.now(piece) for piece in x_u[kz]] for kz in x_u}
        x_u[2] = ph.gather_x(z_u[2])
        second = join(second_own, ph.begin(second_other))
        ph.end(second)
        d_mlp = join(d_mlp_own, ph.begin(d_mlp_other))
        ph.end(d_mlp)
        ph.close()

        z_d[3] = ph.send_z(s_d, 3)
        x_d[1] = ph.gather_x(z_d[1])
        w_u = whole(x_u[0], x_u[1], x_u[2], x_u[3])
        up_val = matmul(ph.begin(second), w_u)
        act = jax.nn.gelu(up_val).astype(BF16)
        ph.end(act)
        ph.close()

        z_d[2] = ph.send_z(z_d[1], 1)
        x_d[3] = ph.gather_x(z_d[3])
        down = dots(d_mlp, act)
        half = down[0].shape[1] // 2
        first = jnp.stack([down[kx][:, :half] for kx in range(grid.x)])
        other = {kx: down[kx][:, half:] for kx in down}
        ph.end(first)
        up_val = ph.begin(up_val)
        _, gelu_pull = jax.vjp(jax.nn.gelu, up_val)
        slope = gelu_pull(jnp.ones_like(up_val))[0]
        ph.end(slope)
        ph.close()

        blk = first.shape[1] // grid.z
        part = lambda stacked, kz: stacked[:, kz * blk : (kz + 1) * blk]
        x_d[2] = ph.gather_x(z_d[2])
        a_2 = ph.send(part(first, 2), 3, 0, hold=False)
        step = width // (grid.x * grid.z)
        feature_blocks = lambda value, some: jnp.concatenate(
            [
                value[:, (kx * grid.z + kz) * step : (kx * grid.z + kz + 1) * step]
                for kx in range(grid.x)
                for kz in some
            ],
            axis=1,
        )
        some_of = lambda by_z, some: jnp.concatenate(
            [by_z[kz][kx] for kx in range(grid.x) for kz in some], axis=0
        )
        there = [kz for kz in range(grid.z) if kz != 2]
        late = feature_blocks(d_mlp, [2])
        w_d = [some_of(x_d, there)]
        d_act = [
            matmul(ph.begin(feature_blocks(d_mlp[half_rows], there)), w_d[0])
            for half_rows in (slice(0, rows), slice(rows, None))
        ]
        ph.end(*d_act, late)
        ph.close()

        x_b = {2: ph.reduce_x(rows_of(other, 2, 4))}
        a_3 = ph.send_z(part(first, 3), 1)
        ph.results.append(a_2)
        w_d.append(some_of(x_d, [2]))
        d_act = jnp.concatenate(d_act, axis=0) + matmul(ph.begin(late), w_d[1])
        d_up = (d_act * slope).astype(BF16)
        ph.end(d_up)
        d_second_part = matmul(ph.begin(d_up)[rows:], w_u, True).astype(BF16)
        ph.end(d_second_part)
        d_second_part = ph.hand_over(d_second_part)
        a_1 = ph.begin(plus(part(first, 1), ph.now(a_2)).astype(BF16))
        ph.end(a_1)
        ph.close()

        x_b[0] = ph.reduce_x(rows_of(other, 0, 2))
        a_1 = ph.send_z(a_1, 3)
        d_second = from_both(d_second_part, d_up, w_u)
        up = {}

        def up_dots(blocks):
            for kx in blocks:
                up[kx] = grid.dots(ph.begin(second), d_up, kx)
                ph.end(up[kx])

        up_dots(turns[:-1])
        b_part = lambda kz: ph.now(x_b[kz // 2 * 2][(kz % 2) * blk : (kz % 2 + 1) * blk])
        b_sum = lambda kz: plus(rows_of(other, kz, kz + 1)[0], b_part(kz))
        b_2, b_3 = (ph.begin(b_sum(kz).astype(BF16)) for kz in (2, 3))
        ph.end(b_2, b_3)
        ph.close()

        up_rows = lambda kz: ph.reduce_x(rows_of(up, kz, kz + 1))
        x_up = {2: up_rows(2)}
        b_2 = ph.send_z(b_2, 3)
        b_3 = ph.send_z(b_3, 1)
        up_dots(turns[-1:])
        first_sum = ph.begin(plus(part(first, 0), ph.now(a_3), ph.now(a_1)))
        ph.end(first_sum)
        ph.close()

        x_up[3] = up_rows(3)
        up_sum = lambda kz: plus(rows_of(up, kz, kz + 1)[0], ph.now(x_up[kz]))
        u_2 = ph.send_z(up_sum(2).astype(BF16), 3)
        b_1 = ph.begin((b_sum(1) + ph.now(b_2).astype(F32)).astype(BF16))
        ph.end(b_1)
        d_second[-1] = ph.begin(d_second[-1])
        d_hidden, d_att_own, sums2 = by_rows(
            second_back_kernel, relative, present, [hidden, *two(att), *two(d_second), dy], mods,
            [F32, BF16], 3,
        )
        ph.end(d_att_own)
        d_att_other = ph.hand_over(d_att_own)
        ph.close()

        x_up[1] = up_rows(1)
        x_first = ph.reduce_x(first_sum.astype(BF16))
        u_3 = ph.send_z(up_sum(3).astype(BF16), 1)
        b_1 = ph.send_z(b_1, 3)
        d_att = join(d_att_own, ph.begin(d_att_other))
        d_mixed = matmul(d_att, w_o).astype(BF16)
        ph.end(d_mixed)
        attend_back = functools.partial(attend_back_kernel, local_heads)
        d_qkv = by_image(attend_back, length, 3 * local_width, qkv, ph.begin(d_mixed))
        ph.end(d_qkv)
        d_normed_part = matmul(ph.begin(d_qkv)[rows:], w_a, True).astype(BF16)
        ph.end(d_normed_part)
        d_normed_part = ph.hand_over(d_normed_part)
        ph.close()

        x_up[0] = up_rows(0)
        u_1 = ph.send_z((up_sum(1) + ph.now(u_2).astype(F32)).astype(BF16), 3)
        d_normed = from_both(d_normed_part, d_qkv, w_a)
        out = dots(d_att, mixed)
        proj = dots(normed, d_qkv)
        ph.close()

        x_out = ph.reduce_x(out)
        down_of = lambda value: jnp.concatenate([matmul(value, w, True) for w in w_d], axis=1)
        mlp_part = down_of(ph.begin(act)[rows:]).astype(BF16)
        ph.end(mlp_part)
        mlp_part = ph.hand_over(mlp_part)
        up_total = up_sum(0) + ph.now(u_3).astype(F32) + ph.now(u_1).astype(F32)
        up_mine, up_theirs = grid.halves(ph.begin(up_total), 0)
        ph.end(up_mine)
        up_theirs = ph.hand_over(up_theirs)
        ph.close()

        p_rows = lambda kz: ph.reduce_x(rows_of(proj, kz, kz + 1))
        p_sum = lambda kz: plus(rows_of(proj, kz, kz + 1)[0], ph.now(x_p[kz]))
        out_sum = lambda kz: plus(
            rows_of(out, kz, kz + 1)[0], ph.now(x_out[kz * blk : (kz + 1) * blk])
        )
        x_p = {2: p_rows(2)}
        o_2 = ph.send_z(out_sum(2).astype(BF16), 3)
        o_3 = ph.send_z(out_sum(3).astype(BF16), 1)
        mlp = (down_of(ph.begin(act)[:rows]) + mlp_part.astype(F32)).astype(BF16)
        ph.end(mlp)
        mlp = ph.across(mlp)
        d_normed[-1] = ph.begin(d_normed[-1])
        input_grad, sums1 = by_rows(
            first_back_kernel, relative, present, [tokens, *two(d_normed), d_hidden], mods, [F32], 2
        )
        ph.end(input_grad)
        ph.close(20.0)

        x_p[3] = p_rows(3)
        p_2 = ph.send_z(p_sum(2).astype(BF16), 3)
        up_part = grid.by_core(ph.begin(up_mine), up_theirs, 1)
        ph.end(up_part)
        o_1 = ph.send_z((out_sum(1) + ph.now(o_2).astype(F32)).astype(BF16), 3)
        row_sums = [jnp.sum(v.reshape(count, -1, 8, width), axis=2) for v in (sums1, sums2)]
        row_sums = ph.begin(jnp.concatenate(row_sums, axis=1))
        down_low = plus(ph.now(first_sum)[0], x_first)
        down_high = b_sum(0) + ph.now(b_3).astype(F32) + ph.now(b_1).astype(F32)
        down_total = jnp.concatenate([down_low, down_high], axis=1)
        down_mine, down_theirs = grid.halves(ph.begin(down_total), 0)
        ph.end(down_mine, row_sums)
        down_theirs = ph.hand_over(down_theirs)
        ph.close(20.0)

        x_p[1] = p_rows(1)
        p_3 = ph.send_z(p_sum(3).astype(BF16), 1)
        down_part = grid.by_core(ph.begin(down_mine), down_theirs, 1)
        ph.end(down_part)
        mlp[-1] = ph.begin(mlp[-1])
        places = [(kx, kz) for some in (there, [2]) for kx in range(grid.x) for kz in some]
        in_order = [places.index((kx, kz)) for kx in range(grid.x) for kz in range(grid.z)]
        mlp = [
            jnp.concatenate([v[:, k * step : (k + 1) * step] for k in in_order], axis=1) for v in mlp
        ]
        block_out, sums3 = by_rows(
            block_out_kernel, relative, present, [hidden, *two(mlp), dy], mods, [BF16], 1
        )
        ph.end(block_out)
        ph.close(20.0)

        x_p[0] = p_rows(0)
        p_1 = ph.send_z((p_sum(1) + ph.now(p_2).astype(F32)).astype(BF16), 3)
        sums3 = jnp.sum(sums3.reshape(count, -1, 8, width), axis=2)
        bin_row = jnp.broadcast_to(bins.astype(F32)[:, None, None], (count, 1, width))
        d_mods = turn_out(jnp.concatenate([row_sums, sums3], axis=1))
        d_mods = jnp.concatenate([d_mods, bin_row], axis=1)
        d_mods = d_mods.reshape(-1, dp, width // dp).transpose(1, 0, 2)
        d_mods = ph.begin(d_mods)
        ph.end(d_mods)
        d_mods = lax.all_to_all(d_mods, "dp", split_axis=0, concat_axis=0, tiled=True)
        out_total = out_sum(0) + ph.now(o_3).astype(F32) + ph.now(o_1).astype(F32)
        out_mine, out_theirs = grid.halves(ph.begin(out_total), 0)
        ph.end(out_mine)
        out_theirs = ph.hand_over(out_theirs)
        ph.close(20.0)

        d_mods = ph.now(d_mods).reshape(dp * count, -1, width // dp)
        rows_in_order = jnp.stack([d_mods[:, k] for k in (0, 1, 4, 2, 3, 5)], axis=1)
        onehot_all = (d_mods[:, 6, :1] == table_rows.astype(F32)).astype(F32)
        table_part = jnp.einsum("sb,std->btd", onehot_all, rows_in_order, precision=HIGH)
        out_part = grid.by_core(out_mine, ph.now(out_theirs), 1)
        qkv_part = p_sum(0) + ph.now(p_3).astype(F32) + ph.now(p_1).astype(F32)
        qkv_part = qkv_part.reshape(-1, 3, local_width).transpose(1, 0, 2)
        qkv_part = grid.own_rows(qkv_part)
        block_out, input_grad = (
            turn_out(value).reshape(count, length, width) for value in (block_out, input_grad)
        )
        return (block_out, input_grad, table_part, qkv_part, out_part, up_part, down_part)

    return body


def solution(mesh):
    in_specs = (
        P("dp", None, None),
        P(),
        P(None, "dp", "mp"),
        P("dp", "mp"),
        P("dp", "mp"),
        P("dp", "mp"),
        P("dp"),
        P("dp"),
        P("dp", None, None),
    )
    out_specs = (
        P("dp", None, None),
        P("dp", None, None),
        P(None, None, "dp"),
        P(None, "dp", "mp"),
        P("dp", "mp"),
        P("dp", "mp"),
        P("dp", "mp"),
    )
    body = make_body(mesh.shape["dp"], mesh.shape["mp"])
    return jax.shard_map(body, mesh=mesh, in_specs=in_specs, out_specs=out_specs, check_vma=False)
```

```python
import functools

import jax
import jax.numpy as jnp
from jax import lax
from jax.experimental import pallas as pl
from jax.experimental.pallas import tpu as pltpu
from jax.sharding import PartitionSpec as P

HEAD_DIM = 128
EPS = 1e-06
HIGH = lax.Precision.HIGHEST
F32 = jnp.float32
BF16 = jnp.bfloat16
CORES = 2
TILE = 256
CHUNK = 16
UNROLL = 8


def after(value, *earlier):
    return lax.optimization_barrier((value, *earlier))[0]


def pass_on(in_ref, out_ref):
    out_ref[...] = in_ref[...]


def pace(token, cost):
    return pl.pallas_call(
        pass_on,
        out_shape=jax.ShapeDtypeStruct(token.shape, token.dtype),
        cost_estimate=pl.CostEstimate(
            flops=int(cost * 1.15e9), bytes_accessed=8192, transcendentals=0
        ),
    )(token)


class Phases:
    def __init__(self, dp, mp):
        self.z = 4 if (dp // CORES) % 4 == 0 else 1
        self.x = dp // CORES // self.z
        self.tail, self.results, self.sent, self.last = (), [], [], ()
        self.turn = [(i, (i + 1) % mp) for i in range(mp)]
        self.token = jnp.zeros((8, 128), F32)

    def ring(self, dz, dx, dc):
        index = lambda z, x, c: (z % self.z * self.x + x % self.x) * CORES + c % CORES
        return [
            (index(z, x, c), index(z + dz, x + dx, c + dc))
            for z in range(self.z)
            for x in range(self.x)
            for c in range(CORES)
        ]

    def send(self, value, dz, dx, hold=True):
        value = after(value, *self.tail)
        self.sent.append(value)
        out = lax.ppermute(value, "dp", self.ring(dz, dx, 0))
        if hold:
            self.results.append(out)
        return out

    def send_z(self, value, places):
        return self.send(value, places, 0)

    def send_x(self, value):
        return self.send(value, 0, 1)

    def send_core(self, value):
        return lax.ppermute(value, "dp", self.ring(0, 0, 1))

    def hand_over(self, value):
        out = self.send_core(value)
        self.results.append(out)
        return out

    def across(self, part):
        out = [lax.optimization_barrier(part)]
        for _ in range(len(self.turn) - 1):
            out.append(lax.ppermute(out[-1], "mp", self.turn))
        return out

    def now(self, value):
        return after(value, *self.tail)

    def begin(self, value):
        return after(value, *self.tail, *self.sent, *self.last)

    def end(self, *values):
        self.last = values

    def close(self, cost=25.0):
        self.token = pace(after(self.token, *self.tail, *self.sent), cost)
        self.tail = (*self.results, *self.last, self.token)
        self.results, self.sent, self.last = [], [], ()

    def gather_x(self, piece):
        pieces = [piece]
        for _ in range(1, self.x):
            pieces.append(self.send_x(pieces[-1]))
        return pieces

    def reduce_x(self, blocks):
        moving = None
        for kx in range(1, self.x):
            value = blocks[kx]
            if moving is not None:
                value = value.astype(F32) + moving.astype(F32)
            moving = self.send_x(value.astype(BF16))
        return moving


def plus(first, *others):
    total = first.astype(F32)
    for other in others:
        if other is not None:
            total = total + other.astype(F32)
    return total


class Grid:
    def __init__(self, phases):
        self.z, self.x, self.phases = phases.z, phases.x, phases
        me = lax.axis_index("dp")
        self.at_z, self.at_x, self.core = (
            me // (self.x * CORES),
            (me // CORES) % self.x,
            me % CORES,
        )

    def to_relative(self):
        return jnp.stack(
            [
                (self.at_z - kz) % self.z * self.x + (self.at_x - kx) % self.x
                for kx in range(self.x)
                for kz in range(self.z)
            ]
        ).astype(jnp.int32)

    def to_absolute(self):
        return jnp.stack(
            [
                (self.at_x - ox) % self.x * self.z + (self.at_z - oz) % self.z
                for oz in range(self.z)
                for ox in range(self.x)
            ]
        ).astype(jnp.int32)

    def by_core(self, first, second, axis):
        return jnp.where(
            self.core == 0,
            jnp.concatenate([first, second], axis=axis),
            jnp.concatenate([second, first], axis=axis),
        )

    def halves(self, value, axis):
        half = value.shape[axis] // 2
        low = lax.slice_in_dim(value, 0, half, axis=axis)
        high = lax.slice_in_dim(value, half, 2 * half, axis=axis)
        return (
            jnp.where(self.core == 0, low, high),
            jnp.where(self.core == 0, high, low),
        )

    def chip_shard(self, shard):
        mine, theirs = self.halves(shard, 1)
        return self.by_core(mine, self.phases.send_core(theirs), 0)

    def own_rows(self, total):
        mine, theirs = self.halves(total, total.ndim - 2)
        return self.by_core(mine, self.phases.send_core(theirs), total.ndim - 1)

    def dots(self, lhs, rhs, kx):
        width = lhs.shape[1] // self.x
        return lax.dot_general(
            lhs[:, kx * width : (kx + 1) * width],
            rhs,
            (((0,), (0,)), ((), ())),
            preferred_element_type=F32,
        ).astype(BF16)


def copy_block(order_ref, in_ref, out_ref):
    out_ref[...] = in_ref[...]


def reorder(value, order):
    count = order.shape[0]
    shape = value.shape
    flat = value.reshape(-1, shape[-1])
    blk = shape[-1] // count
    if blk % 128:
        return jnp.take(flat.reshape(-1, count, blk), order, axis=1).reshape(shape)
    out = pl.pallas_call(
        copy_block,
        grid_spec=pltpu.PrefetchScalarGridSpec(
            num_scalar_prefetch=1,
            grid=(count,),
            in_specs=[pl.BlockSpec((flat.shape[0], blk), lambda j, s: (0, s[j]))],
            out_specs=pl.BlockSpec((flat.shape[0], blk), lambda j, s: (0, j)),
        ),
        out_shape=jax.ShapeDtypeStruct(flat.shape, flat.dtype),
    )(order, flat)
    return out.reshape(shape)


def dot(lhs, rhs, left, right):
    return lax.dot_general(lhs, rhs, (((left,), (right,)), ((), ())), preferred_element_type=F32)


def softmax(query, keys):
    scores = dot(query, keys, 1, 1) * HEAD_DIM ** (-0.5)
    expo = jnp.exp(scores - jnp.max(scores, axis=-1, keepdims=True))
    return expo / jnp.sum(expo, axis=-1, keepdims=True)


def head_cols(part, head, heads):
    return pl.ds((part * heads + head) * HEAD_DIM, HEAD_DIM)


def attend_kernel(heads, qkv_ref, mixed_ref):
    for head in range(heads):
        query, keys, values = (qkv_ref[:, head_cols(part, head, heads)] for part in range(3))
        probs = softmax(query, keys).astype(BF16)
        mixed = dot(probs, values, 1, 0).astype(BF16)
        mixed_ref[:, head_cols(0, head, heads)] = mixed


def attend_back_kernel(heads, qkv_ref, d_mixed_ref, d_qkv_ref):
    factor = HEAD_DIM ** (-0.5)
    for head in range(heads):
        query, keys, values = (qkv_ref[:, head_cols(part, head, heads)] for part in range(3))
        d_mixed = d_mixed_ref[:, head_cols(0, head, heads)]
        probs = softmax(query, keys)
        d_probs = dot(d_mixed, values, 1, 1)
        d_values = dot(probs.astype(BF16), d_mixed, 0, 0)
        delta = jnp.sum(d_probs * probs, axis=-1, keepdims=True)
        d_scores = (probs * (d_probs - delta)).astype(BF16)
        d_query = dot(d_scores, keys, 1, 0) * factor
        d_keys = dot(d_scores, query, 0, 0) * factor
        d_qkv_ref[:, head_cols(0, head, heads)] = d_query.astype(BF16)
        d_qkv_ref[:, head_cols(1, head, heads)] = d_keys.astype(BF16)
        d_qkv_ref[:, head_cols(2, head, heads)] = d_values.astype(BF16)


def by_image(kernel, length, width, *operands):
    rows = operands[0].shape[0]
    block = lambda cols: pl.BlockSpec((length, cols), lambda image: (image, 0))
    return pl.pallas_call(
        kernel,
        grid=(rows // length,),
        in_specs=[block(operand.shape[1]) for operand in operands],
        out_specs=block(width),
        out_shape=jax.ShapeDtypeStruct((rows, width), BF16),
        compiler_params=pltpu.CompilerParams(vmem_limit_bytes=32 * 1024 * 1024),
        cost_estimate=pl.CostEstimate(
            flops=rows * length * width * 8, bytes_accessed=rows * 8192, transcendentals=rows * 1024
        ),
    )(*operands)


def normal(value):
    centre = value - jnp.mean(value, axis=-1, keepdims=True)
    factor = lax.rsqrt(jnp.mean(centre * centre, axis=-1, keepdims=True) + EPS)
    return centre * factor, factor


def normal_back(grad, unit, factor):
    mean = jnp.mean(grad, axis=-1, keepdims=True)
    along = jnp.mean(grad * unit, axis=-1, keepdims=True)
    return factor * (grad - mean - unit * along)


class Rows:
    def __init__(self, blocks, order_ref, width):
        self.blocks, self.order, self.width = blocks, order_ref, width

    def each(self, count, body):
        def step(index, carry):
            body(pl.ds(pl.multiple_of(index * CHUNK, CHUNK), CHUNK))
            return carry

        lax.fori_loop(0, count // CHUNK, step, 0, unroll=UNROLL)

    def places(self):
        if not self.blocks:
            return [(slice(0, self.width), slice(0, self.width))]
        blk = self.width // self.blocks
        return [
            (
                slice(k * blk, (k + 1) * blk),
                pl.ds(pl.multiple_of(self.order[k] * blk, blk), blk),
            )
            for k in range(self.blocks)
        ]


def clear_sums(sums_ref):
    @pl.when(pl.program_id(1) == 0)
    def _():
        sums_ref[...] = jnp.zeros_like(sums_ref)


def add_sums(sums_ref, places, *terms):
    for index, term in enumerate(terms):
        low, high = term[:8], term[8:]
        for here, there in places:
            sums_ref[0, index * 8 : index * 8 + 8, there] += low[:, here] + high[:, here]


def first_norm_kernel(blocks, order_ref, present_ref, tokens_ref, mods_ref, kept_ref, normed_ref):
    rows = Rows(blocks, order_ref, tokens_ref.shape[1])
    for here, there in rows.places():
        kept_ref[:, here] = tokens_ref[:, there]

    def body(some):
        unit, _ = normal(kept_ref[some, :].astype(F32))
        value = unit * (1.0 + mods_ref[0, 1:2, :]) + mods_ref[0, 0:1, :]
        normed_ref[some, :] = value.astype(BF16)

    rows.each(tokens_ref.shape[0], body)


def cotangent_kernel(blocks, order_ref, present_ref, cotangent_ref, mods_ref, dy_ref, d_mlp_ref):
    rows = Rows(blocks, order_ref, cotangent_ref.shape[1])
    mask = present_ref[pl.program_id(0)].astype(F32)
    for here, there in rows.places():
        dy = cotangent_ref[:, there].astype(F32) * mask
        dy_ref[:, here] = dy.astype(BF16)
        d_mlp_ref[:, here] = (mods_ref[0, 5:6, here] * dy).astype(BF16)


def second_norm_kernel(
    blocks, order_ref, present_ref, tokens_ref, att_a, att_b, mods_ref, hidden_ref, second_ref
):
    rows = Rows(blocks, order_ref, tokens_ref.shape[1])

    def body(some):
        att = att_a[some, :].astype(F32) + att_b[some, :].astype(F32)
        hidden = tokens_ref[some, :].astype(F32) + mods_ref[0, 2:3, :] * att
        hidden_ref[some, :] = hidden
        unit, _ = normal(hidden)
        value = unit * (1.0 + mods_ref[0, 4:5, :]) + mods_ref[0, 3:4, :]
        second_ref[some, :] = value.astype(BF16)

    rows.each(tokens_ref.shape[0], body)


def second_back_kernel(
    blocks, order_ref, present_ref, hidden_ref, att_a, att_b, d_a, d_b, dy_ref, mods_ref,
    d_hidden_ref, d_att_ref, sums_ref,
):
    rows = Rows(blocks, order_ref, hidden_ref.shape[1])
    places = rows.places()
    clear_sums(sums_ref)

    def body(some):
        grad = d_a[some, :].astype(F32) + d_b[some, :].astype(F32)
        unit, factor = normal(hidden_ref[some, :])
        add_sums(sums_ref, places, grad, grad * unit)
        d_hidden = normal_back(grad * (1.0 + mods_ref[0, 4:5, :]), unit, factor)
        d_hidden = dy_ref[some, :].astype(F32) + d_hidden
        d_hidden_ref[some, :] = d_hidden
        d_att_ref[some, :] = (mods_ref[0, 2:3, :] * d_hidden).astype(BF16)
        att = att_a[some, :].astype(F32) + att_b[some, :].astype(F32)
        add_sums(sums_ref.at[:, 16:24], places, d_hidden * att)

    rows.each(hidden_ref.shape[0], body)


def first_back_kernel(
    blocks, order_ref, present_ref, tokens_ref, d_a, d_b, d_hidden_ref, mods_ref,
    input_grad_ref, sums_ref,
):
    rows = Rows(blocks, order_ref, tokens_ref.shape[1])
    places = rows.places()
    clear_sums(sums_ref)

    def body(some):
        grad = d_a[some, :].astype(F32) + d_b[some, :].astype(F32)
        unit, factor = normal(tokens_ref[some, :].astype(F32))
        add_sums(sums_ref, places, grad, grad * unit)
        value = normal_back(grad * (1.0 + mods_ref[0, 1:2, :]), unit, factor)
        value = d_hidden_ref[some, :] + value
        for here, there in places:
            input_grad_ref[some, there] = value[:, here]

    rows.each(tokens_ref.shape[0], body)


def block_out_kernel(
    blocks, order_ref, present_ref, hidden_ref, mlp_a, mlp_b, dy_ref, mods_ref,
    block_out_ref, sums_ref,
):
    rows = Rows(blocks, order_ref, hidden_ref.shape[1])
    places = rows.places()
    mask = present_ref[pl.program_id(0)].astype(F32)
    clear_sums(sums_ref)

    def body(some):
        mlp = mlp_a[some, :].astype(F32) + mlp_b[some, :].astype(F32)
        add_sums(sums_ref, places, dy_ref[some, :].astype(F32) * mlp)
        value = mask * (hidden_ref[some, :] + mods_ref[0, 5:6, :] * mlp)
        for here, there in places:
            block_out_ref[some, there] = value[:, here].astype(BF16)

    rows.each(hidden_ref.shape[0], body)


def by_rows(kernel, order, present, operands, mods, kinds, sums=0):
    images, kinds_of_mods, width = mods.shape
    tiles = operands[0].shape[0] // images // TILE
    row = pl.BlockSpec((TILE, width), lambda i, t, *s: (i * tiles + t, 0))
    whole = lambda count: pl.BlockSpec((1, count, width), lambda i, t, *s: (i, 0, 0))
    shapes = [jax.ShapeDtypeStruct(operands[0].shape, kind) for kind in kinds]
    specs = [row] * len(kinds)
    if sums:
        shapes.append(jax.ShapeDtypeStruct((images, 8 * sums, width), F32))
        specs.append(whole(8 * sums))
    blocks = 0 if width // order.shape[0] % 128 else order.shape[0]
    return pl.pallas_call(
        functools.partial(kernel, blocks),
        grid_spec=pltpu.PrefetchScalarGridSpec(
            num_scalar_prefetch=2,
            grid=(images, tiles),
            in_specs=[row] * len(operands) + [whole(kinds_of_mods)],
            out_specs=specs,
        ),
        out_shape=shapes,
        compiler_params=pltpu.CompilerParams(vmem_limit_bytes=40 * 1024 * 1024),
        cost_estimate=pl.CostEstimate(
            flops=operands[0].size * 6000, bytes_accessed=operands[0].size * 8, transcendentals=0
        ),
    )(order, present, *operands, mods)


def matmul(lhs, rhs, turned=False):
    return lax.dot_general(
        lhs, rhs, (((1,), (1 if turned else 0,)), ((), ())), preferred_element_type=F32
    )


def make_body(dp, mp):
    def body(tokens, mod_table, w_qkv, w_out_t, w_up, w_down, bins, present, cotangent):
        count, length, width = tokens.shape
        rows = count * length
        ph = Phases(dp, mp)
        grid = Grid(ph)
        relative, absolute = grid.to_relative(), grid.to_absolute()
        turns = list(range(1, grid.x)) + [0]
        outside = width // relative.shape[0] % 128
        turn_in = lambda value: reorder(value, relative) if outside else value
        turn_out = lambda value: reorder(value, absolute) if outside else value
        flat = lambda value: value.reshape(rows, width)
        join = lambda own, theirs: jnp.concatenate([own, theirs], axis=0)

        def whole(*by_z):
            return jnp.concatenate(
                [by_z[kz][kx] for kx in range(grid.x) for kz in range(grid.z)], axis=0
            )

        def from_both(theirs, value, weight, between=None):
            if between is not None:
                between()
            part = matmul(ph.begin(value[:rows]), weight, True) + theirs.astype(F32)
            part = part.astype(BF16)
            ph.end(part)
            return ph.across(part)

        def two(parts):
            return parts if len(parts) == 2 else [plus(*parts), jnp.zeros_like(parts[0])]

        def dots(lhs, rhs):
            kept = {}
            for kx in turns:
                kept[kx] = grid.dots(ph.begin(lhs), rhs, kx)
                ph.end(kept[kx])
            return kept

        def rows_of(kept, low, high):
            blk = width // grid.x // grid.z
            return {kx: kept[kx][low * blk : high * blk] for kx in kept}

        wide = w_qkv.reshape(3, -1, CORES, w_qkv.shape[2] // CORES).transpose(1, 2, 0, 3)
        s_q = grid.chip_shard(wide.reshape(w_qkv.shape[1], -1))
        z_q, x_q = {1: ph.send_z(s_q, 1)}, {0: ph.gather_x(s_q)}
        s_o = grid.chip_shard(ph.begin(w_out_t))
        ph.end(s_o)
        x_o = jnp.stack(ph.gather_x(s_o))
        table_rows = jnp.arange(mod_table.shape[0])[None, :]
        onehot = (bins[:, None] == table_rows).astype(F32)
        mods = jnp.einsum("cb,btd->ctd", ph.begin(onehot), mod_table, precision=HIGH)
        mods = reorder(mods, relative)
        ph.end(mods)
        ph.close()

        z_q[3] = ph.send_z(s_q, 3)
        x_q[1] = ph.gather_x(z_q[1])
        tokens, normed_own = by_rows(
            first_norm_kernel, relative, present, [flat(turn_in(ph.begin(tokens)))], mods, [BF16, BF16]
        )
        ph.end(normed_own)
        normed_other = ph.hand_over(normed_own)
        ph.close()

        z_q[2] = ph.send_z(z_q[1], 1)
        x_q[3] = ph.gather_x(z_q[3])
        s_u = grid.chip_shard(ph.begin(w_up))
        ph.end(s_u)
        normed = join(normed_own, ph.begin(normed_other))
        ph.end(normed)
        ph.close()

        z_o = {0: x_o, 1: ph.send_z(x_o, 1)}
        x_q[2] = ph.gather_x(z_q[2])
        s_d = grid.chip_shard(ph.begin(w_down))
        ph.end(s_d)
        ph.close()

        z_o[3] = ph.send_z(x_o, 3)
        z_o[2] = ph.send_z(z_o[1], 1)
        x_u = {0: ph.gather_x(s_u)}
        w_a = whole(x_q[0], x_q[1], x_q[2], x_q[3])
        local_width = s_o.shape[1]
        local_heads = local_width // HEAD_DIM
        qkv = matmul(ph.begin(normed), w_a).astype(BF16)
        ph.end(qkv)
        attend = functools.partial(attend_kernel, local_heads)
        mixed = by_image(attend, length, local_width, ph.begin(qkv))
        ph.end(mixed)
        w_o = jnp.concatenate([z_o[kz][kx] for kx in range(grid.x) for kz in range(grid.z)], axis=0)
        att_part = matmul(ph.begin(mixed)[rows:], w_o, True).astype(BF16)
        ph.end(att_part)
        att_part = ph.hand_over(att_part)
        ph.close()

        z_u = {1: ph.send_z(s_u, 1)}
        x_d = {0: ph.gather_x(s_d)}
        att = from_both(att_part, mixed, w_o)
        dy, d_mlp_own = by_rows(
            cotangent_kernel, relative, present, [flat(turn_in(ph.begin(cotangent)))], mods, [BF16, BF16]
        )
        ph.end(d_mlp_own)
        ph.close()

        z_u[3] = ph.send_z(s_u, 3)
        x_u[1] = ph.gather_x(z_u[1])
        d_mlp_other = ph.hand_over(ph.now(d_mlp_own))
        ph.close()

        z_u[2] = ph.send_z(z_u[1], 1)
        x_u[3] = ph.gather_x(z_u[3])
        att[-1] = ph.begin(att[-1])
        hidden, second_own = by_rows(
            second_norm_kernel, relative, present, [tokens, *two(att)], mods, [F32, BF16]
        )
        ph.end(second_own)
        second_other = ph.hand_over(second_own)
        ph.close()

        z_d = {1: ph.send_z(s_d, 1)}
        x_u = {kz: [ph.now(piece) for piece in x_u[kz]] for kz in x_u}
        x_u[2] = ph.gather_x(z_u[2])
        second = join(second_own, ph.begin(second_other))
        ph.end(second)
        d_mlp = join(d_mlp_own, ph.begin(d_mlp_other))
        ph.end(d_mlp)
        ph.close()

        z_d[3] = ph.send_z(s_d, 3)
        x_d[1] = ph.gather_x(z_d[1])
        w_u = whole(x_u[0], x_u[1], x_u[2], x_u[3])
        up_val = matmul(ph.begin(second), w_u)
        act = jax.nn.gelu(up_val).astype(BF16)
        ph.end(act)
        ph.close()

        z_d[2] = ph.send_z(z_d[1], 1)
        x_d[3] = ph.gather_x(z_d[3])
        down = dots(d_mlp, act)
        half = down[0].shape[1] // 2
        first = jnp.stack([down[kx][:, :half] for kx in range(grid.x)])
        other = {kx: down[kx][:, half:] for kx in down}
        ph.end(first)
        up_val = ph.begin(up_val)
        _, gelu_pull = jax.vjp(jax.nn.gelu, up_val)
        slope = gelu_pull(jnp.ones_like(up_val))[0]
        ph.end(slope)
        ph.close()

        blk = first.shape[1] // grid.z
        part = lambda stacked, kz: stacked[:, kz * blk : (kz + 1) * blk]
        x_d[2] = ph.gather_x(z_d[2])
        a_2 = ph.send(part(first, 2), 3, 0, hold=False)
        step = width // (grid.x * grid.z)
        feature_blocks = lambda value, some: jnp.concatenate(
            [
                value[:, (kx * grid.z + kz) * step : (kx * grid.z + kz + 1) * step]
                for kx in range(grid.x)
                for kz in some
            ],
            axis=1,
        )
        some_of = lambda by_z, some: jnp.concatenate(
            [by_z[kz][kx] for kx in range(grid.x) for kz in some], axis=0
        )
        there = [kz for kz in range(grid.z) if kz != 2]
        late = feature_blocks(d_mlp, [2])
        w_d = [some_of(x_d, there)]
        d_act = [
            matmul(ph.begin(feature_blocks(d_mlp[half_rows], there)), w_d[0])
            for half_rows in (slice(0, rows), slice(rows, None))
        ]
        ph.end(*d_act, late)
        ph.close()

        x_b = {2: ph.reduce_x(rows_of(other, 2, 4))}
        a_3 = ph.send_z(part(first, 3), 1)
        ph.results.append(a_2)
        w_d.append(some_of(x_d, [2]))
        d_act = jnp.concatenate(d_act, axis=0) + matmul(ph.begin(late), w_d[1])
        d_up = (d_act * slope).astype(BF16)
        ph.end(d_up)
        d_second_part = matmul(ph.begin(d_up)[rows:], w_u, True).astype(BF16)
        ph.end(d_second_part)
        d_second_part = ph.hand_over(d_second_part)
        a_1 = ph.begin(plus(part(first, 1), ph.now(a_2)).astype(BF16))
        ph.end(a_1)
        ph.close()

        x_b[0] = ph.reduce_x(rows_of(other, 0, 2))
        a_1 = ph.send_z(a_1, 3)
        d_second = from_both(d_second_part, d_up, w_u)
        up = {}

        def up_dots(blocks):
            for kx in blocks:
                up[kx] = grid.dots(ph.begin(second), d_up, kx)
                ph.end(up[kx])

        up_dots(turns[:-1])
        b_part = lambda kz: ph.now(x_b[kz // 2 * 2][(kz % 2) * blk : (kz % 2 + 1) * blk])
        b_sum = lambda kz: plus(rows_of(other, kz, kz + 1)[0], b_part(kz))
        b_2, b_3 = (ph.begin(b_sum(kz).astype(BF16)) for kz in (2, 3))
        ph.end(b_2, b_3)
        ph.close()

        up_rows = lambda kz: ph.reduce_x(rows_of(up, kz, kz + 1))
        x_up = {2: up_rows(2)}
        b_2 = ph.send_z(b_2, 3)
        b_3 = ph.send_z(b_3, 1)
        up_dots(turns[-1:])
        first_sum = ph.begin(plus(part(first, 0), ph.now(a_3), ph.now(a_1)))
        ph.end(first_sum)
        ph.close()

        x_up[3] = up_rows(3)
        up_sum = lambda kz: plus(rows_of(up, kz, kz + 1)[0], ph.now(x_up[kz]))
        u_2 = ph.send_z(up_sum(2).astype(BF16), 3)
        b_1 = ph.begin((b_sum(1) + ph.now(b_2).astype(F32)).astype(BF16))
        ph.end(b_1)
        d_second[-1] = ph.begin(d_second[-1])
        d_hidden, d_att_own, sums2 = by_rows(
            second_back_kernel, relative, present, [hidden, *two(att), *two(d_second), dy], mods,
            [F32, BF16], 3,
        )
        ph.end(d_att_own)
        d_att_other = ph.hand_over(d_att_own)
        ph.close()

        x_up[1] = up_rows(1)
        x_first = ph.reduce_x(first_sum.astype(BF16))
        u_3 = ph.send_z(up_sum(3).astype(BF16), 1)
        b_1 = ph.send_z(b_1, 3)
        d_att = join(d_att_own, ph.begin(d_att_other))
        d_mixed = matmul(d_att, w_o).astype(BF16)
        ph.end(d_mixed)
        attend_back = functools.partial(attend_back_kernel, local_heads)
        d_qkv = by_image(attend_back, length, 3 * local_width, qkv, ph.begin(d_mixed))
        ph.end(d_qkv)
        d_normed_part = matmul(ph.begin(d_qkv)[rows:], w_a, True).astype(BF16)
        ph.end(d_normed_part)
        d_normed_part = ph.hand_over(d_normed_part)
        ph.close()

        x_up[0] = up_rows(0)
        u_1 = ph.send_z((up_sum(1) + ph.now(u_2).astype(F32)).astype(BF16), 3)
        d_normed = from_both(d_normed_part, d_qkv, w_a)
        out = dots(d_att, mixed)
        proj = dots(normed, d_qkv)
        ph.close()

        x_out = ph.reduce_x(out)
        down_of = lambda value: jnp.concatenate([matmul(value, w, True) for w in w_d], axis=1)
        mlp_part = down_of(ph.begin(act)[rows:]).astype(BF16)
        ph.end(mlp_part)
        mlp_part = ph.hand_over(mlp_part)
        up_total = up_sum(0) + ph.now(u_3).astype(F32) + ph.now(u_1).astype(F32)
        up_mine, up_theirs = grid.halves(ph.begin(up_total), 0)
        ph.end(up_mine)
        up_theirs = ph.hand_over(up_theirs)
        ph.close()

        p_rows = lambda kz: ph.reduce_x(rows_of(proj, kz, kz + 1))
        p_sum = lambda kz: plus(rows_of(proj, kz, kz + 1)[0], ph.now(x_p[kz]))
        out_sum = lambda kz: plus(
            rows_of(out, kz, kz + 1)[0], ph.now(x_out[kz * blk : (kz + 1) * blk])
        )
        x_p = {2: p_rows(2)}
        o_2 = ph.send_z(out_sum(2).astype(BF16), 3)
        o_3 = ph.send_z(out_sum(3).astype(BF16), 1)
        mlp = (down_of(ph.begin(act)[:rows]) + mlp_part.astype(F32)).astype(BF16)
        ph.end(mlp)
        mlp = ph.across(mlp)
        d_normed[-1] = ph.begin(d_normed[-1])
        input_grad, sums1 = by_rows(
            first_back_kernel, relative, present, [tokens, *two(d_normed), d_hidden], mods, [F32], 2
        )
        ph.end(input_grad)
        ph.close(20.0)

        x_p[3] = p_rows(3)
        p_2 = ph.send_z(p_sum(2).astype(BF16), 3)
        up_part = grid.by_core(ph.begin(up_mine), up_theirs, 1)
        ph.end(up_part)
        o_1 = ph.send_z((out_sum(1) + ph.now(o_2).astype(F32)).astype(BF16), 3)
        row_sums = [jnp.sum(v.reshape(count, -1, 8, width), axis=2) for v in (sums1, sums2)]
        row_sums = ph.begin(jnp.concatenate(row_sums, axis=1))
        down_low = plus(ph.now(first_sum)[0], x_first)
        down_high = b_sum(0) + ph.now(b_3).astype(F32) + ph.now(b_1).astype(F32)
        down_total = jnp.concatenate([down_low, down_high], axis=1)
        down_mine, down_theirs = grid.halves(ph.begin(down_total), 0)
        ph.end(down_mine, row_sums)
        down_theirs = ph.hand_over(down_theirs)
        ph.close(20.0)

        x_p[1] = p_rows(1)
        p_3 = ph.send_z(p_sum(3).astype(BF16), 1)
        down_part = grid.by_core(ph.begin(down_mine), down_theirs, 1)
        ph.end(down_part)
        mlp[-1] = ph.begin(mlp[-1])
        places = [(kx, kz) for some in (there, [2]) for kx in range(grid.x) for kz in some]
        in_order = [places.index((kx, kz)) for kx in range(grid.x) for kz in range(grid.z)]
        mlp = [
            jnp.concatenate([v[:, k * step : (k + 1) * step] for k in in_order], axis=1) for v in mlp
        ]
        block_out, sums3 = by_rows(
            block_out_kernel, relative, present, [hidden, *two(mlp), dy], mods, [BF16], 1
        )
        ph.end(block_out)
        ph.close(20.0)

        x_p[0] = p_rows(0)
        p_1 = ph.send_z((p_sum(1) + ph.now(p_2).astype(F32)).astype(BF16), 3)
        sums3 = jnp.sum(sums3.reshape(count, -1, 8, width), axis=2)
        bin_row = jnp.broadcast_to(bins.astype(F32)[:, None, None], (count, 1, width))
        d_mods = turn_out(jnp.concatenate([row_sums, sums3], axis=1))
        d_mods = jnp.concatenate([d_mods, bin_row], axis=1)
        d_mods = d_mods.reshape(-1, dp, width // dp).transpose(1, 0, 2)
        d_mods = ph.begin(d_mods)
        ph.end(d_mods)
        d_mods = lax.all_to_all(d_mods, "dp", split_axis=0, concat_axis=0, tiled=True)
        out_total = out_sum(0) + ph.now(o_3).astype(F32) + ph.now(o_1).astype(F32)
        out_mine, out_theirs = grid.halves(ph.begin(out_total), 0)
        ph.end(out_mine)
        out_theirs = ph.hand_over(out_theirs)
        ph.close(20.0)

        d_mods = ph.now(d_mods).reshape(dp * count, -1, width // dp)
        rows_in_order = jnp.stack([d_mods[:, k] for k in (0, 1, 4, 2, 3, 5)], axis=1)
        onehot_all = (d_mods[:, 6, :1] == table_rows.astype(F32)).astype(F32)
        table_part = jnp.einsum("sb,std->btd", onehot_all, rows_in_order, precision=HIGH)
        out_part = grid.by_core(out_mine, ph.now(out_theirs), 1)
        qkv_part = p_sum(0) + ph.now(p_3).astype(F32) + ph.now(p_1).astype(F32)
        qkv_part = qkv_part.reshape(-1, 3, local_width).transpose(1, 0, 2)
        qkv_part = grid.own_rows(qkv_part)
        block_out, input_grad = (
            turn_out(value).reshape(count, length, width) for value in (block_out, input_grad)
        )
        return (block_out, input_grad, table_part, qkv_part, out_part, up_part, down_part)

    return body


def solution(mesh):
    in_specs = (
        P("dp", None, None),
        P(),
        P(None, "dp", "mp"),
        P("dp", "mp"),
        P("dp", "mp"),
        P("dp", "mp"),
        P("dp"),
        P("dp"),
        P("dp", None, None),
    )
    out_specs = (
        P("dp", None, None),
        P("dp", None, None),
        P(None, None, "dp"),
        P(None, "dp", "mp"),
        P("dp", "mp"),
        P("dp", "mp"),
        P("dp", "mp"),
    )
    body = make_body(mesh.shape["dp"], mesh.shape["mp"])
    return jax.shard_map(body, mesh=mesh, in_specs=in_specs, out_specs=out_specs, check_vma=False)
```
